32 devices in a mesh: dp: 8 (over z, y), rep: 4 (over x, core).
Axes of the slice: x: 2, y: 2, z: 4, core: 2. Of those that a mesh axis runs over, the one named last changes fastest.
Arguments:
- tokens: bfloat16 [31488, 384], P(('dp', 'rep')), may hold values from -6 to 6
- cotangent: bfloat16 [31488, 384], P(('dp', 'rep')), may hold values from -6 to 6
- lengths: int32 [384], P(('dp', 'rep')), may hold values from 50 to 145, as said below
- pos_map: int32 [31488], P(('dp', 'rep')), may hold values from 0 to 144
- attn_params: float32 [592128], P(('dp', 'rep'))
- attn_first: float32 [592128], P(('dp', 'rep')), may hold values from -4 to 4
- attn_second: float32 [592128], P(('dp', 'rep')), may hold values from 0.0001 to 0.01
- mlp_params: float32 [1238016], P(('dp', 'rep'))
- mlp_first: float32 [1238016], P(('dp', 'rep')), may hold values from -4 to 4
- mlp_second: float32 [1238016], P(('dp', 'rep')), may hold values from 0.0001 to 0.01
Outputs:
- output: bfloat16 [31488, 384], P(('dp', 'rep'))
- in_grad: bfloat16 [31488, 384], P(('dp', 'rep'))
- attn_grad: float32 [592128], P(('dp', 'rep'))
- attn_step: float32 [592128], P(('dp', 'rep'))
- attn_first_new: float32 [592128], P(('dp', 'rep'))
- attn_second_new: float32 [592128], P(('dp', 'rep'))
- mlp_grad: float32 [1238016], P(('dp', 'rep'))
- mlp_step: float32 [1238016], P(('dp', 'rep'))
- mlp_first_new: float32 [1238016], P(('dp', 'rep'))
- mlp_second_new: float32 [1238016], P(('dp', 'rep'))
The draws below stay inside these ranges and needn't reach their ends.
Inputs may be any that keep to these rules, and one draw needn't show every extreme that they name: `lengths`: every image has 50 or 145 tokens; one device's 12 images hold at most 4 of 145 tokens, and some device holds exactly 4 in every draw.
All inputs are finite; a program needn't handle non-finite values.
Results may differ from the reference program's by a relative error of at most 0.014.
Values may be sent and summed in bfloat16 or wider, within the bound.
No kernel may reach another device: no remote copies, remote signals or barrier semaphores. Data moves between devices by JAX's collectives and lax.ppermute only.
A program may use at most 128 MiB of HBM per device.

```python
import math
import jax
import jax.numpy as jnp
from jax import lax

D = 384
H = 6
DH = 64
FF = 1536
POS = 145
SHORT = 50
LONG = 145
MOST_LONG = 4
STEP = 10
IMGS_DEV = 12
TOK_DEV = 984
TOKENS = 31488
IMAGES = 384
PA = 592128
PM = 1238016


def normal_piece(key, entries, scale):
    return jax.random.normal(key, (entries,), jnp.float32) * scale


def draw_lengths(key, part):
    key = jax.random.fold_in(key, 1)
    device_count = IMAGES // IMGS_DEV
    key_counts, key_chosen, key_orders = jax.random.split(key, 3)
    counts = jax.random.randint(key_counts, (device_count,), 0, MOST_LONG + 1)
    chosen = jax.random.randint(key_chosen, (), 0, device_count)
    counts = jnp.where(jnp.arange(device_count) == chosen, MOST_LONG, counts)
    orders = jax.vmap(lambda sub_key: jax.random.permutation(sub_key, IMGS_DEV))(jax.random.split(key_orders, device_count))
    long_mask = orders < counts[:, None]
    return jnp.where(long_mask, LONG, SHORT).astype(jnp.int32).reshape(-1)


def draw_attn_params(key, part):
    key = jax.random.fold_in(key, 2)
    streams = jax.random.split(key, 6)
    pieces = [1.0 + normal_piece(streams[0], D, 0.1), normal_piece(streams[1], D, 0.1), normal_piece(streams[2], 3 * D * D, D ** (-0.5)), normal_piece(streams[3], 3 * D, 0.1), normal_piece(streams[4], D * D, (SHORT / D) ** 0.5), normal_piece(streams[5], D, 0.1)]
    return jnp.concatenate(pieces)


def draw_mlp_params(key, part):
    key = jax.random.fold_in(key, 3)
    streams = jax.random.split(key, 7)
    pieces = [normal_piece(streams[0], POS * D, 1.0), 1.0 + normal_piece(streams[1], D, 0.1), normal_piece(streams[2], D, 0.1), normal_piece(streams[3], D * FF, D ** (-0.5)), normal_piece(streams[4], FF, 0.1), normal_piece(streams[5], FF * D, FF ** (-0.5)), normal_piece(streams[6], D, 0.1)]
    return jnp.concatenate(pieces)


def plant(drawn, own_key, least, largest):
    index_at = [jax.random.randint(jax.random.fold_in(own_key, axis), (), 0, length) for axis, length in enumerate(drawn.shape)]
    widest = drawn.shape.index(max(drawn.shape))
    neighbour = index_at[:widest] + [(index_at[widest] + 1) % drawn.shape[widest]] + index_at[widest + 1:]
    return drawn.at[tuple(index_at)].set(least).at[tuple(neighbour)].set(largest)


def shard_levels(rng, dims, shards, smallest, largest):
    gain, own = 1.0, jax.random.fold_in(rng, 6)
    for dim, shards_of in shards:
        steps = jnp.exp(jax.random.uniform(jax.random.fold_in(own, dim), (shards_of,), jnp.float32, smallest / len(shards), largest / len(shards)))
        gain = gain * jnp.repeat(steps, dims[dim] // shards_of).reshape([-1 if axis == dim else 1 for axis in range(len(dims))])
    return gain


def normal_values(stream_key, dims, deviation, reach, cuts=(), kind=jnp.bfloat16):
    result = jax.random.normal(stream_key, dims, jnp.float32) * deviation
    if len(cuts) > 0:
        result = shard_levels(stream_key, dims, cuts, -0.22, 0.18) * result
    return jnp.clip(result, min=-reach, max=reach).astype(kind)


def setup_inputs(seed: int = 0) -> dict:
    key_list = jax.random.split(jax.random.key(seed), 11)
    return {
        "tokens": normal_values(key_list[0], (TOKENS, D), 1.0, 6.0, ((0, 32),)),
        "cotangent": normal_values(key_list[1], (TOKENS, D), 1.0, 6.0, ((0, 32),)),
        "lengths": draw_lengths(jax.random.fold_in(key_list[10], 71), 0),
        "pos_map": plant(jax.random.randint(key_list[3], (TOKENS,), 0, POS), jax.random.fold_in(key_list[3], 1), 0, POS - 1).astype(jnp.int32),
        "attn_params": draw_attn_params(jax.random.fold_in(key_list[10], 71), 0),
        "attn_first": normal_values(key_list[5], (PA,), 0.3, 4.0, ((0, 32),), jnp.float32),
        "attn_second": jnp.clip(jnp.exp(math.log(0.01) - 4.6051702 * jax.random.uniform(key_list[6], (PA,), jnp.float32) ** shard_levels(key_list[6], (PA,), ((0, 32),), -0.2, 0.2)), 0.0001, 0.01),
        "mlp_params": draw_mlp_params(jax.random.fold_in(key_list[10], 71), 0),
        "mlp_first": normal_values(key_list[8], (PM,), 0.3, 4.0, ((0, 32),), jnp.float32),
        "mlp_second": jnp.clip(jnp.exp(math.log(0.01) - 4.6051702 * jax.random.uniform(key_list[9], (PM,), jnp.float32) ** shard_levels(key_list[9], (PM,), ((0, 32),), -0.2, 0.2)), 0.0001, 0.01),
    }


@jax.custom_vjp
def low(v):
    return lax.optimization_barrier(v.astype(jnp.bfloat16)).astype(jnp.float32)

@jax.custom_vjp
def low_back(v):
    return v

def low_keep(v):
    return (low(v), None)

def low_pass(kept, grad):
    return (grad,)

def back_keep(v):
    return (v, None)

def back_low(kept, grad):
    return (low(grad),)
low.defvjp(low_keep, low_pass)
low_back.defvjp(back_keep, back_low)
PRECISE = lax.Precision.HIGHEST
LEARNING_RATE = 0.001
WEIGHT_DECAY = 0.05
BETA_FIRST = 0.9
BETA_SECOND = 0.999
adam_eps = 1e-08

def cut_pieces(vector, piece_shapes):
    pieces = []
    offset = 0
    for piece_shape in piece_shapes:
        entries = math.prod(piece_shape)
        pieces.append(vector[offset:offset + entries].reshape(piece_shape))
        offset += entries
    return pieces

def split_attn(vector):
    return cut_pieces(vector, [(D,), (D,), (D, 3 * D), (3 * D,), (D, D), (D,)])

def split_mlp(vector):
    return cut_pieces(vector, [(POS, D), (D,), (D,), (D, FF), (FF,), (FF, D), (D,)])

def layer_norm(values, gain_term, bias_term):
    average = lax.optimization_barrier(jnp.mean(values, axis=-1, keepdims=True))
    centred = values - average
    variance = lax.optimization_barrier(jnp.mean(centred * centred, axis=-1, keepdims=True))
    return centred * lax.rsqrt(variance + 1e-06) * gain_term + bias_term

def segment_ids(lengths_dev, row_count):
    image_ends = jnp.cumsum(lengths_dev).astype(jnp.int32)
    slot_index = jnp.arange(row_count, dtype=jnp.int32)
    return lax.optimization_barrier(jnp.sum((slot_index[:, None] >= image_ends[None, :]).astype(jnp.int32), axis=1)).astype(jnp.int32)

def block_forward(tokens_block, onehot_block, segment_block, attn_weights, mlp_weights):
    gain_one, bias_one, w_qkv, b_qkv, w_out, b_out = attn_weights
    pos_table, gain_two, bias_two, w_in, b_in, w_back, b_back = mlp_weights
    row_count = tokens_block.shape[0]
    embedded = tokens_block + jnp.dot(onehot_block, pos_table, precision=PRECISE)
    normed = low(layer_norm(embedded, gain_one, bias_one))
    projected = low_back(low(jnp.dot(normed, w_qkv, precision=PRECISE) + b_qkv))
    queries = projected[:, :D].reshape(row_count, H, DH)
    keys_h = projected[:, D:2 * D].reshape(row_count, H, DH)
    values_h = projected[:, 2 * D:].reshape(row_count, H, DH)
    scores = low_back(jnp.einsum('qhd,khd->hqk', queries, keys_h, precision=PRECISE) * DH ** (-0.5))
    same_image = segment_block[:, None] == segment_block[None, :]
    scores = jnp.where(same_image[None], scores, -1e+30)
    att_probs = jax.nn.softmax(scores, axis=-1)
    mixed_out = jnp.einsum('hqk,khd->qhd', low(att_probs), values_h, precision=PRECISE).reshape(row_count, D)
    mixed_out = low_back(low(mixed_out))
    branch = low_back(jnp.dot(mixed_out, w_out, precision=PRECISE) + b_out)
    residual = embedded + branch
    normed_two = low(layer_norm(residual, gain_two, bias_two))
    hidden = low_back(jnp.dot(normed_two, w_in, precision=PRECISE) + b_in)
    active = low(jax.nn.gelu(hidden, approximate=False))
    return residual + low_back(jnp.dot(active, w_back, precision=PRECISE) + b_back)

def adamw_step(gradient, params, first, second):
    first_new = BETA_FIRST * first + (1.0 - BETA_FIRST) * gradient
    second_new = BETA_SECOND * second + (1.0 - BETA_SECOND) * gradient * gradient
    first_hat = first_new / (1.0 - BETA_FIRST ** STEP)
    second_hat = second_new / (1.0 - BETA_SECOND ** STEP)
    update = LEARNING_RATE * (first_hat / (jnp.sqrt(second_hat) + adam_eps) + WEIGHT_DECAY * params)
    return (update, first_new, second_new)

def reference(tokens, cotangent, lengths, pos_map, attn_params, attn_first, attn_second, mlp_params, mlp_first, mlp_second):
    groups = TOKENS // TOK_DEV
    segments = jax.vmap(lambda lens_dev: segment_ids(lens_dev, TOK_DEV))(lengths.reshape(groups, IMGS_DEV))
    live_rows = (segments < IMGS_DEV).astype(jnp.float32)
    onehot = (pos_map.reshape(groups, TOK_DEV)[..., None] == jnp.arange(POS, dtype=jnp.int32)[None, None, :]).astype(jnp.float32)
    inputs = tokens.astype(jnp.float32).reshape(groups, TOK_DEV, D)
    checked = jax.checkpoint(block_forward)

    def forward(inputs_f, attn_f, mlp_f):
        attn_weights = tuple(split_attn(low(attn_f)))
        mlp_weights = tuple(split_mlp(low(mlp_f)))

        def scan_body(carried, step_items):
            return (carried, checked(step_items[0], step_items[1], step_items[2], attn_weights, mlp_weights))
        _, outputs = lax.scan(scan_body, jnp.zeros((), jnp.float32), (inputs_f, onehot, segments))
        return outputs
    outputs, pullback = jax.vjp(forward, inputs, attn_params, mlp_params)
    out_seed_grad = cotangent.astype(jnp.float32).reshape(groups, TOK_DEV, D) * live_rows[..., None]
    grad_input, grad_attn, grad_mlp = pullback(out_seed_grad)
    grad_scale = 1.0 / math.sqrt(TOKENS)
    grad_attn = grad_attn * grad_scale
    grad_mlp = grad_mlp * grad_scale
    attn_step, attn_first_new, attn_second_new = adamw_step(grad_attn, attn_params, attn_first, attn_second)
    mlp_step, mlp_first_new, mlp_second_new = adamw_step(grad_mlp, mlp_params, mlp_first, mlp_second)
    return (outputs.reshape(TOKENS, D).astype(jnp.bfloat16), grad_input.reshape(TOKENS, D).astype(jnp.bfloat16), grad_attn, attn_step, attn_first_new, attn_second_new, grad_mlp, mlp_step, mlp_first_new, mlp_second_new)
```

```python
import functools
import math

import jax
import jax.numpy as jnp
from jax import lax
from jax.experimental import pallas as pl
from jax.experimental.pallas import tpu as pltpu
from jax.sharding import PartitionSpec as P

D = 384
H = 6
DH = 64
FF = 1536
POS = 145
SHORT = 50
LONG = 145
STEP = 10
LANES = 128
TILE = 8 * LANES
PAIRS = H // 2
QKV_COLS = 3 * D // LANES
D_COLS = D // LANES
FF_COLS = FF // LANES

LEARNING_RATE = 0.001
WEIGHT_DECAY = 0.05
BETA_FIRST = 0.9
BETA_SECOND = 0.999
adam_eps = 1e-08

F32 = jnp.float32
BF16 = jnp.bfloat16
NT = (((1,), (1,)), ((), ()))
TN = (((0,), (0,)), ((), ()))
NN = (((1,), (0,)), ((), ()))
VMEM_BYTES = 56 * 1024 * 1024
BLOCK = 128

ROW_GAIN_ONE = 0
ROW_BIAS_ONE = ROW_GAIN_ONE + D_COLS
ROW_W_QKV = ROW_BIAS_ONE + D_COLS
ROW_B_QKV = ROW_W_QKV + D * QKV_COLS
ROW_W_OUT = ROW_B_QKV + QKV_COLS
ROW_B_OUT = ROW_W_OUT + D * D_COLS
ATTN_ROWS = ROW_B_OUT + D_COLS
ROW_POS = 0
ROW_GAIN_TWO = ROW_POS + POS * D_COLS
ROW_BIAS_TWO = ROW_GAIN_TWO + D_COLS
ROW_W_IN = ROW_BIAS_TWO + D_COLS
ROW_B_IN = ROW_W_IN + D * FF_COLS
ROW_W_BACK = ROW_B_IN + FF_COLS
ROW_B_BACK = ROW_W_BACK + FF * D_COLS
MLP_ROWS = ROW_B_BACK + D_COLS


def dot(a, b, dims=NN):
    return lax.dot_general(a, b, dims, preferred_element_type=F32)


def tile_row(entries, j):
    return pl.multiple_of(((j * entries) // TILE) * 8, 8)


def piece_rows(entries, count):
    most = max((entries * j) % TILE + entries for j in range(count))
    return -(-most // (16 * LANES)) * 16


def flat_rows(entries, count, rows):
    return max((entries * j) // TILE * 8 + rows for j in range(count))


def params(**more):
    return pltpu.CompilerParams(vmem_limit_bytes=VMEM_BYTES, **more)


def whole(shape):
    return pl.BlockSpec(shape, lambda *_: (0,) * len(shape))


SMEM_SPEC = pl.BlockSpec(memory_space=pltpu.SMEM)


def align_kernel(place, attn, mlp, attn_out, mlp_out):
    for n, (source, target) in enumerate(((attn, attn_out), (mlp, mlp_out))):
        lanes, rows = place[2 * n], place[2 * n + 1]
        value = source[...]
        turned = pltpu.roll(value, lanes, 1)
        below = pltpu.roll(turned, 1, 0)
        lane = lax.broadcasted_iota(jnp.int32, value.shape, 1)
        moved = jnp.where(lane >= lanes, turned, below)
        target[...] = pltpu.roll(moved, rows, 0).astype(BF16)


def take_share(value, lanes, rows):
    height = value.shape[0]
    value = pltpu.roll(value, (height - rows) % height, 0)
    turned = pltpu.roll(value, (LANES - lanes) % LANES, 1)
    above = pltpu.roll(turned, height - 1, 0)
    lane = lax.broadcasted_iota(jnp.int32, value.shape, 1)
    return jnp.where(lane < LANES - lanes, turned, above)


def unpack(flat, arrays, entries, rows, me):
    flat[...] = jnp.zeros_like(flat)
    for ref, numbers in arrays:
        for t, number in enumerate(numbers):
            start = tile_row(entries, number ^ me)
            flat[pl.ds(start, rows), :] += ref[t * rows : (t + 1) * rows, :].astype(F32)


def read_matrix(flat, row, depth, cols, target):
    for c in range(cols):
        target[:, c * LANES : (c + 1) * LANES] = flat[pl.ds(row + c, depth, stride=cols), :].astype(BF16)


def read_row(flat, row, cols):
    return jnp.concatenate([flat[row + c : row + c + 1, :] for c in range(cols)], axis=1)


def write_row(flat, row, value):
    for c in range(value.shape[1] // LANES):
        flat[row + c : row + c + 1, :] = value[:, c * LANES : (c + 1) * LANES]


def norm_parts(value):
    average = jnp.mean(value, axis=-1, keepdims=True)
    centred = value - average
    variance = jnp.mean(centred * centred, axis=-1, keepdims=True)
    inverse = lax.rsqrt(variance + 1e-06)
    return centred * inverse, inverse


def norm_back(normed, inverse, gain, grad):
    scaled = grad * gain
    first = jnp.mean(scaled, axis=-1, keepdims=True)
    second = jnp.mean(scaled * normed, axis=-1, keepdims=True)
    return (scaled - first - normed * second) * inverse


def fold_rows(value):
    return jnp.sum(value.reshape(-1, 8, value.shape[-1]), axis=0)


def key_window(block, rows, images, padding):
    low = max(0, block * BLOCK - (LONG - 1)) // BLOCK * BLOCK
    high = min(rows, (block + 1) * BLOCK + LONG - 1)
    if padding and (block + 1) * BLOCK > images * SHORT:
        low = min(low, images * SHORT // BLOCK * BLOCK)
        high = rows
    return low, min(rows, -(-high // BLOCK) * BLOCK)


def both_heads(value, left):
    zero = jnp.zeros_like(value)
    return jnp.concatenate([jnp.where(left, value, zero), jnp.where(left, zero, value)], axis=0)


def attn_forward_kernel(
    images, attn_entries, mlp_entries, attn_plan, pos_plan, attn_rows, mlp_rows, names, *refs
):
    me, pos_names = names, refs[0]
    refs = refs[1:]
    seg_row, seg_col, onehot, tokens = refs[:4]
    refs = refs[4:]
    attn_arrays = [(refs[i], plan) for i, plan in enumerate(attn_plan)]
    refs = refs[len(attn_plan) :]
    pos_arrays = refs[:pos_plan]
    refs = refs[pos_plan:]
    (embedded, normed_out, qkv, key_t, mixed, log_total, residual, w_qkv, w_out, vectors) = refs[:10]
    flat, pos_flat, pos_table, value_t = refs[10:]
    rows = tokens.shape[0]

    pos_flat[...] = jnp.zeros_like(pos_flat)
    for n, ref in enumerate(pos_arrays):
        start = tile_row(mlp_entries, pos_names[n])
        pos_flat[pl.ds(start, mlp_rows), :] += ref[...].astype(F32)
    pos_table[...] = jnp.zeros_like(pos_table)
    for c in range(D_COLS):
        pos_table[0:144, c * LANES : (c + 1) * LANES] = pos_flat[pl.ds(ROW_POS + c, 144, stride=D_COLS), :].astype(BF16)
    last = read_row(pos_flat, ROW_POS + 144 * D_COLS, D_COLS)
    pos_table[144:160, :] = jnp.concatenate([last, jnp.zeros((15, D), F32)], axis=0).astype(BF16)

    unpack(flat, attn_arrays, attn_entries, attn_rows, me[0])
    read_matrix(flat, ROW_W_QKV, D, QKV_COLS, w_qkv)
    read_matrix(flat, ROW_W_OUT, D, D_COLS, w_out)
    gain = read_row(flat, ROW_GAIN_ONE, D_COLS)
    bias = read_row(flat, ROW_BIAS_ONE, D_COLS)
    b_qkv = read_row(flat, ROW_B_QKV, QKV_COLS)
    b_out = read_row(flat, ROW_B_OUT, D_COLS)
    vectors[0:1, :] = gain

    def project(i, _):
        at = pl.ds(pl.multiple_of(i * BLOCK, BLOCK), BLOCK)
        value = tokens[at, :].astype(F32) + dot(onehot[at, :], pos_table[...])
        embedded[at, :] = value
        normed, _ = norm_parts(value)
        normed = (normed * gain + bias).astype(BF16)
        normed_out[at, :] = normed
        for c in range(QKV_COLS):
            part = dot(normed, w_qkv[:, c * LANES : (c + 1) * LANES]) + b_qkv[:, c * LANES : (c + 1) * LANES]
            part = part.astype(BF16)
            if c < PAIRS:
                part = part * jnp.asarray(DH ** (-0.5), BF16)
            qkv[c, at, :] = part
            if c >= 2 * PAIRS:
                value_t[c - 2 * PAIRS, :, at] = part.T
            elif c >= PAIRS:
                key_t[c - PAIRS, :, at] = part.T
        return 0

    lax.fori_loop(0, rows // BLOCK, project, 0)

    left = lax.broadcasted_iota(jnp.int32, (BLOCK, LANES), 1) < DH
    for block in range(rows // BLOCK):
        low, high = key_window(block, rows, images, True)
        here = slice(block * BLOCK, (block + 1) * BLOCK)
        seg_q = seg_row[:, here]
        same = seg_col[low:high, :] == jnp.concatenate([seg_q, seg_q], axis=1)
        for pair in range(PAIRS):
            queries = both_heads(qkv[pair, here, :], left)
            scores = dot(qkv[PAIRS + pair, low:high, :], queries, NT)
            scores = jnp.where(same, scores, -1e30)
            peak = jnp.max(scores, axis=0, keepdims=True)
            probs = jnp.exp(scores - peak)
            total = jnp.sum(probs, axis=0, keepdims=True)
            out = dot(value_t[pair, :, low:high], probs.astype(BF16)) / total
            log_total[block * PAIRS + pair] = peak + jnp.log(total)
            out = out.T
            mixed[here, pair * LANES : (pair + 1) * LANES] = jnp.where(left, out[:BLOCK], out[BLOCK:]).astype(BF16)

    def finish(i, _):
        at = pl.ds(pl.multiple_of(i * BLOCK, BLOCK), BLOCK)
        residual[at, :] = embedded[at, :] + dot(mixed[at, :], w_out[...]) + b_out
        return 0

    lax.fori_loop(0, rows // BLOCK, finish, 0)


def attn_forward(images, entries, attn_arrays, pos_arrays, pos_names, me, seg_row, seg_col, onehot, tokens, sizes):
    rows = tokens.shape[0]
    plan = [numbers for _, numbers in attn_arrays]
    operands = [seg_row, seg_col, onehot, tokens] + [a for a, _ in attn_arrays] + list(pos_arrays)
    outs = [
        ((rows, D), F32),
        ((rows, D), BF16),
        ((QKV_COLS, rows, LANES), BF16),
        ((PAIRS, LANES, rows), BF16),
        ((rows, D), BF16),
        ((rows // BLOCK * PAIRS, 1, 2 * BLOCK), F32),
        ((rows, D), F32),
        ((D, 3 * D), BF16),
        ((D, D), BF16),
        ((8, D), F32),
    ]
    kernel = functools.partial(
        attn_forward_kernel, images, entries[0], entries[1], plan, len(pos_arrays), sizes.attn_rows, sizes.mlp_rows
    )
    return pl.pallas_call(
        kernel,
        grid=(1,),
        in_specs=[SMEM_SPEC, SMEM_SPEC] + [whole(a.shape) for a in operands],
        out_specs=[whole(s) for s, _ in outs],
        out_shape=[jax.ShapeDtypeStruct(s, t) for s, t in outs],
        scratch_shapes=[
            pltpu.VMEM((sizes.attn_flat, LANES), F32),
            pltpu.VMEM((sizes.pos_flat, LANES), F32),
            pltpu.VMEM((256, D), BF16),
            pltpu.VMEM((PAIRS, LANES, rows), BF16),
        ],
        compiler_params=params(),
        name="attn_forward",
    )(me, pos_names, *operands)


def gelu_parts(value):
    size = jnp.abs(value)
    near = 1.0 / (1.0 + (0.3275911 * math.sqrt(0.5)) * size)
    bell = jnp.exp(-0.5 * value * value)
    series = near * (
        0.5 * 0.254829592
        + near
        * (0.5 * -0.284496736 + near * (0.5 * 1.421413741 + near * (0.5 * -1.453152027 + near * (0.5 * 1.061405429))))
    )
    tail = series * bell
    share = jnp.where(value >= 0, 1.0 - tail, tail)
    return value * share, share + value * bell * (1.0 / math.sqrt(2.0 * math.pi))


def pack(flat, entries, rows, me, targets):
    for ref, numbers in targets:
        for t, number in enumerate(numbers):
            start = tile_row(entries, number ^ me)
            ref[t * rows : (t + 1) * rows, :] = flat[pl.ds(start, rows), :].astype(BF16)


def mlp_kernel(entries, in_plan, out_plan, piece, me, residual, out_grad, *refs):
    arrays = [(refs[i], plan) for i, plan in enumerate(in_plan)]
    refs = refs[len(in_plan) :]
    output, d_residual = refs[:2]
    targets = [(refs[2 + i], plan) for i, plan in enumerate(out_plan)]
    refs = refs[2 + len(out_plan) :]
    flat, w_in, w_back, normed_b, active_b, d_hidden_b, out_f32, sums_in, sums = refs
    rows = residual.shape[0]
    step_rows = 2 * BLOCK

    unpack(flat, arrays, entries, piece, me[0])
    read_matrix(flat, ROW_W_IN, D, FF_COLS, w_in)
    read_matrix(flat, ROW_W_BACK, FF, D_COLS, w_back)
    gain = read_row(flat, ROW_GAIN_TWO, D_COLS)
    bias = read_row(flat, ROW_BIAS_TWO, D_COLS)
    b_in = read_row(flat, ROW_B_IN, FF_COLS)
    b_back = read_row(flat, ROW_B_BACK, D_COLS)
    sums[...] = jnp.zeros_like(sums)
    sums_in[...] = jnp.zeros_like(sums_in)

    def step(i, _):
        at = pl.ds(pl.multiple_of(i * step_rows, step_rows), step_rows)
        value = residual[at, :]
        grad_b = out_grad[at, :]
        normed, inverse = norm_parts(value)
        low = (normed * gain + bias).astype(BF16)
        normed_b[at, :] = low
        total = value + b_back
        d_normed = jnp.zeros((step_rows, D), F32)
        for c in range(FF // 256):
            cols = slice(c * 256, (c + 1) * 256)
            hidden = dot(low, w_in[:, cols]) + b_in[:, cols]
            d_active = dot(grad_b, w_back[cols, :], NT)
            active, slope = gelu_parts(hidden)
            active = active.astype(BF16)
            d_hidden = (d_active * slope).astype(BF16)
            active_b[at, cols] = active
            d_hidden_b[at, cols] = d_hidden
            sums_in[:, cols] += fold_rows(d_hidden.astype(F32))
            total = total + dot(active, w_back[cols, :])
            d_normed = d_normed + dot(d_hidden, w_in[:, cols], NT)
        out_f32[at, :] = total
        grad = grad_b.astype(F32)
        d_residual[at, :] = grad + norm_back(normed, inverse, gain, d_normed)
        sums[0] += fold_rows(d_normed * normed)
        sums[1] += fold_rows(d_normed)
        sums[2] += fold_rows(grad)
        return 0

    lax.fori_loop(0, rows // step_rows, step, 0)
    output[...] = out_f32[0 : output.shape[0], :].astype(BF16)

    flat[...] = jnp.zeros_like(flat)
    write_row(flat, ROW_GAIN_TWO, jnp.sum(sums[0], axis=0, keepdims=True))
    write_row(flat, ROW_BIAS_TWO, jnp.sum(sums[1], axis=0, keepdims=True))
    write_row(flat, ROW_B_IN, jnp.sum(sums_in[...], axis=0, keepdims=True))
    write_row(flat, ROW_B_BACK, jnp.sum(sums[2], axis=0, keepdims=True))
    normed_t = normed_b[...].T
    for c in range(0, FF_COLS, 2):
        part = dot(normed_t, d_hidden_b[:, c * LANES : (c + 2) * LANES])
        for k in range(2):
            flat[pl.ds(ROW_W_IN + c + k, D, stride=FF_COLS), :] = part[:, k * LANES : (k + 1) * LANES]
    for r in range(0, FF, 256):
        part = dot(active_b[:, r : r + 256], out_grad[...], TN)
        for c in range(D_COLS):
            flat[pl.ds(ROW_W_BACK + r * D_COLS + c, 256, stride=D_COLS), :] = part[:, c * LANES : (c + 1) * LANES]
    pack(flat, entries, piece, me[0], targets)


def mlp_both(entries, arrays, me, residual, out_grad, out_rows, out_plan, sizes):
    rows = residual.shape[0]
    plan = [numbers for _, numbers in arrays]
    operands = [residual, out_grad] + [a for a, _ in arrays]
    outs = [((out_rows, D), BF16), ((rows, D), F32)] + [((len(n) * sizes.mlp_rows, LANES), BF16) for n in out_plan]
    return pl.pallas_call(
        functools.partial(mlp_kernel, entries, plan, out_plan, sizes.mlp_rows),
        grid=(1,),
        in_specs=[SMEM_SPEC] + [whole(a.shape) for a in operands],
        out_specs=[whole(s) for s, _ in outs],
        out_shape=[jax.ShapeDtypeStruct(s, t) for s, t in outs],
        scratch_shapes=[
            pltpu.VMEM((sizes.mlp_flat, LANES), F32),
            pltpu.VMEM((D, FF), BF16),
            pltpu.VMEM((FF, D), BF16),
            pltpu.VMEM((rows, D), BF16),
            pltpu.VMEM((rows, FF), BF16),
            pltpu.VMEM((rows, FF), BF16),
            pltpu.VMEM((rows, D), F32),
            pltpu.VMEM((8, FF), F32),
            pltpu.VMEM((3, 8, D), F32),
        ],
        compiler_params=params(),
        name="feed_forward",
    )(me, *operands)


def attn_backward_kernel(images, entries, out_plan, piece, me, *refs):
    (seg_row, seg_col, onehot, embedded, normed_b, qkv, key_t, mixed, log_total, w_qkv, w_out, vectors, d_residual) = refs[:13]
    in_grad, pos_out = refs[13:15]
    targets = [(refs[15 + i], plan) for i, plan in enumerate(out_plan)]
    refs = refs[15 + len(out_plan) :]
    flat, d_branch_b, d_mixed, d_keys, d_values, d_qkv, d_embedded_b, sums = refs
    rows = embedded.shape[0]
    gain = vectors[0:1, :]
    sums[...] = jnp.zeros_like(sums)

    def enter(i, _):
        at = pl.ds(pl.multiple_of(i * BLOCK, BLOCK), BLOCK)
        branch = d_residual[at, :].astype(BF16)
        d_branch_b[at, :] = branch
        sums[0] += fold_rows(branch.astype(F32))
        value = dot(branch, w_out[...], NT).astype(BF16)
        for c in range(D_COLS):
            d_mixed[c, at, :] = value[:, c * LANES : (c + 1) * LANES]
        return 0

    lax.fori_loop(0, rows // BLOCK, enter, 0)

    d_keys[...] = jnp.zeros_like(d_keys)
    d_values[...] = jnp.zeros_like(d_values)
    left = lax.broadcasted_iota(jnp.int32, (BLOCK, LANES), 1) < DH
    ones = jnp.ones((8, LANES), BF16)
    for block in range(rows // BLOCK):
        low, high = key_window(block, rows, images, False)
        here = slice(block * BLOCK, (block + 1) * BLOCK)
        seg_q = seg_row[:, here]
        same = seg_col[low:high, :] == jnp.concatenate([seg_q, seg_q], axis=1)
        for pair in range(PAIRS):
            cols = slice(pair * LANES, (pair + 1) * LANES)
            queries = both_heads(qkv[pair, here, :], left)
            out_now = d_mixed[pair, here, :]
            grads = both_heads(out_now, left)
            scores = dot(qkv[PAIRS + pair, low:high, :], queries, NT)
            scores = jnp.where(same, scores, -1e30)
            probs = jnp.exp(scores - log_total[block * PAIRS + pair])
            product = both_heads(out_now.astype(F32) * mixed[here, cols].astype(F32), left)
            upper = product.astype(BF16)
            lower = (product - upper.astype(F32)).astype(BF16)
            delta = (dot(ones, upper, NT) + dot(ones, lower, NT))[0:1, :]
            d_probs = dot(qkv[2 * PAIRS + pair, low:high, :], grads, NT)
            d_scores = (probs * (d_probs - delta)).astype(BF16)
            d_values[pair, low:high, :] += dot(probs.astype(BF16), grads)
            d_keys[pair, low:high, :] += dot(d_scores, queries)
            d_queries = (dot(key_t[pair, :, low:high], d_scores) * DH ** (-0.5)).T
            d_qkv[here, cols] = jnp.where(left, d_queries[:BLOCK], d_queries[BLOCK:]).astype(BF16)
    for pair in range(PAIRS):
        d_qkv[:, (PAIRS + pair) * LANES : (PAIRS + pair + 1) * LANES] = d_keys[pair].astype(BF16)
        d_qkv[:, (2 * PAIRS + pair) * LANES : (2 * PAIRS + pair + 1) * LANES] = d_values[pair].astype(BF16)

    def leave(i, _):
        at = pl.ds(pl.multiple_of(i * BLOCK, BLOCK), BLOCK)
        d_normed = dot(d_qkv[at, :], w_qkv[...], NT)
        normed, inverse = norm_parts(embedded[at, :])
        value = d_residual[at, :] + norm_back(normed, inverse, gain, d_normed)
        d_embedded_b[at, :] = value.astype(BF16)
        sums[1] += fold_rows(d_normed * normed)
        sums[2] += fold_rows(d_normed)
        return 0

    lax.fori_loop(0, rows // BLOCK, leave, 0)
    in_grad[...] = d_embedded_b[0 : in_grad.shape[0], :]

    flat[...] = jnp.zeros_like(flat)
    write_row(flat, ROW_GAIN_ONE, jnp.sum(sums[1], axis=0, keepdims=True))
    write_row(flat, ROW_BIAS_ONE, jnp.sum(sums[2], axis=0, keepdims=True))
    write_row(flat, ROW_B_OUT, jnp.sum(sums[0], axis=0, keepdims=True))
    normed_t = normed_b[...].T
    for c in range(QKV_COLS):
        cols = slice(c * LANES, (c + 1) * LANES)
        column = d_qkv[:, cols]
        flat[pl.ds(ROW_W_QKV + c, D, stride=QKV_COLS), :] = dot(normed_t, column)
        flat[ROW_B_QKV + c : ROW_B_QKV + c + 1, :] = jnp.sum(fold_rows(column.astype(F32)), axis=0, keepdims=True)
    mixed_t = mixed[...].T
    for c in range(D_COLS):
        flat[pl.ds(ROW_W_OUT + c, D, stride=D_COLS), :] = dot(mixed_t, d_branch_b[:, c * LANES : (c + 1) * LANES])
    pack(flat, entries, piece, me[0], targets)

    pos_grad = dot(onehot[...], d_embedded_b[...], TN)
    flat[...] = jnp.zeros_like(flat)
    for c in range(D_COLS):
        flat[pl.ds(ROW_POS + c, POS, stride=D_COLS), :] = pos_grad[0:POS, c * LANES : (c + 1) * LANES]
    pos_out[...] = flat[0 : pos_out.shape[0], :].astype(BF16)


def attn_backward(images, entries, me, kept, d_residual, out_rows, out_plan, sizes):
    rows = d_residual.shape[0]
    operands = list(kept) + [d_residual]
    outs = [((out_rows, D), BF16), ((sizes.pos_flat, LANES), BF16)]
    outs += [((len(n) * sizes.attn_rows, LANES), BF16) for n in out_plan]
    return pl.pallas_call(
        functools.partial(attn_backward_kernel, images, entries, out_plan, sizes.attn_rows),
        grid=(1,),
        in_specs=[SMEM_SPEC] + [whole(a.shape) for a in operands],
        out_specs=[whole(s) for s, _ in outs],
        out_shape=[jax.ShapeDtypeStruct(s, t) for s, t in outs],
        scratch_shapes=[
            pltpu.VMEM((max(sizes.attn_flat, sizes.pos_flat), LANES), F32),
            pltpu.VMEM((rows, D), BF16),
            pltpu.VMEM((PAIRS, rows, LANES), BF16),
            pltpu.VMEM((PAIRS, rows, LANES), F32),
            pltpu.VMEM((PAIRS, rows, LANES), F32),
            pltpu.VMEM((rows, 3 * D), BF16),
            pltpu.VMEM((rows, D), BF16),
            pltpu.VMEM((3, 8, D), F32),
        ],
        compiler_params=params(),
        name="attn_backward",
    )(me, *operands)


def settle_kernel(scale, attn_count, mlp_count, pos_count, place, *refs):
    attn = refs[:attn_count]
    mlp = refs[attn_count : attn_count + mlp_count]
    pos = refs[attn_count + mlp_count : attn_count + mlp_count + pos_count]
    attn_out, mlp_out = refs[-2:]
    total = sum(ref[...].astype(F32) for ref in attn)
    attn_out[...] = take_share(total, place[0], place[1]) * scale
    total = sum(ref[...].astype(F32) for ref in mlp)
    extra = sum(ref[...].astype(F32) for ref in pos)
    total = total + jnp.where(place[4] > 0, extra, 0.0)
    mlp_out[...] = take_share(total, place[2], place[3]) * scale


def settle(scale, place, attn, mlp, pos):
    operands = list(attn) + list(mlp) + list(pos)
    return pl.pallas_call(
        functools.partial(settle_kernel, scale, len(attn), len(mlp), len(pos)),
        grid=(1,),
        in_specs=[SMEM_SPEC] + [whole(a.shape) for a in operands],
        out_specs=[whole(attn[0].shape), whole(mlp[0].shape)],
        out_shape=[jax.ShapeDtypeStruct(attn[0].shape, F32), jax.ShapeDtypeStruct(mlp[0].shape, F32)],
        compiler_params=params(),
        name="settle",
    )(place, *operands)


def adamw_step(gradient, weights, first, second):
    first_new = BETA_FIRST * first + (1.0 - BETA_FIRST) * gradient
    second_new = BETA_SECOND * second + (1.0 - BETA_SECOND) * gradient * gradient
    first_hat = first_new / (1.0 - BETA_FIRST**STEP)
    second_hat = second_new / (1.0 - BETA_SECOND**STEP)
    update = LEARNING_RATE * (first_hat / (jnp.sqrt(second_hat) + adam_eps) + WEIGHT_DECAY * weights)
    return (update, first_new, second_new)


AXES = ("dp", "rep")
BIT_CORE, BIT_X, BIT_Y, BIT_Z = 1, 2, 4, 8
DEVICES = 32


def swap(value, bits):
    return lax.ppermute(value, AXES, [(j, j ^ bits) for j in range(DEVICES)])


def spread_z(piece):
    return [piece] + [swap(piece, k * BIT_Z) for k in (1, 2, 3)]


def spread_rest(along_z):
    one = [(jnp.concatenate(along_z[:2], axis=0), [0, BIT_Z])]
    two = [(jnp.concatenate(along_z[2:], axis=0), [2 * BIT_Z, 3 * BIT_Z])]

    def grow(held, bits):
        return held + [(swap(a, bits), [n ^ bits for n in numbers]) for a, numbers in held]

    one, two = grow(one, BIT_X), grow(two, BIT_Y)
    one, two = grow(one, BIT_Y), grow(two, BIT_X)
    return grow(one + two, BIT_CORE)


def sum_plan():
    plans = []
    for core in (1, 0):
        plans.append([core + x * BIT_X + y * BIT_Y + z * BIT_Z for x in (0, 1) for y in (0, 1) for z in (0, 1)])
        plans.append([core + x * BIT_X + y * BIT_Y + z * BIT_Z for y in (0, 1) for x in (0, 1) for z in (2, 3)])
    return plans


def halve(value, bits):
    half = value.shape[0] // 2
    return value[:half] + swap(value[half:].astype(BF16), bits).astype(F32)


def sum_pieces(send_one, send_two, keep_one, keep_two):
    one = keep_one.astype(F32) + swap(send_one, BIT_CORE).astype(F32)
    two = keep_two.astype(F32) + swap(send_two, BIT_CORE).astype(F32)
    one, two = halve(one, BIT_X), halve(two, BIT_Y)
    one, two = halve(one, BIT_Y), halve(two, BIT_X)
    one, two = one.astype(BF16), two.astype(BF16)
    rows = one.shape[0] // 2
    return [
        one[:rows],
        swap(one[rows:], BIT_Z),
        swap(two[:rows], 2 * BIT_Z),
        swap(two[rows:], 3 * BIT_Z),
    ]


def sum_everywhere(value):
    value = (value.astype(F32) + swap(value, BIT_X).astype(F32)).astype(BF16)
    value = (value.astype(F32) + swap(value, BIT_Y).astype(F32)).astype(BF16)
    return [value] + [swap(value, k * BIT_Z) for k in (1, 2, 3)]


class Sizes:
    def __init__(self, count, attn_entries, mlp_entries):
        self.attn_rows = piece_rows(attn_entries, count)
        self.mlp_rows = piece_rows(mlp_entries, count)
        self.attn_flat = max(flat_rows(attn_entries, count, self.attn_rows), ATTN_ROWS)
        self.mlp_flat = max(flat_rows(mlp_entries, count, self.mlp_rows), MLP_ROWS)
        self.pos_count = -(-POS * D // mlp_entries)
        self.pos_flat = flat_rows(mlp_entries, self.pos_count, self.mlp_rows)
        self.pos_flat = max(-(-self.pos_flat // 16) * 16, -(-POS * D_COLS // 16) * 16)


def padded(vector, rows):
    return jnp.pad(vector, (0, rows * LANES - vector.shape[0])).reshape(rows, LANES)


def body(
    by_hand,
    tokens,
    cotangent,
    lengths,
    pos_map,
    attn_params,
    attn_first,
    attn_second,
    mlp_params,
    mlp_first,
    mlp_second,
):
    slots = tokens.shape[0]
    images = lengths.shape[0]
    rows = -(-slots // (2 * BLOCK)) * 2 * BLOCK
    count = lax.axis_size("dp") * lax.axis_size("rep")
    entries = (attn_params.shape[0], mlp_params.shape[0])
    sizes = Sizes(count, *entries)
    me = lax.axis_index("dp") * lax.axis_size("rep") + lax.axis_index("rep")
    me = me.astype(jnp.int32)

    starts = [(me * n) % TILE for n in entries]
    place = jnp.stack(
        [starts[0] % LANES, starts[0] // LANES, starts[1] % LANES, starts[1] // LANES, (me < 2).astype(jnp.int32)]
    )
    attn_piece, mlp_piece = pl.pallas_call(
        align_kernel,
        grid=(1,),
        in_specs=[SMEM_SPEC, whole((sizes.attn_rows, LANES)), whole((sizes.mlp_rows, LANES))],
        out_specs=[whole((sizes.attn_rows, LANES)), whole((sizes.mlp_rows, LANES))],
        out_shape=[
            jax.ShapeDtypeStruct((sizes.attn_rows, LANES), BF16),
            jax.ShapeDtypeStruct((sizes.mlp_rows, LANES), BF16),
        ],
        compiler_params=params(),
        name="align",
    )(place, padded(attn_params, sizes.attn_rows), padded(mlp_params, sizes.mlp_rows))

    if by_hand:
        mask = me
        attn_z, mlp_z = spread_z(attn_piece), spread_z(mlp_piece)
        z, y, x, core = me // BIT_Z, (me // BIT_Y) % 2, (me // BIT_X) % 2, me % 2
        pos_piece = lax.select_n(z, *mlp_z)
        pos_piece = jnp.where(y == 0, pos_piece, swap(pos_piece, BIT_Y))
        pos_piece = jnp.where(x == 0, pos_piece, swap(pos_piece, BIT_X))
        pos_arrays = [pos_piece, swap(pos_piece, BIT_CORE)]
        pos_names = jnp.stack([core, 1 - core])
        attn_arrays, mlp_arrays = spread_rest(attn_z), spread_rest(mlp_z)
        out_plan = sum_plan()
    else:
        mask = jnp.zeros_like(me)
        order = list(range(count))
        attn_arrays = [(lax.all_gather(attn_piece, AXES, axis=0, tiled=True), order)]
        mlp_arrays = [(lax.all_gather(mlp_piece, AXES, axis=0, tiled=True), order)]
        height = sizes.mlp_rows
        pos_arrays = [mlp_arrays[0][0][j * height : (j + 1) * height] for j in range(sizes.pos_count)]
        pos_names = jnp.arange(sizes.pos_count, dtype=jnp.int32)
        out_plan = [order]
    mask = mask.reshape(1)

    ends = jnp.cumsum(lengths)
    slot_index = jnp.arange(rows, dtype=jnp.int32)
    segments = jnp.sum((slot_index[:, None] >= ends[None, :]).astype(jnp.int32), axis=1)
    segments = jnp.where(slot_index < slots, segments, images + 1)
    live = (segments < images)[:slots, None]
    seg_row = segments.astype(F32).reshape(1, rows)
    seg_col = segments.astype(F32).reshape(rows, 1)
    extra = ((0, rows - slots), (0, 0))
    out_grad = jnp.pad(jnp.where(live, cotangent, jnp.zeros_like(cotangent)), extra)
    tokens_full = jnp.pad(tokens, extra)
    pos_full = jnp.pad(pos_map, (0, rows - slots), constant_values=255)
    onehot = (pos_full[:, None] == jnp.arange(256, dtype=jnp.int32)[None, :]).astype(BF16)

    (embedded, normed_b, qkv, key_t, mixed, log_total, residual, w_qkv, w_out, vectors) = attn_forward(
        images, entries, attn_arrays, pos_arrays, pos_names, mask, seg_row, seg_col, onehot, tokens_full, sizes
    )
    output, d_residual, *mlp_sent = mlp_both(
        entries[1], mlp_arrays, mask, residual, out_grad, slots, out_plan, sizes
    )
    kept = (seg_row, seg_col, onehot, embedded, normed_b, qkv, key_t, mixed, log_total, w_qkv, w_out, vectors)
    in_grad, pos_grad, *attn_sent = attn_backward(
        images, entries[0], mask, kept, d_residual, slots, out_plan, sizes
    )

    if by_hand:
        mlp_terms = sum_pieces(*mlp_sent)
        attn_terms = sum_pieces(*attn_sent)
        offset = entries[1] // TILE * 8
        halves = [pos_grad[: sizes.mlp_rows], pos_grad[offset : offset + sizes.mlp_rows]]
        keep = jnp.where(core == 0, halves[0], halves[1])
        send = jnp.where(core == 0, halves[1], halves[0])
        keep = (keep.astype(F32) + swap(send, BIT_CORE).astype(F32)).astype(BF16)
        pos_terms = sum_everywhere(keep)
    else:
        mlp_terms = [lax.psum_scatter(mlp_sent[0], AXES, scatter_dimension=0, tiled=True)]
        attn_terms = [lax.psum_scatter(attn_sent[0], AXES, scatter_dimension=0, tiled=True)]
        pos_sum = jnp.pad(lax.psum(pos_grad, AXES), ((0, sizes.mlp_rows), (0, 0)))
        first_row = jnp.minimum((me * entries[1]) // TILE * 8, sizes.pos_flat)
        pos_terms = [lax.dynamic_slice_in_dim(pos_sum, first_row, sizes.mlp_rows, axis=0)]
        place = place.at[4].set(1)
    scale = 1.0 / math.sqrt(slots * count)
    attn_grad, mlp_grad = settle(scale, place, attn_terms, mlp_terms, pos_terms)
    attn_grad = attn_grad.reshape(-1)[: entries[0]]
    mlp_grad = mlp_grad.reshape(-1)[: entries[1]]
    attn_step, attn_first_new, attn_second_new = adamw_step(attn_grad, attn_params, attn_first, attn_second)
    mlp_step, mlp_first_new, mlp_second_new = adamw_step(mlp_grad, mlp_params, mlp_first, mlp_second)
    return (
        output,
        in_grad,
        attn_grad,
        attn_step,
        attn_first_new,
        attn_second_new,
        mlp_grad,
        mlp_step,
        mlp_first_new,
        mlp_second_new,
    )


def solution(mesh):
    split = P(AXES)
    split_rows = P(AXES, None)
    by_hand = mesh.shape["dp"] == 8 and mesh.shape["rep"] == 4
    return jax.shard_map(
        functools.partial(body, by_hand),
        mesh=mesh,
        in_specs=(split_rows, split_rows) + (split,) * 8,
        out_specs=(split_rows, split_rows) + (split,) * 8,
        check_vma=False,
    )
```

```python
import functools
import math

import jax
import jax.numpy as jnp
from jax import lax
from jax.experimental import pallas as pl
from jax.experimental.pallas import tpu as pltpu
from jax.sharding import PartitionSpec as P

D = 384
H = 6
DH = 64
FF = 1536
POS = 145
SHORT = 50
LONG = 145
MOST_LONG = 4
STEP = 10
LANES = 128
TILE = 8 * LANES
PAIRS = H // 2
QKV_COLS = 3 * D // LANES
D_COLS = D // LANES
FF_COLS = FF // LANES

LEARNING_RATE = 0.001
WEIGHT_DECAY = 0.05
BETA_FIRST = 0.9
BETA_SECOND = 0.999
adam_eps = 1e-08

F32 = jnp.float32
BF16 = jnp.bfloat16
NT = (((1,), (1,)), ((), ()))
TN = (((0,), (0,)), ((), ()))
NN = (((1,), (0,)), ((), ()))
BLOCK = 128
PART = 256

ROW_GAIN_ONE = 0
ROW_BIAS_ONE = ROW_GAIN_ONE + D_COLS
ROW_W_QKV = ROW_BIAS_ONE + D_COLS
ROW_B_QKV = ROW_W_QKV + D * QKV_COLS
ROW_W_OUT = ROW_B_QKV + QKV_COLS
ROW_B_OUT = ROW_W_OUT + D * D_COLS
ATTN_ROWS = ROW_B_OUT + D_COLS
ROW_POS = 0
ROW_GAIN_TWO = ROW_POS + POS * D_COLS
ROW_BIAS_TWO = ROW_GAIN_TWO + D_COLS
ROW_W_IN = ROW_BIAS_TWO + D_COLS
ROW_B_IN = ROW_W_IN + D * FF_COLS
ROW_W_BACK = ROW_B_IN + FF_COLS
ROW_B_BACK = ROW_W_BACK + FF * D_COLS
MLP_ROWS = ROW_B_BACK + D_COLS


def dot(a, b, dims=NN):
    return lax.dot_general(a, b, dims, preferred_element_type=F32)


def tile_row(entries, j):
    return pl.multiple_of(((j * entries) // TILE) * 8, 8)


def piece_rows(entries, count):
    most = max((entries * j) % TILE + entries for j in range(count))
    return -(-most // (16 * LANES)) * 16


def flat_rows(entries, count, rows):
    return max((entries * j) // TILE * 8 + rows for j in range(count))


def params(mebibytes):
    return pltpu.CompilerParams(vmem_limit_bytes=mebibytes * 1024 * 1024)


def cost(microseconds):
    return pl.CostEstimate(flops=int(microseconds * 1.15e9), bytes_accessed=1024, transcendentals=0)


def whole(shape):
    return pl.BlockSpec(shape, lambda *_: (0,) * len(shape))


SMEM_SPEC = pl.BlockSpec(memory_space=pltpu.SMEM)
VMEM_SPEC = pl.BlockSpec(memory_space=pltpu.VMEM)


def tall(vector, rows):
    entries = vector.shape[0]
    full = entries // TILE * TILE
    parts = [vector[pl.ds(0, full)].reshape(full // LANES, LANES)] if full else []
    if entries > full:
        rest = jnp.concatenate([vector[pl.ds(full, entries - full)], jnp.zeros((full + TILE - entries,), F32)])
        parts.append(rest.reshape(8, LANES))
    height = sum(part.shape[0] for part in parts)
    if height < rows:
        parts.append(jnp.zeros((rows - height, LANES), F32))
    return jnp.concatenate(parts, axis=0)


def put_flat(vector, value):
    entries = vector.shape[0]
    full = entries // TILE * TILE
    if full:
        vector[pl.ds(0, full)] = value[: full // LANES].reshape(full)
    if entries > full:
        vector[pl.ds(full, entries - full)] = value[full // LANES : full // LANES + 8].reshape(TILE)[: entries - full]


def align_kernel(place, attn, mlp, attn_out, mlp_out):
    for n, (source, target) in enumerate(((attn, attn_out), (mlp, mlp_out))):
        lanes, rows = place[2 * n], place[2 * n + 1]
        value = tall(source, target.shape[0])
        turned = pltpu.roll(value, lanes, 1)
        below = pltpu.roll(turned, 1, 0)
        lane = lax.broadcasted_iota(jnp.int32, value.shape, 1)
        moved = jnp.where(lane >= lanes, turned, below)
        target[...] = pltpu.roll(moved, rows, 0).astype(BF16)


def take_share(value, lanes, rows):
    height = value.shape[0]
    value = pltpu.roll(value, (height - rows) % height, 0)
    turned = pltpu.roll(value, (LANES - lanes) % LANES, 1)
    above = pltpu.roll(turned, height - 1, 0)
    lane = lax.broadcasted_iota(jnp.int32, value.shape, 1)
    return jnp.where(lane < LANES - lanes, turned, above)


def unpack(flat, arrays, entries, rows, me):
    flat[...] = jnp.zeros_like(flat)
    for ref, numbers in arrays:
        for t, number in enumerate(numbers):
            start = tile_row(entries, number ^ me)
            flat[pl.ds(start, rows), :] += ref[t * rows : (t + 1) * rows, :].astype(F32)


def read_matrix(flat, row, depth, cols, target):
    for c in range(cols):
        target[:, c * LANES : (c + 1) * LANES] = flat[pl.ds(row + c, depth, stride=cols), :].astype(BF16)


def read_row(flat, row, cols):
    return jnp.concatenate([flat[row + c : row + c + 1, :] for c in range(cols)], axis=1)


def write_row(flat, row, value):
    for c in range(value.shape[1] // LANES):
        flat[row + c : row + c + 1, :] = value[:, c * LANES : (c + 1) * LANES]


def norm_parts(value):
    average = jnp.mean(value, axis=-1, keepdims=True)
    centred = value - average
    variance = jnp.mean(centred * centred, axis=-1, keepdims=True)
    inverse = lax.rsqrt(variance + 1e-06)
    return centred * inverse, inverse


def norm_back(normed, inverse, gain, grad):
    scaled = grad * gain
    first = jnp.mean(scaled, axis=-1, keepdims=True)
    second = jnp.mean(scaled * normed, axis=-1, keepdims=True)
    return (scaled - first - normed * second) * inverse


def fold_rows(value):
    return jnp.sum(value.reshape(-1, 8, value.shape[-1]), axis=0)


def call(kernel, name, operands, outs, scratch, mebibytes, microseconds):
    return pl.pallas_call(
        kernel,
        in_specs=[SMEM_SPEC if a.dtype == jnp.int32 and a.ndim == 1 else VMEM_SPEC for a in operands],
        out_specs=[VMEM_SPEC] * len(outs),
        out_shape=[jax.ShapeDtypeStruct(shape, kind) for shape, kind in outs],
        scratch_shapes=scratch,
        compiler_params=params(mebibytes),
        cost_estimate=cost(microseconds),
        name=name,
    )(*operands)


def project_kernel(entries, attn_plan, pos_count, attn_rows, mlp_rows, me, pos_names, onehot, tokens, *refs):
    attn_arrays = [(refs[i], plan) for i, plan in enumerate(attn_plan)]
    refs = refs[len(attn_plan) :]
    pos_arrays, refs = refs[:pos_count], refs[pos_count:]
    embedded, normed_out, qkv, w_qkv, w_out, vectors = refs[:6]
    flat, pos_flat, pos_table = refs[6:]
    slots, rows = tokens.shape[0], embedded.shape[0]

    pos_flat[...] = jnp.zeros_like(pos_flat)
    for n, ref in enumerate(pos_arrays):
        start = tile_row(entries[1], pos_names[n])
        pos_flat[pl.ds(start, mlp_rows), :] += ref[...].astype(F32)
    pos_table[...] = jnp.zeros_like(pos_table)
    most = POS // 16 * 16
    for c in range(D_COLS):
        column = pos_flat[pl.ds(ROW_POS + c, most, stride=D_COLS), :]
        pos_table[0:most, c * LANES : (c + 1) * LANES] = column.astype(BF16)
    last = [read_row(pos_flat, ROW_POS + r * D_COLS, D_COLS) for r in range(most, POS)]
    last = jnp.concatenate(last + [jnp.zeros((16 - len(last), D), F32)], axis=0)
    pos_table[most : most + 16, :] = last.astype(BF16)

    unpack(flat, attn_arrays, entries[0], attn_rows, me[0])
    read_matrix(flat, ROW_W_QKV, D, QKV_COLS, w_qkv)
    read_matrix(flat, ROW_W_OUT, D, D_COLS, w_out)
    gain = read_row(flat, ROW_GAIN_ONE, D_COLS)
    bias = read_row(flat, ROW_BIAS_ONE, D_COLS)
    b_qkv = read_row(flat, ROW_B_QKV, QKV_COLS)
    vectors[...] = jnp.zeros_like(vectors)
    vectors[0:1, :] = gain
    vectors[1:2, :] = read_row(flat, ROW_B_OUT, D_COLS)

    embedded[0:slots, :] = tokens[...].astype(F32)
    embedded[slots:rows, :] = jnp.zeros((rows - slots, D), F32)
    for c in range(QKV_COLS):
        qkv[c, rows : qkv.shape[1], :] = jnp.zeros((qkv.shape[1] - rows, LANES), F32)

    def project(i, _):
        at = pl.ds(pl.multiple_of(i * PART, PART), PART)
        value = embedded[at, :] + dot(onehot[at, :], pos_table[...])
        embedded[at, :] = value
        normed, _ = norm_parts(value)
        normed = (normed * gain + bias).astype(BF16)
        normed_out[at, :] = normed
        for k in range(3):
            cols = slice(k * D, (k + 1) * D)
            part = (dot(normed, w_qkv[:, cols]) + b_qkv[:, cols]).astype(BF16).astype(F32)
            if k == 0:
                part = part * DH ** (-0.5)
            for c in range(D_COLS):
                qkv[k * D_COLS + c, at, :] = part[:, c * LANES : (c + 1) * LANES]
        return 0

    lax.fori_loop(0, rows // PART, project, 0)


def project(entries, attn_arrays, pos_arrays, pos_names, me, onehot, tokens, sizes):
    rows = onehot.shape[0]
    plan = [numbers for _, numbers in attn_arrays]
    operands = [me, pos_names, onehot, tokens] + [a for a, _ in attn_arrays] + list(pos_arrays)
    outs = [
        ((rows, D), F32),
        ((rows, D), BF16),
        ((QKV_COLS, sizes.reach, LANES), F32),
        ((D, 3 * D), BF16),
        ((D, D), BF16),
        ((8, D), F32),
    ]
    scratch = [
        pltpu.VMEM((sizes.attn_flat, LANES), F32),
        pltpu.VMEM((sizes.pos_flat, LANES), F32),
        pltpu.VMEM((256, D), BF16),
    ]
    kernel = functools.partial(
        project_kernel, entries, plan, len(pos_arrays), sizes.attn_rows, sizes.mlp_rows
    )
    return call(kernel, "project", operands, outs, scratch, 24, 8)


def image_table(lengths, table):
    images = table.shape[1]
    longs = sum((lengths[i] == LONG).astype(jnp.int32) for i in range(images))
    start, long_seen, short_seen = jnp.int32(0), jnp.int32(0), longs
    for i in range(images):
        length = lengths[i]
        is_long = length == LONG
        place = jnp.where(is_long, long_seen, short_seen)
        table[0, place] = start
        table[1, place] = length
        start = start + length
        long_seen = long_seen + is_long.astype(jnp.int32)
        short_seen = short_seen + 1 - is_long.astype(jnp.int32)
    return start


def image_rows(slot):
    return -(-((LONG if slot < MOST_LONG else SHORT) + 7) // 32) * 32


def both_heads(value):
    left = lax.broadcasted_iota(jnp.int32, value.shape, 1) < DH
    zero = jnp.zeros_like(value)
    return jnp.concatenate([jnp.where(left, value, zero), jnp.where(left, zero, value)], axis=0)


def one_of_heads(value):
    height = value.shape[0] // 2
    left = lax.broadcasted_iota(jnp.int32, (height, LANES), 1) < DH
    return jnp.where(left, value[:height], value[height:])


def inside(height, low, length):
    row = lax.broadcasted_iota(jnp.int32, (height, LANES), 0)
    return (row >= low) & (row < low + length)


def attend(queries, keys, values, mask):
    scores = dot(keys, both_heads(queries), NT)
    scores = jnp.where(mask, scores, -1e30)
    peak = jnp.max(scores, axis=0, keepdims=True)
    probs = jnp.exp(scores - peak)
    total = jnp.sum(probs, axis=0, keepdims=True)
    out = dot(values.T.astype(BF16), probs.astype(BF16)) * (1.0 / total)
    return one_of_heads(out.T), peak + jnp.log(total)


def key_mask(height, width, low, length):
    row = lax.broadcasted_iota(jnp.int32, (height, width), 0)
    return (row >= low) & (row < low + length)


def attend_kernel(slots, lengths, qkv, embedded, w_out, vectors, mixed, log_total, residual, table):
    images = lengths.shape[0]
    rows = residual.shape[0]
    live = image_table(lengths, table)
    mixed[...] = jnp.zeros_like(mixed)
    for slot in range(images):
        height = image_rows(slot)
        low = table[0, slot] % 8
        at = pl.ds(pl.multiple_of(table[0, slot] - low, 8), height)
        length = table[1, slot]
        mask = key_mask(height, 2 * height, low, length)
        valid = inside(height, low, length)
        for pair in range(PAIRS):
            out, total = attend(
                qkv[pair, at, :].astype(BF16),
                qkv[PAIRS + pair, at, :].astype(BF16),
                qkv[2 * PAIRS + pair, at, :],
                mask,
            )
            log_total[slot * PAIRS + pair, :, 0 : 2 * height] = total
            pltpu.store(mixed.at[pair, at, :], out.astype(BF16).astype(F32), mask=valid)

    low = live % 8
    base = pl.multiple_of(live - low, 8)
    length = slots - live
    most = -(-(slots - images * SHORT + 7) // BLOCK) if (images * SHORT) % 8 else -(-(slots - images * SHORT) // BLOCK)
    for blocks in range(1, most + 1):

        @pl.when((low + length > (blocks - 1) * BLOCK) & (low + length <= blocks * BLOCK))
        def _():
            height = blocks * BLOCK
            mask = key_mask(height, 2 * BLOCK, low, length)
            for pair in range(PAIRS):
                keys = qkv[PAIRS + pair, pl.ds(base, height), :].astype(BF16)
                values = qkv[2 * PAIRS + pair, pl.ds(base, height), :]
                for block in range(blocks):
                    at = pl.ds(pl.multiple_of(base + block * BLOCK, 8), BLOCK)
                    out, _ = attend(qkv[pair, at, :].astype(BF16), keys, values, mask)
                    valid = inside(BLOCK, low - block * BLOCK, length)
                    pltpu.store(mixed.at[pair, at, :], out.astype(BF16).astype(F32), mask=valid)

    def finish(i, _):
        at = pl.ds(pl.multiple_of(i * PART, PART), PART)
        together = jnp.concatenate([mixed[c, at, :] for c in range(D_COLS)], axis=1).astype(BF16)
        residual[at, :] = embedded[at, :] + dot(together, w_out[...]) + vectors[1:2, :]
        return 0

    lax.fori_loop(0, rows // PART, finish, 0)


def attend_all(slots, lengths, qkv, embedded, w_out, vectors):
    rows = embedded.shape[0]
    images = lengths.shape[0]
    outs = [((PAIRS,) + qkv.shape[1:], F32), ((images * PAIRS, 1, 2 * image_rows(0)), F32), ((rows, D), F32)]
    scratch = [pltpu.SMEM((2, images), jnp.int32)]
    operands = [lengths, qkv, embedded, w_out, vectors]
    return call(functools.partial(attend_kernel, slots), "attend", operands, outs, scratch, 24, 10)


def gelu_parts(value):
    size = jnp.abs(value)
    near = 1.0 / (1.0 + (0.3275911 * math.sqrt(0.5)) * size)
    bell = jnp.exp(-0.5 * value * value)
    series = near * (
        0.5 * 0.254829592
        + near
        * (0.5 * -0.284496736 + near * (0.5 * 1.421413741 + near * (0.5 * -1.453152027 + near * (0.5 * 1.061405429))))
    )
    tail = series * bell
    share = jnp.where(value >= 0, 1.0 - tail, tail)
    return value * share, share + value * bell * (1.0 / math.sqrt(2.0 * math.pi))


def pack(flat, entries, rows, me, targets):
    for ref, numbers in targets:
        for t, number in enumerate(numbers):
            start = tile_row(entries, number ^ me)
            ref[t * rows : (t + 1) * rows, :] = flat[pl.ds(start, rows), :].astype(BF16)


def mlp_kernel(entries, in_plan, out_plan, piece, mask, me, lengths, residual, cotangent, *refs):
    arrays = [(refs[i], plan) for i, plan in enumerate(in_plan)]
    refs = refs[len(in_plan) :]
    output, d_residual = refs[:2]
    targets = [(refs[2 + i], plan) for i, plan in enumerate(out_plan)]
    refs = refs[2 + len(out_plan) :]
    flat, w_in, w_back, normed_b, active_b, d_hidden_b, out_f32, sums_in, sums, out_grad = refs
    slots, rows = cotangent.shape[0], residual.shape[0]
    live = sum(lengths[i] for i in range(lengths.shape[0]))
    row = lax.broadcasted_iota(jnp.int32, (slots, D), 0)
    out_grad[0:slots, :] = jnp.where(row < live, cotangent[...].astype(F32), 0.0).astype(BF16)
    out_grad[slots:rows, :] = jnp.zeros((rows - slots, D), BF16)

    unpack(flat, arrays, entries, piece, mask[0])
    read_matrix(flat, ROW_W_IN, D, FF_COLS, w_in)
    read_matrix(flat, ROW_W_BACK, FF, D_COLS, w_back)
    gain = read_row(flat, ROW_GAIN_TWO, D_COLS)
    bias = read_row(flat, ROW_BIAS_TWO, D_COLS)
    b_in = read_row(flat, ROW_B_IN, FF_COLS)
    b_back = read_row(flat, ROW_B_BACK, D_COLS)
    sums[...] = jnp.zeros_like(sums)
    sums_in[...] = jnp.zeros_like(sums_in)

    def step(i, _):
        at = pl.ds(pl.multiple_of(i * PART, PART), PART)
        value = residual[at, :]
        grad_b = out_grad[at, :]
        normed, inverse = norm_parts(value)
        low = (normed * gain + bias).astype(BF16)
        normed_b[at, :] = low
        for c in range(FF // 256):
            cols = slice(c * 256, (c + 1) * 256)
            hidden = dot(low, w_in[:, cols]) + b_in[:, cols]
            d_active = dot(grad_b, w_back[cols, :], NT)
            active, slope = gelu_parts(hidden)
            d_hidden = (d_active * slope).astype(BF16)
            active_b[at, cols] = active.astype(BF16)
            d_hidden_b[at, cols] = d_hidden
            sums_in[:, cols] += fold_rows(d_hidden.astype(F32))
        out_f32[at, :] = value + b_back + dot(active_b[at, :], w_back[...])
        d_normed = dot(d_hidden_b[at, :], w_in[...], NT)
        grad = grad_b.astype(F32)
        d_residual[at, :] = grad + norm_back(normed, inverse, gain, d_normed)
        sums[0] += fold_rows(d_normed * normed)
        sums[1] += fold_rows(d_normed)
        sums[2] += fold_rows(grad)
        return 0

    lax.fori_loop(0, rows // PART, step, 0)
    output[...] = out_f32[0 : output.shape[0], :].astype(BF16)

    flat[...] = jnp.zeros_like(flat)
    write_row(flat, ROW_GAIN_TWO, jnp.sum(sums[0], axis=0, keepdims=True))
    write_row(flat, ROW_BIAS_TWO, jnp.sum(sums[1], axis=0, keepdims=True))
    write_row(flat, ROW_B_IN, jnp.sum(sums_in[...], axis=0, keepdims=True))
    write_row(flat, ROW_B_BACK, jnp.sum(sums[2], axis=0, keepdims=True))
    normed_t = normed_b[...].T
    for c in range(0, FF_COLS, 2):
        part = dot(normed_t, d_hidden_b[:, c * LANES : (c + 2) * LANES])
        for k in range(2):
            flat[pl.ds(ROW_W_IN + c + k, D, stride=FF_COLS), :] = part[:, k * LANES : (k + 1) * LANES]
    for r in range(0, FF, 256):
        part = dot(active_b[:, r : r + 256], out_grad[...], TN)
        for c in range(D_COLS):
            flat[pl.ds(ROW_W_BACK + r * D_COLS + c, 256, stride=D_COLS), :] = part[:, c * LANES : (c + 1) * LANES]
    pack(flat, entries, piece, me[0], targets)


def mlp_both(entries, arrays, mask, me, lengths, residual, cotangent, out_plan, sizes):
    rows = residual.shape[0]
    plan = [numbers for _, numbers in arrays]
    operands = [mask, me, lengths, residual, cotangent] + [a for a, _ in arrays]
    outs = [(cotangent.shape, BF16), ((rows, D), F32)]
    outs += [((len(n) * sizes.mlp_rows, LANES), BF16) for n in out_plan]
    scratch = [
        pltpu.VMEM((sizes.mlp_flat, LANES), F32),
        pltpu.VMEM((D, FF), BF16),
        pltpu.VMEM((FF, D), BF16),
        pltpu.VMEM((rows, D), BF16),
        pltpu.VMEM((rows, FF), BF16),
        pltpu.VMEM((rows, FF), BF16),
        pltpu.VMEM((rows, D), F32),
        pltpu.VMEM((8, FF), F32),
        pltpu.VMEM((3, 8, D), F32),
        pltpu.VMEM((rows, D), BF16),
    ]
    kernel = functools.partial(mlp_kernel, entries, plan, out_plan, sizes.mlp_rows)
    return call(kernel, "feed_forward", operands, outs, scratch, 36, 18)


def attend_back_kernel(lengths, qkv, mixed, log_total, w_out, d_residual, d_qkv, d_branch_b, b_out_sum, d_mixed, table):
    images = lengths.shape[0]
    rows = d_residual.shape[0]
    image_table(lengths, table)
    d_qkv[...] = jnp.zeros_like(d_qkv)
    b_out_sum[...] = jnp.zeros_like(b_out_sum)

    def enter(i, _):
        at = pl.ds(pl.multiple_of(i * PART, PART), PART)
        branch = d_residual[at, :].astype(BF16)
        d_branch_b[at, :] = branch
        b_out_sum[...] += fold_rows(branch.astype(F32))
        value = dot(branch, w_out[...], NT).astype(BF16).astype(F32)
        for c in range(D_COLS):
            d_mixed[c, at, :] = value[:, c * LANES : (c + 1) * LANES]
        return 0

    lax.fori_loop(0, rows // PART, enter, 0)
    for c in range(D_COLS):
        d_mixed[c, rows : d_mixed.shape[1], :] = jnp.zeros((d_mixed.shape[1] - rows, LANES), F32)

    ones = jnp.ones((8, LANES), BF16)
    for slot in range(images):
        height = image_rows(slot)
        low = table[0, slot] % 8
        at = pl.ds(pl.multiple_of(table[0, slot] - low, 8), height)
        length = table[1, slot]
        mask = key_mask(height, 2 * height, low, length)
        valid = inside(height, low, length)
        for pair in range(PAIRS):
            queries = both_heads(qkv[pair, at, :].astype(BF16))
            keys = qkv[PAIRS + pair, at, :]
            grad = jnp.where(valid, d_mixed[pair, at, :], 0.0)
            grads = both_heads(grad.astype(BF16))
            scores = dot(keys.astype(BF16), queries, NT)
            scores = jnp.where(mask, scores, -1e30)
            probs = jnp.exp(scores - log_total[slot * PAIRS + pair, :, 0 : 2 * height])
            product = both_heads(grad * mixed[pair, at, :])
            upper = product.astype(BF16)
            lower = (product - upper.astype(F32)).astype(BF16)
            delta = (dot(ones, upper, NT) + dot(ones, lower, NT))[0:1, :]
            d_probs = dot(qkv[2 * PAIRS + pair, at, :].astype(BF16), grads, NT)
            d_scores = (probs * (d_probs - delta)).astype(BF16)
            d_values = dot(probs.astype(BF16), grads)
            d_keys = dot(d_scores, queries)
            d_queries = one_of_heads((dot(keys.T.astype(BF16), d_scores) * DH ** (-0.5)).T)
            pltpu.store(d_qkv.at[pair, at, :], d_queries, mask=valid)
            pltpu.store(d_qkv.at[PAIRS + pair, at, :], d_keys, mask=valid)
            pltpu.store(d_qkv.at[2 * PAIRS + pair, at, :], d_values, mask=valid)


def attend_back(lengths, qkv, mixed, log_total, w_out, d_residual):
    rows = d_residual.shape[0]
    outs = [(qkv.shape, F32), ((rows, D), BF16), ((8, D), F32)]
    scratch = [pltpu.VMEM(mixed.shape, F32), pltpu.SMEM((2, lengths.shape[0]), jnp.int32)]
    operands = [lengths, qkv, mixed, log_total, w_out, d_residual]
    return call(attend_back_kernel, "attend_back", operands, outs, scratch, 28, 12)


def project_back_kernel(entries, out_plan, piece, me, *refs):
    (onehot, embedded, normed_b, mixed, d_qkv, d_branch_b, b_out_sum, w_qkv, vectors, d_residual) = refs[:10]
    in_grad, pos_out = refs[10:12]
    targets = [(refs[12 + i], plan) for i, plan in enumerate(out_plan)]
    flat, d_qkv_b, d_embedded_b, mixed_b, sums = refs[12 + len(out_plan) :]
    rows = embedded.shape[0]
    gain = vectors[0:1, :]
    sums[...] = jnp.zeros_like(sums)

    def leave(i, _):
        at = pl.ds(pl.multiple_of(i * PART, PART), PART)
        grads = jnp.concatenate([d_qkv[c, at, :] for c in range(QKV_COLS)], axis=1).astype(BF16)
        d_qkv_b[at, :] = grads
        mixed_b[at, :] = jnp.concatenate([mixed[c, at, :] for c in range(D_COLS)], axis=1).astype(BF16)
        d_normed = dot(grads, w_qkv[...], NT)
        normed, inverse = norm_parts(embedded[at, :])
        value = d_residual[at, :] + norm_back(normed, inverse, gain, d_normed)
        d_embedded_b[at, :] = value.astype(BF16)
        sums[0] += fold_rows(d_normed * normed)
        sums[1] += fold_rows(d_normed)
        return 0

    lax.fori_loop(0, rows // PART, leave, 0)
    in_grad[...] = d_embedded_b[0 : in_grad.shape[0], :]

    flat[...] = jnp.zeros_like(flat)
    write_row(flat, ROW_GAIN_ONE, jnp.sum(sums[0], axis=0, keepdims=True))
    write_row(flat, ROW_BIAS_ONE, jnp.sum(sums[1], axis=0, keepdims=True))
    write_row(flat, ROW_B_OUT, jnp.sum(b_out_sum[...], axis=0, keepdims=True))
    normed_t = normed_b[...].T
    for k in range(3):
        cols = slice(k * D, (k + 1) * D)
        part = dot(normed_t, d_qkv_b[:, cols])
        total = jnp.sum(fold_rows(d_qkv_b[:, cols].astype(F32)), axis=0, keepdims=True)
        write_row(flat, ROW_B_QKV + k * D_COLS, total)
        for c in range(D_COLS):
            flat[pl.ds(ROW_W_QKV + k * D_COLS + c, D, stride=QKV_COLS), :] = part[:, c * LANES : (c + 1) * LANES]
    part = dot(mixed_b[...].T, d_branch_b[...])
    for c in range(D_COLS):
        flat[pl.ds(ROW_W_OUT + c, D, stride=D_COLS), :] = part[:, c * LANES : (c + 1) * LANES]
    pack(flat, entries, piece, me[0], targets)

    pos_grad = dot(onehot[...], d_embedded_b[...], TN)
    flat[...] = jnp.zeros_like(flat)
    for c in range(D_COLS):
        flat[pl.ds(ROW_POS + c, POS, stride=D_COLS), :] = pos_grad[0:POS, c * LANES : (c + 1) * LANES]
    pos_out[...] = flat[0 : pos_out.shape[0], :].astype(BF16)


def project_back(entries, me, kept, out_rows, out_plan, sizes):
    rows = kept[1].shape[0]
    outs = [((out_rows, D), BF16), ((sizes.pos_flat, LANES), BF16)]
    outs += [((len(n) * sizes.attn_rows, LANES), BF16) for n in out_plan]
    scratch = [
        pltpu.VMEM((max(sizes.attn_flat, sizes.pos_flat), LANES), F32),
        pltpu.VMEM((rows, 3 * D), BF16),
        pltpu.VMEM((rows, D), BF16),
        pltpu.VMEM((rows, D), BF16),
        pltpu.VMEM((2, 8, D), F32),
    ]
    kernel = functools.partial(project_back_kernel, entries, out_plan, sizes.attn_rows)
    return call(kernel, "project_back", [me, *kept], outs, scratch, 28, 10)


def adamw_step(gradient, weights, first, second):
    first_new = BETA_FIRST * first + (1.0 - BETA_FIRST) * gradient
    second_new = BETA_SECOND * second + (1.0 - BETA_SECOND) * gradient * gradient
    first_hat = first_new / (1.0 - BETA_FIRST**STEP)
    second_hat = second_new / (1.0 - BETA_SECOND**STEP)
    update = LEARNING_RATE * (first_hat / (jnp.sqrt(second_hat) + adam_eps) + WEIGHT_DECAY * weights)
    return (update, first_new, second_new)


def settle_kernel(scale, counts, place, *refs):
    attn = refs[: counts[0]]
    mlp = refs[counts[0] : counts[0] + counts[1]]
    pos = refs[counts[0] + counts[1] : sum(counts)]
    refs = refs[sum(counts) :]
    state, outs = (refs[:3], refs[3:6]), (refs[6:10], refs[10:14])
    total = sum(ref[...].astype(F32) for ref in attn)
    extra = sum(ref[...].astype(F32) for ref in pos)
    other = sum(ref[...].astype(F32) for ref in mlp) + jnp.where(place[4] > 0, extra, 0.0)
    for n, value in enumerate((total, other)):
        rows = value.shape[0]
        gradient = take_share(value, place[2 * n], place[2 * n + 1]) * scale
        weights, first, second = (tall(ref, rows) for ref in state[n])
        for ref, result in zip(outs[n], (gradient, *adamw_step(gradient, weights, first, second))):
            put_flat(ref, result)


def settle(scale, place, attn, mlp, pos, attn_state, mlp_state):
    operands = list(attn) + list(mlp) + list(pos) + list(attn_state) + list(mlp_state)
    shapes = [attn_state[0].shape] * 4 + [mlp_state[0].shape] * 4
    return pl.pallas_call(
        functools.partial(settle_kernel, scale, (len(attn), len(mlp), len(pos))),
        in_specs=[SMEM_SPEC] + [VMEM_SPEC] * len(operands),
        out_specs=[VMEM_SPEC] * len(shapes),
        out_shape=[jax.ShapeDtypeStruct(shape, F32) for shape in shapes],
        compiler_params=params(8),
        name="settle",
    )(place, *operands)


AXES = ("dp", "rep")
BIT_CORE, BIT_X, BIT_Y, BIT_Z = 1, 2, 4, 8
PLANE = (BIT_X, BIT_Y, BIT_X | BIT_Y)
DEVICES = 32


def swap(value, bits):
    return lax.ppermute(value, AXES, [(j, j ^ bits) for j in range(DEVICES)])


def together(*values):
    return lax.optimization_barrier(values)


def spread_z(piece):
    return [piece] + [swap(piece, k * BIT_Z) for k in (1, 2, 3)]


def spread_xy(value):
    return [value] + [swap(value, bits) for bits in PLANE]


def numbered(arrays):
    offsets = [core | bits for core in (0, BIT_CORE) for bits in (0, *PLANE)]
    return [(a, [offset | z * BIT_Z for z in range(4)]) for a, offset in zip(arrays, offsets)]


def sum_plan():
    return [[BIT_CORE | bits | z * BIT_Z for bits in (0, *PLANE) for z in range(4)]] + [
        [bits | z * BIT_Z for z in range(4)] for bits in (0, *PLANE)
    ]


def total(values):
    return sum(value.astype(F32) for value in values).astype(BF16)


def quarters(value):
    return [value[k * value.shape[0] // 4 : (k + 1) * value.shape[0] // 4] for k in range(4)]


def add_core(sent):
    came = quarters(swap(sent[0], BIT_CORE))
    return [total(both) for both in zip(sent[1:], came)]


def swap_xy(parts):
    return [parts[0]] + [swap(part, bits) for part, bits in zip(parts[1:], PLANE)]


def swap_z(parts):
    return [parts[0]] + [swap(parts[k], k * BIT_Z) for k in (1, 2, 3)]


class Sizes:
    def __init__(self, count, slots, attn_entries, mlp_entries):
        self.attn_rows = piece_rows(attn_entries, count)
        self.mlp_rows = piece_rows(mlp_entries, count)
        self.attn_flat = max(flat_rows(attn_entries, count, self.attn_rows), ATTN_ROWS)
        self.mlp_flat = max(flat_rows(mlp_entries, count, self.mlp_rows), MLP_ROWS)
        self.pos_count = -(-POS * D // mlp_entries)
        self.pos_flat = flat_rows(mlp_entries, self.pos_count, self.mlp_rows)
        self.pos_flat = max(-(-self.pos_flat // 16) * 16, -(-POS * D_COLS // 16) * 16)
        self.reach = slots + max(image_rows(0), 2 * BLOCK)


class Layer:
    def __init__(self, entries, sizes, slots, tokens, cotangent, lengths, onehot):
        self.entries, self.sizes, self.slots = entries, sizes, slots
        self.tokens, self.cotangent, self.lengths, self.onehot = tokens, cotangent, lengths, onehot

    def project(self, mask, attn_arrays, pos_arrays, pos_names):
        self.mask = mask
        (self.embedded, self.normed_b, self.qkv, self.w_qkv, self.w_out, self.vectors) = project(
            self.entries, attn_arrays, pos_arrays, pos_names, mask, self.onehot, self.tokens, self.sizes
        )

    def attend(self):
        self.mixed, self.log_total, self.residual = attend_all(
            self.slots, self.lengths, self.qkv, self.embedded, self.w_out, self.vectors
        )

    def feed_forward(self, mlp_arrays, mask, plan):
        self.output, self.d_residual, *sent = mlp_both(
            self.entries[1], mlp_arrays, mask, self.mask, self.lengths, self.residual, self.cotangent, plan, self.sizes
        )
        return sent

    def attend_back(self):
        self.d_qkv, self.d_branch_b, self.b_out_sum = attend_back(
            self.lengths, self.qkv, self.mixed, self.log_total, self.w_out, self.d_residual
        )

    def project_back(self, plan):
        kept = (self.onehot, self.embedded, self.normed_b, self.mixed, self.d_qkv, self.d_branch_b)
        kept += (self.b_out_sum, self.w_qkv, self.vectors, self.d_residual)
        self.in_grad, pos_grad, *sent = project_back(self.entries[0], self.mask, kept, self.slots, plan, self.sizes)
        return pos_grad, sent


def step_by_axes(layer, me, attn_piece, mlp_piece):
    sizes, count = layer.sizes, lax.axis_size("dp") * lax.axis_size("rep")
    order = list(range(count))
    height = sizes.mlp_rows
    attn_all = lax.all_gather(attn_piece, AXES, axis=0, tiled=True)
    mlp_all = lax.all_gather(mlp_piece, AXES, axis=0, tiled=True)
    pos_arrays = [mlp_all[j * height : (j + 1) * height] for j in range(sizes.pos_count)]
    pos_names = jnp.arange(sizes.pos_count, dtype=jnp.int32)
    layer.project(jnp.zeros((1,), jnp.int32), [(attn_all, order)], pos_arrays, pos_names)
    layer.attend()
    mlp_sent = layer.feed_forward([(mlp_all, order)], layer.mask, [order])
    layer.attend_back()
    pos_grad, attn_sent = layer.project_back([order])
    mlp_terms = [lax.psum_scatter(mlp_sent[0], AXES, scatter_dimension=0, tiled=True)]
    attn_terms = [lax.psum_scatter(attn_sent[0], AXES, scatter_dimension=0, tiled=True)]
    pos_sum = jnp.pad(lax.psum(pos_grad, AXES), ((0, height), (0, 0)))
    first_row = jnp.minimum((me * layer.entries[1]) // TILE * 8, sizes.pos_flat)
    pos_terms = [lax.dynamic_slice_in_dim(pos_sum, first_row, height, axis=0)]
    return (layer.output, layer.in_grad), (attn_terms, mlp_terms, pos_terms)


def step_by_hand(layer, me, attn_piece, mlp_piece):
    sizes = layer.sizes
    z, plane, core = me // BIT_Z, (me // BIT_X) % 4, me % 2
    plan = sum_plan()
    attn_z, mlp_z = spread_z(attn_piece), spread_z(mlp_piece)
    attn_z, layer.onehot = together(attn_z, layer.onehot)
    attn = jnp.concatenate(attn_z, axis=0)
    attn = spread_xy(attn)
    pos = lax.select_n(z, *mlp_z)
    pos = lax.select_n(plane, *spread_xy(pos))
    attn, pos, mlp_z = together(attn, pos, mlp_z)
    attn = attn + [swap(a, BIT_CORE) for a in attn]
    pos_arrays = [pos, swap(pos, BIT_CORE)]
    pos_names = jnp.stack([core, 1 - core])
    mlp = jnp.concatenate(mlp_z, axis=0)
    attn, pos_arrays, mlp = together(attn, pos_arrays, mlp)
    mlp = spread_xy(mlp)
    layer.project(me.reshape(1), numbered(attn), pos_arrays, pos_names)
    layer.attend()
    mlp, layer.residual = together(mlp, layer.residual)
    mlp = mlp + [swap(a, BIT_CORE) for a in mlp]
    mlp_sent = layer.feed_forward(numbered(mlp), layer.mask, plan)

    parts = add_core(mlp_sent)
    parts, layer.d_residual = together(parts, layer.d_residual)
    mlp_terms = swap_xy(parts)
    layer.attend_back()
    pos_grad, attn_sent = layer.project_back(plan)
    mlp_terms, pos_grad, attn_sent = together(mlp_terms, pos_grad, attn_sent)

    offset = layer.entries[1] // TILE * 8
    pos_parts = [pos_grad[: sizes.mlp_rows], pos_grad[offset : offset + sizes.mlp_rows]]
    pos_keep = jnp.where(core == 0, pos_parts[0], pos_parts[1])
    pos_send = jnp.where(core == 0, pos_parts[1], pos_parts[0])
    parts, pos = add_core(attn_sent), total([pos_keep, swap(pos_send, BIT_CORE)])
    mlp_parts = quarters(total(mlp_terms))
    parts, pos, mlp_parts = together(parts, pos, mlp_parts)
    attn_terms, pos_terms = swap_xy(parts), spread_xy(pos)
    mlp_terms = swap_z(mlp_parts)
    parts, pos = quarters(total(attn_terms)), total(pos_terms)
    parts, pos = together(parts, pos)
    attn_terms, pos_terms = swap_z(parts), spread_z(pos)
    return (layer.output, layer.in_grad), (attn_terms, mlp_terms, pos_terms)


def body(
    by_hand,
    tokens,
    cotangent,
    lengths,
    pos_map,
    attn_params,
    attn_first,
    attn_second,
    mlp_params,
    mlp_first,
    mlp_second,
):
    slots = tokens.shape[0]
    rows = -(-slots // PART) * PART
    count = lax.axis_size("dp") * lax.axis_size("rep")
    entries = (attn_params.shape[0], mlp_params.shape[0])
    sizes = Sizes(count, slots, *entries)
    me = lax.axis_index("dp") * lax.axis_size("rep") + lax.axis_index("rep")
    me = me.astype(jnp.int32)

    starts = [(me * n) % TILE for n in entries]
    place = jnp.stack(
        [starts[0] % LANES, starts[0] // LANES, starts[1] % LANES, starts[1] // LANES, (me < 2).astype(jnp.int32)]
    )
    attn_piece, mlp_piece = pl.pallas_call(
        align_kernel,
        in_specs=[SMEM_SPEC, VMEM_SPEC, VMEM_SPEC],
        out_specs=[VMEM_SPEC, VMEM_SPEC],
        out_shape=[
            jax.ShapeDtypeStruct((sizes.attn_rows, LANES), BF16),
            jax.ShapeDtypeStruct((sizes.mlp_rows, LANES), BF16),
        ],
        compiler_params=params(8),
        name="align",
    )(place, attn_params, mlp_params)

    pos_full = jnp.pad(pos_map, (0, rows - slots), constant_values=255)
    onehot = (pos_full[:, None] == jnp.arange(256, dtype=jnp.int32)[None, :]).astype(BF16)
    layer = Layer(entries, sizes, slots, tokens, cotangent, lengths, onehot)
    if by_hand:
        outputs, terms = step_by_hand(layer, me, attn_piece, mlp_piece)
    else:
        outputs, terms = step_by_axes(layer, me, attn_piece, mlp_piece)
        place = place.at[4].set(1)
    scale = 1.0 / math.sqrt(slots * count)
    attn_state, mlp_state = (attn_params, attn_first, attn_second), (mlp_params, mlp_first, mlp_second)
    updated = settle(scale, place, *terms, attn_state, mlp_state)
    return (*outputs, *updated)


def solution(mesh):
    split = P(AXES)
    split_rows = P(AXES, None)
    by_hand = mesh.shape["dp"] == 8 and mesh.shape["rep"] == 4
    return jax.shard_map(
        functools.partial(body, by_hand),
        mesh=mesh,
        in_specs=(split_rows, split_rows) + (split,) * 8,
        out_specs=(split_rows, split_rows) + (split,) * 8,
        check_vma=False,
    )
```

```python
import functools
import math

import jax
import jax.numpy as jnp
from jax import lax
from jax.experimental import pallas as pl
from jax.experimental.pallas import tpu as pltpu
from jax.sharding import PartitionSpec as P

D = 384
H = 6
DH = 64
FF = 1536
POS = 145
SHORT = 50
LONG = 145
MOST_LONG = 4
STEP = 10
LANES = 128
TILE = 8 * LANES
PAIRS = H // 2
QKV_COLS = 3 * D // LANES
D_COLS = D // LANES
FF_COLS = FF // LANES

LEARNING_RATE = 0.001
WEIGHT_DECAY = 0.05
BETA_FIRST = 0.9
BETA_SECOND = 0.999
adam_eps = 1e-08

F32 = jnp.float32
BF16 = jnp.bfloat16
NT = (((1,), (1,)), ((), ()))
TN = (((0,), (0,)), ((), ()))
NN = (((1,), (0,)), ((), ()))
BLOCK = 128
PART = 512

ROW_GAIN_ONE = 0
ROW_BIAS_ONE = ROW_GAIN_ONE + D_COLS
ROW_W_QKV = ROW_BIAS_ONE + D_COLS
ROW_B_QKV = ROW_W_QKV + D * QKV_COLS
ROW_W_OUT = ROW_B_QKV + QKV_COLS
ROW_B_OUT = ROW_W_OUT + D * D_COLS
ATTN_ROWS = ROW_B_OUT + D_COLS
ROW_POS = 0
ROW_GAIN_TWO = ROW_POS + POS * D_COLS
ROW_BIAS_TWO = ROW_GAIN_TWO + D_COLS
ROW_W_IN = ROW_BIAS_TWO + D_COLS
ROW_B_IN = ROW_W_IN + D * FF_COLS
ROW_W_BACK = ROW_B_IN + FF_COLS
ROW_B_BACK = ROW_W_BACK + FF * D_COLS
MLP_ROWS = ROW_B_BACK + D_COLS


def dot(a, b, dims=NN):
    return lax.dot_general(a, b, dims, preferred_element_type=F32)


def tile_row(entries, j):
    return pl.multiple_of(((j * entries) // TILE) * 8, 8)


def piece_rows(entries, count):
    most = max((entries * j) % TILE + entries for j in range(count))
    return -(-most // (16 * LANES)) * 16


def flat_rows(entries, count, rows):
    return max((entries * j) // TILE * 8 + rows for j in range(count))


def params(mebibytes):
    return pltpu.CompilerParams(vmem_limit_bytes=mebibytes * 1024 * 1024)


def cost(microseconds):
    return pl.CostEstimate(flops=int(microseconds * 1.15e9), bytes_accessed=1024, transcendentals=0)


def whole(shape):
    return pl.BlockSpec(shape, lambda *_: (0,) * len(shape))


SMEM_SPEC = pl.BlockSpec(memory_space=pltpu.SMEM)
VMEM_SPEC = pl.BlockSpec(memory_space=pltpu.VMEM)
HBM_SPEC = pl.BlockSpec(memory_space=pltpu.HBM)


def tall(vector, rows):
    entries = vector.shape[0]
    full = entries // TILE * TILE
    parts = [vector[pl.ds(0, full)].reshape(full // LANES, LANES)] if full else []
    if entries > full:
        rest = jnp.concatenate([vector[pl.ds(full, entries - full)], jnp.zeros((full + TILE - entries,), F32)])
        parts.append(rest.reshape(8, LANES))
    height = sum(part.shape[0] for part in parts)
    if height < rows:
        parts.append(jnp.zeros((rows - height, LANES), F32))
    return jnp.concatenate(parts, axis=0)


def put_flat(vector, value):
    entries = vector.shape[0]
    full = entries // TILE * TILE
    if full:
        vector[pl.ds(0, full)] = value[: full // LANES].reshape(full)
    if entries > full:
        vector[pl.ds(full, entries - full)] = value[full // LANES : full // LANES + 8].reshape(TILE)[: entries - full]


def align_kernel(heights, place, attn, mlp, out, attn_here, mlp_here, arrived):
    sources = ((attn, attn_here), (mlp, mlp_here))
    copies = [pltpu.make_async_copy(*source, arrived.at[n]) for n, source in enumerate(sources)]
    for copy in copies:
        copy.start()
    first = 0
    for n, height in enumerate(heights):
        copies[n].wait()
        lanes, rows = place[2 * n], place[2 * n + 1]
        value = tall(sources[n][1], height)
        turned = pltpu.roll(value, lanes, 1)
        below = pltpu.roll(turned, 1, 0)
        lane = lax.broadcasted_iota(jnp.int32, value.shape, 1)
        moved = jnp.where(lane >= lanes, turned, below)
        out[first : first + height, :] = pltpu.roll(moved, rows, 0).astype(BF16)
        first += height


def take_share(value, lanes, rows):
    height = value.shape[0]
    value = pltpu.roll(value, (height - rows) % height, 0)
    turned = pltpu.roll(value, (LANES - lanes) % LANES, 1)
    above = pltpu.roll(turned, height - 1, 0)
    lane = lax.broadcasted_iota(jnp.int32, value.shape, 1)
    return jnp.where(lane < LANES - lanes, turned, above)


def unpack(flat, arrays, entries, rows, me):
    alone = entries // TILE * 8
    edges = [(0, 8), (alone, rows)] if alone > 8 else [(0, rows)]
    for add in (False, True):
        for ref, numbers in arrays:
            for t, number in enumerate(numbers):
                start = tile_row(entries, number ^ me)
                for low, high in edges:
                    at = pl.ds(pl.multiple_of(start + low, 8), high - low)
                    if add:
                        flat[at, :] += ref[t * rows + low : t * rows + high, :].astype(F32)
                    else:
                        flat[at, :] = jnp.zeros((high - low, LANES), F32)
                if add and alone > 8:
                    at = pl.ds(pl.multiple_of(start + 8, 8), alone - 8)
                    flat[at, :] = ref[t * rows + 8 : t * rows + alone, :].astype(F32)


def read_matrix(flat, row, depth, cols, target):
    for c in range(cols):
        target[:, c * LANES : (c + 1) * LANES] = flat[pl.ds(row + c, depth, stride=cols), :].astype(BF16)


def read_row(flat, row, cols):
    return jnp.concatenate([flat[row + c : row + c + 1, :] for c in range(cols)], axis=1)


def write_row(flat, row, value):
    for c in range(value.shape[1] // LANES):
        flat[row + c : row + c + 1, :] = value[:, c * LANES : (c + 1) * LANES]


def norm_parts(value):
    average = jnp.mean(value, axis=-1, keepdims=True)
    centred = value - average
    variance = jnp.mean(centred * centred, axis=-1, keepdims=True)
    inverse = lax.rsqrt(variance + 1e-06)
    return centred * inverse, inverse


def norm_back(normed, inverse, gain, grad):
    scaled = grad * gain
    first = jnp.mean(scaled, axis=-1, keepdims=True)
    second = jnp.mean(scaled * normed, axis=-1, keepdims=True)
    return (scaled - first - normed * second) * inverse


def fold_rows(value):
    return jnp.sum(value.reshape(-1, 8, value.shape[-1]), axis=0)


def call(kernel, name, operands, outs, scratch, mebibytes, microseconds):
    return pl.pallas_call(
        kernel,
        in_specs=[SMEM_SPEC if a.dtype == jnp.int32 and a.ndim == 1 else VMEM_SPEC for a in operands],
        out_specs=[VMEM_SPEC] * len(outs),
        out_shape=[jax.ShapeDtypeStruct(shape, kind) for shape, kind in outs],
        scratch_shapes=scratch,
        compiler_params=params(mebibytes),
        cost_estimate=cost(microseconds),
        name=name,
    )(*operands)


def project_kernel(entries, attn_plan, pos_plan, attn_rows, mlp_rows, me, pos_names, onehot, tokens, *refs):
    attn_arrays = [(refs[i], plan) for i, plan in enumerate(attn_plan)]
    refs = refs[len(attn_plan) :]
    embedded, normed_out, qkv, w_qkv, w_out, vectors = refs[:6]
    flat, pos_flat, pos_table = refs[6:]
    slots, rows = tokens.shape[0], embedded.shape[0]

    pos_flat[...] = jnp.zeros_like(pos_flat)
    for n, (array, first) in enumerate(pos_plan):
        name = pos_names[n]

        @pl.when(name >= 0)
        def _():
            at = pl.ds(tile_row(entries[1], name), mlp_rows)
            pos_flat[at, :] += attn_arrays[array][0][first : first + mlp_rows, :].astype(F32)

    pos_table[...] = jnp.zeros_like(pos_table)
    most = POS // 16 * 16
    for c in range(D_COLS):
        column = pos_flat[pl.ds(ROW_POS + c, most, stride=D_COLS), :]
        pos_table[0:most, c * LANES : (c + 1) * LANES] = column.astype(BF16)
    last = [read_row(pos_flat, ROW_POS + r * D_COLS, D_COLS) for r in range(most, POS)]
    last = jnp.concatenate(last + [jnp.zeros((16 - len(last), D), F32)], axis=0)
    pos_table[most : most + 16, :] = last.astype(BF16)

    unpack(flat, attn_arrays, entries[0], attn_rows, me[0])
    read_matrix(flat, ROW_W_QKV, D, QKV_COLS, w_qkv)
    read_matrix(flat, ROW_W_OUT, D, D_COLS, w_out)
    gain = read_row(flat, ROW_GAIN_ONE, D_COLS)
    bias = read_row(flat, ROW_BIAS_ONE, D_COLS)
    b_qkv = read_row(flat, ROW_B_QKV, QKV_COLS)
    vectors[...] = jnp.zeros_like(vectors)
    vectors[0:1, :] = gain
    vectors[1:2, :] = read_row(flat, ROW_B_OUT, D_COLS)

    embedded[0:slots, :] = tokens[...].astype(F32)
    embedded[slots:rows, :] = jnp.zeros((rows - slots, D), F32)
    for c in range(QKV_COLS):
        qkv[c, rows : qkv.shape[1], :] = jnp.zeros((qkv.shape[1] - rows, LANES), F32)

    def project(i, _):
        at = pl.ds(pl.multiple_of(i * PART, PART), PART)
        value = embedded[at, :] + dot(onehot[at, :], pos_table[...])
        embedded[at, :] = value
        normed, _ = norm_parts(value)
        normed = (normed * gain + bias).astype(BF16)
        normed_out[at, :] = normed
        for k in range(3):
            cols = slice(k * D, (k + 1) * D)
            part = (dot(normed, w_qkv[:, cols]) + b_qkv[:, cols]).astype(BF16).astype(F32)
            if k == 0:
                part = part * DH ** (-0.5)
            for c in range(D_COLS):
                qkv[k * D_COLS + c, at, :] = part[:, c * LANES : (c + 1) * LANES]
        return 0

    lax.fori_loop(0, rows // PART, project, 0)


def project(entries, attn_arrays, pos_plan, pos_names, me, onehot, tokens, sizes):
    rows = onehot.shape[0]
    plan = [numbers for _, numbers in attn_arrays]
    operands = [me, pos_names, onehot, tokens] + [a for a, _ in attn_arrays]
    outs = [
        ((rows, D), F32),
        ((rows, D), BF16),
        ((QKV_COLS, sizes.reach, LANES), F32),
        ((D, 3 * D), BF16),
        ((D, D), BF16),
        ((8, D), F32),
    ]
    scratch = [
        pltpu.VMEM((sizes.attn_flat, LANES), F32),
        pltpu.VMEM((sizes.pos_flat, LANES), F32),
        pltpu.VMEM((256, D), BF16),
    ]
    kernel = functools.partial(
        project_kernel, entries, plan, pos_plan, sizes.attn_rows, sizes.mlp_rows
    )
    return call(kernel, "project", operands, outs, scratch, 17, 8)


def image_table(lengths, table):
    images = table.shape[1]
    longs = sum((lengths[i] == LONG).astype(jnp.int32) for i in range(images))
    start, long_seen, short_seen = jnp.int32(0), jnp.int32(0), longs
    for i in range(images):
        length = lengths[i]
        is_long = length == LONG
        place = jnp.where(is_long, long_seen, short_seen)
        table[0, place] = start
        table[1, place] = length
        start = start + length
        long_seen = long_seen + is_long.astype(jnp.int32)
        short_seen = short_seen + 1 - is_long.astype(jnp.int32)
    return start


def image_rows(slot):
    return -(-((LONG if slot < MOST_LONG else SHORT) + 7) // 32) * 32


class Unit:
    def __init__(self, slots, table):
        self.slots = slots
        self.height = image_rows(slots[0])
        self.lows = [table[0, slot] % 8 for slot in slots]
        self.at = [pl.ds(pl.multiple_of(table[0, s] - low, 8), self.height) for s, low in zip(slots, self.lows)]
        self.lengths = [table[1, slot] for slot in slots]
        self.valid = jnp.concatenate([inside(self.height, *span) for span in zip(self.lows, self.lengths)], axis=0)

    def load(self, ref, *index):
        return jnp.concatenate([ref[(*index, at, slice(None))] for at in self.at], axis=0)

    def store(self, ref, index, value):
        for n, at in enumerate(self.at):
            here = slice(n * self.height, (n + 1) * self.height)
            pltpu.store(ref.at[index, at, :], value[here], mask=self.valid[here])

    def mask(self):
        count, height = len(self.slots), self.height
        shape = (count * height, count * height)
        key = lax.broadcasted_iota(jnp.int32, shape, 1)
        row = lax.broadcasted_iota(jnp.int32, shape, 0)
        seen = None
        for n in range(count):
            low = n * height + self.lows[n]
            part = (key >= low) & (key < low + self.lengths[n])
            if count > 1:
                part = part & (row >= n * height) & (row < (n + 1) * height)
            seen = part if seen is None else seen | part
        bias = jnp.where(seen, 0.0, -1e30)
        return jnp.concatenate([bias, bias], axis=0)


def units(images, table):
    shorts = list(range(MOST_LONG, images))
    slots = [[slot] for slot in range(MOST_LONG)] + [shorts[i : i + 2] for i in range(0, len(shorts), 2)]
    return [Unit(these, table) for these in slots]


def both_heads(value):
    left = lax.broadcasted_iota(jnp.int32, value.shape, 1) < DH
    zero = jnp.zeros_like(value)
    return jnp.concatenate([jnp.where(left, value, zero), jnp.where(left, zero, value)], axis=0)


def one_of_heads(value):
    height = value.shape[0] // 2
    left = lax.broadcasted_iota(jnp.int32, (height, LANES), 1) < DH
    return jnp.where(left, value[:height], value[height:])


def inside(height, low, length):
    row = lax.broadcasted_iota(jnp.int32, (height, LANES), 0)
    return (row >= low) & (row < low + length)


def attend(queries, keys, values, bias):
    scores = dot(both_heads(queries), keys, NT) + bias
    peak = jnp.max(scores, axis=1, keepdims=True)
    probs = jnp.exp(scores - peak).astype(BF16)
    out = dot(probs, jnp.concatenate([values, jnp.ones_like(values)], axis=1))
    total = out[:, LANES:]
    return one_of_heads(out[:, :LANES] / total), peak + jnp.log(total)


def attend_kernel(slots, lengths, qkv, embedded, w_out, vectors, mixed, log_total, residual, table):
    images = lengths.shape[0]
    rows = residual.shape[0]
    live = image_table(lengths, table)
    ahead = slots // 8 * 8
    for pair in range(PAIRS):
        mixed[pair, ahead:, :] = jnp.zeros((mixed.shape[1] - ahead, LANES), F32)
    items = [(n, unit, pair) for n, unit in enumerate(units(images, table)) for pair in range(PAIRS)]
    biases, log_totals = {}, {}

    def first(n, unit, pair):
        if n not in biases:
            biases[n] = unit.mask()
            log_totals[n] = jnp.zeros((biases[n].shape[0], LANES), F32)
        queries, keys, values = (unit.load(qkv, k * PAIRS + pair).astype(BF16) for k in range(3))
        return values, dot(both_heads(queries), keys, NT)

    def second(n, unit, pair, values, scores):
        scores = scores + biases[n]
        peak = jnp.max(scores, axis=1, keepdims=True)
        return values, peak, jnp.exp(scores - peak).astype(BF16)

    def third(n, unit, pair, values, peak, probs):
        out = dot(probs, jnp.concatenate([values, jnp.ones_like(values)], axis=1))
        total = out[:, LANES:]
        lane = lax.broadcasted_iota(jnp.int32, total.shape, 1)
        log_totals[n] = jnp.where(lane == pair, peak + jnp.log(total), log_totals[n])
        unit.store(mixed, pair, one_of_heads(out[:, :LANES] / total).astype(BF16).astype(F32))
        if pair == PAIRS - 1:
            log_total[n, 0 : total.shape[0], :] = log_totals.pop(n)

    ones, twos = {}, {}
    for t in range(len(items) + 2):
        if t < len(items):
            ones[t] = first(*items[t])
        if 0 <= t - 1 < len(items):
            twos[t - 1] = second(*items[t - 1], *ones.pop(t - 1))
        if 0 <= t - 2 < len(items):
            third(*items[t - 2], *twos.pop(t - 2))

    low = live % 8
    base = pl.multiple_of(live - low, 8)
    length = slots - live
    most = -(-(slots - images * SHORT + (7 if (images * SHORT) % 8 else 0)) // BLOCK)
    for blocks in range(1, most + 1):

        @pl.when((low + length > (blocks - 1) * BLOCK) & (low + length <= blocks * BLOCK))
        def _():
            height = blocks * BLOCK
            key = lax.broadcasted_iota(jnp.int32, (2 * BLOCK, height), 1)
            bias = jnp.where((key >= low) & (key < low + length), 0.0, -1e30)
            for pair in range(PAIRS):
                keys = qkv[PAIRS + pair, pl.ds(base, height), :].astype(BF16)
                values = qkv[2 * PAIRS + pair, pl.ds(base, height), :].astype(BF16)
                for block in range(blocks):
                    at = pl.ds(pl.multiple_of(base + block * BLOCK, 8), BLOCK)
                    out, _ = attend(qkv[pair, at, :].astype(BF16), keys, values, bias)
                    valid = inside(BLOCK, low - block * BLOCK, length)
                    pltpu.store(mixed.at[pair, at, :], out.astype(BF16).astype(F32), mask=valid)

    def finish(i, _):
        at = pl.ds(pl.multiple_of(i * PART, PART), PART)
        together = jnp.concatenate([mixed[c, at, :] for c in range(D_COLS)], axis=1).astype(BF16)
        residual[at, :] = embedded[at, :] + dot(together, w_out[...]) + vectors[1:2, :]
        return 0

    lax.fori_loop(0, rows // PART, finish, 0)


def attend_all(slots, lengths, qkv, embedded, w_out, vectors):
    rows = embedded.shape[0]
    images = lengths.shape[0]
    units_count = MOST_LONG + -(-(images - MOST_LONG) // 2)
    height = 2 * max(image_rows(0), 2 * image_rows(MOST_LONG))
    outs = [((PAIRS,) + qkv.shape[1:], F32), ((units_count, height, LANES), F32), ((rows, D), F32)]
    scratch = [pltpu.SMEM((2, images), jnp.int32)]
    operands = [lengths, qkv, embedded, w_out, vectors]
    return call(functools.partial(attend_kernel, slots), "attend", operands, outs, scratch, 15, 10)


def gelu_parts(value):
    share = 0.5 + 0.5 * lax.erf(value * math.sqrt(0.5))
    bell = jnp.exp2((value * value) * (-0.5 * math.log2(math.e)))
    return value * share, share + value * (bell * (1.0 / math.sqrt(2.0 * math.pi)))


def with_ones(value_t):
    return jnp.concatenate([value_t, jnp.ones((16, value_t.shape[1]), BF16)], axis=0)


def pack(flat, entries, rows, me, targets):
    for ref, numbers in targets:
        for t, number in enumerate(numbers):
            start = tile_row(entries, number ^ me)
            ref[t * rows : (t + 1) * rows, :] = flat[pl.ds(start, rows), :].astype(BF16)


def mlp_kernel(entries, in_plan, out_plan, piece, mask, me, lengths, residual, cotangent, *refs):
    arrays = [(refs[i], plan) for i, plan in enumerate(in_plan)]
    refs = refs[len(in_plan) :]
    output, d_residual = refs[:2]
    targets = [(refs[2 + i], plan) for i, plan in enumerate(out_plan)]
    refs = refs[2 + len(out_plan) :]
    flat, w_in, w_back, normed_b, active_b, d_hidden_b, out_f32, sums, out_grad = refs
    slots, rows = cotangent.shape[0], residual.shape[0]
    live = sum(lengths[i] for i in range(lengths.shape[0]))
    row = lax.broadcasted_iota(jnp.int32, (slots, D), 0)
    out_grad[0:slots, :] = jnp.where(row < live, cotangent[...].astype(F32), 0.0).astype(BF16)
    out_grad[slots:rows, :] = jnp.zeros((rows - slots, D), BF16)

    unpack(flat, arrays, entries, piece, mask[0])
    read_matrix(flat, ROW_W_IN, D, FF_COLS, w_in)
    read_matrix(flat, ROW_W_BACK, FF, D_COLS, w_back)
    gain = read_row(flat, ROW_GAIN_TWO, D_COLS)
    bias = read_row(flat, ROW_BIAS_TWO, D_COLS)
    b_in = read_row(flat, ROW_B_IN, FF_COLS)
    b_back = read_row(flat, ROW_B_BACK, D_COLS)
    sums[...] = jnp.zeros_like(sums)

    def step(i, _):
        at = pl.ds(pl.multiple_of(i * PART, PART), PART)
        value = residual[at, :]
        grad_b = out_grad[at, :]
        normed, inverse = norm_parts(value)
        low = (normed * gain + bias).astype(BF16)
        normed_b[at, :] = low
        for c in range(FF // 256):
            cols = slice(c * 256, (c + 1) * 256)
            hidden = dot(low, w_in[:, cols]) + b_in[:, cols]
            d_active = dot(grad_b, w_back[cols, :], NT)
            active, slope = gelu_parts(hidden)
            d_hidden = (d_active * slope).astype(BF16)
            active_b[at, cols] = active.astype(BF16)
            d_hidden_b[at, cols] = d_hidden
        out_f32[at, :] = value + b_back + dot(active_b[at, :], w_back[...])
        d_normed = dot(d_hidden_b[at, :], w_in[...], NT)
        grad = grad_b.astype(F32)
        d_residual[at, :] = grad + norm_back(normed, inverse, gain, d_normed)
        sums[0] += fold_rows(d_normed * normed)
        sums[1] += fold_rows(d_normed)
        return 0

    lax.fori_loop(0, rows // PART, step, 0)
    output[...] = out_f32[0 : output.shape[0], :].astype(BF16)

    flat[0:ROW_GAIN_TWO, :] = jnp.zeros((ROW_GAIN_TWO, LANES), F32)
    flat[MLP_ROWS:, :] = jnp.zeros((flat.shape[0] - MLP_ROWS, LANES), F32)
    write_row(flat, ROW_GAIN_TWO, jnp.sum(sums[0], axis=0, keepdims=True))
    write_row(flat, ROW_BIAS_TWO, jnp.sum(sums[1], axis=0, keepdims=True))
    normed_t = with_ones(normed_b[...].T)
    column_sums = dot(jnp.ones((16, rows), BF16), out_grad[...])
    write_row(flat, ROW_B_BACK, column_sums[0:1])
    for c in range(0, FF_COLS, 2):
        part = dot(normed_t, d_hidden_b[:, c * LANES : (c + 2) * LANES])
        for k in range(2):
            flat[pl.ds(ROW_W_IN + c + k, D, stride=FF_COLS), :] = part[0:D, k * LANES : (k + 1) * LANES]
        write_row(flat, ROW_B_IN + c, part[D : D + 1])
    for r in range(0, FF, 256):
        part = dot(active_b[:, r : r + 256], out_grad[...], TN)
        for c in range(D_COLS):
            flat[pl.ds(ROW_W_BACK + r * D_COLS + c, 256, stride=D_COLS), :] = part[:, c * LANES : (c + 1) * LANES]
    pack(flat, entries, piece, me[0], targets)


def mlp_both(entries, arrays, mask, me, lengths, residual, cotangent, out_plan, sizes):
    rows = residual.shape[0]
    plan = [numbers for _, numbers in arrays]
    operands = [mask, me, lengths, residual, cotangent] + [a for a, _ in arrays]
    outs = [(cotangent.shape, BF16), ((rows, D), F32)]
    outs += [((len(n) * sizes.mlp_rows, LANES), BF16) for n in out_plan]
    scratch = [
        pltpu.VMEM((sizes.mlp_flat, LANES), F32),
        pltpu.VMEM((D, FF), BF16),
        pltpu.VMEM((FF, D), BF16),
        pltpu.VMEM((rows, D), BF16),
        pltpu.VMEM((rows, FF), BF16),
        pltpu.VMEM((rows, FF), BF16),
        pltpu.VMEM((rows, D), F32),
        pltpu.VMEM((2, 8, D), F32),
        pltpu.VMEM((rows, D), BF16),
    ]
    kernel = functools.partial(mlp_kernel, entries, plan, out_plan, sizes.mlp_rows)
    return call(kernel, "feed_forward", operands, outs, scratch, 28, 18)


def attend_back_kernel(lengths, qkv, mixed, log_total, w_out, d_residual, d_qkv, d_branch_b, d_mixed, table):
    images = lengths.shape[0]
    rows = d_residual.shape[0]
    image_table(lengths, table)
    ahead = images * SHORT // 8 * 8
    for c in range(QKV_COLS):
        d_qkv[c, ahead:, :] = jnp.zeros((d_qkv.shape[1] - ahead, LANES), F32)

    def enter(i, _):
        at = pl.ds(pl.multiple_of(i * PART, PART), PART)
        branch = d_residual[at, :].astype(BF16)
        d_branch_b[at, :] = branch
        value = dot(branch, w_out[...], NT).astype(BF16).astype(F32)
        for c in range(D_COLS):
            d_mixed[c, at, :] = value[:, c * LANES : (c + 1) * LANES]
        return 0

    lax.fori_loop(0, rows // PART, enter, 0)
    for c in range(D_COLS):
        d_mixed[c, rows : d_mixed.shape[1], :] = jnp.zeros((d_mixed.shape[1] - rows, LANES), F32)

    items = [(n, unit, pair) for n, unit in enumerate(units(images, table)) for pair in range(PAIRS)]
    biases = {}

    def first(n, unit, pair):
        if n not in biases:
            biases[n] = unit.mask()
        queries, keys, values = (unit.load(qkv, k * PAIRS + pair).astype(BF16) for k in range(3))
        queries = both_heads(queries)
        grad = jnp.where(unit.valid, unit.load(d_mixed, pair), 0.0)
        grads = both_heads(grad.astype(BF16))
        product = both_heads((grad * unit.load(mixed, pair)).astype(BF16))
        left = jnp.concatenate([grads, product], axis=1)
        right = jnp.concatenate([values, -jnp.ones_like(values)], axis=1)
        return queries, keys, grads, dot(queries, keys, NT), dot(left, right, NT)

    def second(n, unit, pair, queries, keys, grads, scores, d_probs):
        log_totals = log_total[n, 0 : scores.shape[0], :]
        probs = jnp.exp(scores + biases[n] - log_totals[:, pair : pair + 1])
        return queries, keys, grads, probs.astype(BF16), (probs * d_probs).astype(BF16)

    def third(n, unit, pair, queries, keys, grads, probs, d_scores):
        unit.store(d_qkv, pair, one_of_heads(dot(d_scores, keys)) * DH ** (-0.5))
        unit.store(d_qkv, PAIRS + pair, dot(d_scores, queries, TN))
        unit.store(d_qkv, 2 * PAIRS + pair, dot(probs, grads, TN))

    ones, twos = {}, {}
    for t in range(len(items) + 2):
        if t < len(items):
            ones[t] = first(*items[t])
        if 0 <= t - 1 < len(items):
            twos[t - 1] = second(*items[t - 1], *ones.pop(t - 1))
        if 0 <= t - 2 < len(items):
            third(*items[t - 2], *twos.pop(t - 2))


def attend_back(lengths, qkv, mixed, log_total, w_out, d_residual):
    rows = d_residual.shape[0]
    outs = [(qkv.shape, F32), ((rows, D), BF16)]
    scratch = [pltpu.VMEM(mixed.shape, F32), pltpu.SMEM((2, lengths.shape[0]), jnp.int32)]
    operands = [lengths, qkv, mixed, log_total, w_out, d_residual]
    return call(attend_back_kernel, "attend_back", operands, outs, scratch, 22, 12)


def project_back_kernel(entries, out_plan, piece, me, *refs):
    (onehot, embedded, normed_b, mixed, d_qkv, d_branch_b, w_qkv, vectors, d_residual) = refs[:9]
    in_grad, pos_out = refs[9:11]
    targets = [(refs[11 + i], plan) for i, plan in enumerate(out_plan)]
    flat, d_qkv_b, d_embedded_b, mixed_b, sums = refs[11 + len(out_plan) :]
    rows = embedded.shape[0]
    gain = vectors[0:1, :]
    sums[...] = jnp.zeros_like(sums)

    def leave(i, _):
        at = pl.ds(pl.multiple_of(i * PART, PART), PART)
        grads = jnp.concatenate([d_qkv[c, at, :] for c in range(QKV_COLS)], axis=1).astype(BF16)
        d_qkv_b[at, :] = grads
        mixed_b[at, :] = jnp.concatenate([mixed[c, at, :] for c in range(D_COLS)], axis=1).astype(BF16)
        d_normed = dot(grads, w_qkv[...], NT)
        normed, inverse = norm_parts(embedded[at, :])
        value = d_residual[at, :] + norm_back(normed, inverse, gain, d_normed)
        d_embedded_b[at, :] = value.astype(BF16)
        sums[0] += fold_rows(d_normed * normed)
        sums[1] += fold_rows(d_normed)
        return 0

    lax.fori_loop(0, rows // PART, leave, 0)
    in_grad[...] = d_embedded_b[0 : in_grad.shape[0], :]

    flat[ATTN_ROWS:, :] = jnp.zeros((flat.shape[0] - ATTN_ROWS, LANES), F32)
    write_row(flat, ROW_GAIN_ONE, jnp.sum(sums[0], axis=0, keepdims=True))
    write_row(flat, ROW_BIAS_ONE, jnp.sum(sums[1], axis=0, keepdims=True))
    normed_t = with_ones(normed_b[...].T)
    for k in range(3):
        cols = slice(k * D, (k + 1) * D)
        part = dot(normed_t, d_qkv_b[:, cols])
        write_row(flat, ROW_B_QKV + k * D_COLS, part[D : D + 1])
        for c in range(D_COLS):
            flat[pl.ds(ROW_W_QKV + k * D_COLS + c, D, stride=QKV_COLS), :] = part[0:D, c * LANES : (c + 1) * LANES]
    part = dot(with_ones(mixed_b[...].T), d_branch_b[...])
    write_row(flat, ROW_B_OUT, part[D : D + 1])
    for c in range(D_COLS):
        flat[pl.ds(ROW_W_OUT + c, D, stride=D_COLS), :] = part[0:D, c * LANES : (c + 1) * LANES]
    pack(flat, entries, piece, me[0], targets)

    pos_grad = dot(onehot[...], d_embedded_b[...], TN)
    flat[ROW_GAIN_TWO : pos_out.shape[0], :] = jnp.zeros((pos_out.shape[0] - ROW_GAIN_TWO, LANES), F32)
    for c in range(D_COLS):
        flat[pl.ds(ROW_POS + c, POS, stride=D_COLS), :] = pos_grad[0:POS, c * LANES : (c + 1) * LANES]
    pos_out[...] = flat[0 : pos_out.shape[0], :].astype(BF16)


def project_back(entries, me, kept, out_rows, out_plan, sizes):
    rows = kept[1].shape[0]
    outs = [((out_rows, D), BF16), ((sizes.pos_flat, LANES), BF16)]
    outs += [((len(n) * sizes.attn_rows, LANES), BF16) for n in out_plan]
    scratch = [
        pltpu.VMEM((max(sizes.attn_flat, sizes.pos_flat), LANES), F32),
        pltpu.VMEM((rows, 3 * D), BF16),
        pltpu.VMEM((rows, D), BF16),
        pltpu.VMEM((rows, D), BF16),
        pltpu.VMEM((2, 8, D), F32),
    ]
    kernel = functools.partial(project_back_kernel, entries, out_plan, sizes.attn_rows)
    return call(kernel, "project_back", [me, *kept], outs, scratch, 25, 10)


def adamw_step(gradient, weights, first, second):
    first_new = BETA_FIRST * first + (1.0 - BETA_FIRST) * gradient
    second_new = BETA_SECOND * second + (1.0 - BETA_SECOND) * gradient * gradient
    first_hat = first_new / (1.0 - BETA_FIRST**STEP)
    second_hat = second_new / (1.0 - BETA_SECOND**STEP)
    update = LEARNING_RATE * (first_hat / (jnp.sqrt(second_hat) + adam_eps) + WEIGHT_DECAY * weights)
    return (update, first_new, second_new)


def settle_kernel(scale, plans, count, place, *refs):
    terms, refs = refs[:count], refs[count:]
    state, outs = (refs[:3], refs[3:6]), (refs[6:10], refs[10:14])

    def added(plan):
        return sum(terms[n][first : first + rows, :].astype(F32) for n, first, rows in plan)

    other = added(plans[1]) + jnp.where(place[4] > 0, added(plans[2]), 0.0)
    for n, value in enumerate((added(plans[0]), other)):
        rows = value.shape[0]
        gradient = take_share(value, place[2 * n], place[2 * n + 1]) * scale
        weights, first, second = (tall(ref, rows) for ref in state[n])
        for ref, result in zip(outs[n], (gradient, *adamw_step(gradient, weights, first, second))):
            put_flat(ref, result)


def settle(scale, place, terms, plans, attn_state, mlp_state):
    operands = list(terms) + list(attn_state) + list(mlp_state)
    shapes = [attn_state[0].shape] * 4 + [mlp_state[0].shape] * 4
    return pl.pallas_call(
        functools.partial(settle_kernel, scale, plans, len(terms)),
        in_specs=[SMEM_SPEC] + [VMEM_SPEC] * len(operands),
        out_specs=[VMEM_SPEC] * len(shapes),
        out_shape=[jax.ShapeDtypeStruct(shape, F32) for shape in shapes],
        compiler_params=params(8),
        name="settle",
    )(place, *operands)


AXES = ("dp", "rep")
BIT_CORE, BIT_X, BIT_Y, BIT_Z = 1, 2, 4, 8
PLANE = (BIT_X, BIT_Y, BIT_X | BIT_Y)
DEVICES = 32


def swap(value, bits):
    return lax.ppermute(value, AXES, [(j, j ^ bits) for j in range(DEVICES)])


def together(*values):
    return lax.optimization_barrier(values)


def spread_z(piece):
    return [piece] + [swap(piece, k * BIT_Z) for k in (1, 2, 3)]


def spread_xy(value):
    return [value] + [swap(value, bits) for bits in PLANE]


def numbered(arrays):
    offsets = [core | bits for core in (0, BIT_CORE) for bits in (0, *PLANE)]
    return [(a, [offset | z * BIT_Z for z in range(4)]) for a, offset in zip(arrays, offsets)]


def sum_plan():
    return [[BIT_CORE | bits | z * BIT_Z for bits in (0, *PLANE) for z in range(4)]] + [
        [bits | z * BIT_Z for z in range(4)] for bits in (0, *PLANE)
    ]


def total(values):
    return sum(value.astype(F32) for value in values).astype(BF16)


def quarters(value):
    return [value[k * value.shape[0] // 4 : (k + 1) * value.shape[0] // 4] for k in range(4)]


def add_core(sent):
    came = quarters(swap(sent[0], BIT_CORE))
    return [total(both) for both in zip(sent[1:], came)]


def swap_xy(parts):
    return [parts[0]] + [swap(part, bits) for part, bits in zip(parts[1:], PLANE)]


def swap_z(parts):
    return [parts[0]] + [swap(parts[k], k * BIT_Z) for k in (1, 2, 3)]


class Sizes:
    def __init__(self, count, slots, attn_entries, mlp_entries):
        self.attn_rows = piece_rows(attn_entries, count)
        self.mlp_rows = piece_rows(mlp_entries, count)
        self.attn_flat = max(flat_rows(attn_entries, count, self.attn_rows), ATTN_ROWS)
        self.mlp_flat = max(flat_rows(mlp_entries, count, self.mlp_rows), MLP_ROWS)
        self.pos_count = -(-POS * D // mlp_entries)
        self.pos_flat = flat_rows(mlp_entries, self.pos_count, self.mlp_rows)
        self.pos_flat = max(-(-self.pos_flat // 16) * 16, -(-POS * D_COLS // 16) * 16)
        self.reach = -(-max(slots + BLOCK, slots - SHORT + image_rows(0)) // 8) * 8


class Layer:
    def __init__(self, entries, sizes, slots, tokens, cotangent, lengths, onehot):
        self.entries, self.sizes, self.slots = entries, sizes, slots
        self.tokens, self.cotangent, self.lengths, self.onehot = tokens, cotangent, lengths, onehot

    def project(self, mask, attn_arrays, pos_plan, pos_names):
        self.mask = mask
        (self.embedded, self.normed_b, self.qkv, self.w_qkv, self.w_out, self.vectors) = project(
            self.entries, attn_arrays, pos_plan, pos_names, mask, self.onehot, self.tokens, self.sizes
        )

    def attend(self):
        self.mixed, self.log_total, self.residual = attend_all(
            self.slots, self.lengths, self.qkv, self.embedded, self.w_out, self.vectors
        )

    def feed_forward(self, mlp_arrays, mask, plan):
        self.output, self.d_residual, *sent = mlp_both(
            self.entries[1], mlp_arrays, mask, self.mask, self.lengths, self.residual, self.cotangent, plan, self.sizes
        )
        return sent

    def attend_back(self):
        self.d_qkv, self.d_branch_b = attend_back(
            self.lengths, self.qkv, self.mixed, self.log_total, self.w_out, self.d_residual
        )

    def project_back(self, plan):
        kept = (self.onehot, self.embedded, self.normed_b, self.mixed, self.d_qkv, self.d_branch_b)
        kept += (self.w_qkv, self.vectors, self.d_residual)
        self.in_grad, pos_grad, *sent = project_back(self.entries[0], self.mask, kept, self.slots, plan, self.sizes)
        return pos_grad, sent


def step_by_axes(layer, me, piece):
    sizes, count = layer.sizes, lax.axis_size("dp") * lax.axis_size("rep")
    order = list(range(count))
    height = sizes.mlp_rows
    attn_all = lax.all_gather(piece[: sizes.attn_rows], AXES, axis=0, tiled=True)
    mlp_all = lax.all_gather(piece[sizes.attn_rows :], AXES, axis=0, tiled=True)
    pos_plan = [(1, j * height) for j in range(sizes.pos_count)]
    pos_names = jnp.arange(sizes.pos_count, dtype=jnp.int32)
    layer.project(jnp.zeros((1,), jnp.int32), [(attn_all, order), (mlp_all, [])], pos_plan, pos_names)
    layer.attend()
    mlp_sent = layer.feed_forward([(mlp_all, order)], layer.mask, [order])
    layer.attend_back()
    pos_grad, attn_sent = layer.project_back([order])
    mlp_terms = [lax.psum_scatter(mlp_sent[0], AXES, scatter_dimension=0, tiled=True)]
    attn_terms = [lax.psum_scatter(attn_sent[0], AXES, scatter_dimension=0, tiled=True)]
    pos_sum = jnp.pad(lax.psum(pos_grad, AXES), ((0, height), (0, 0)))
    first_row = jnp.minimum((me * layer.entries[1]) // TILE * 8, sizes.pos_flat)
    pos_terms = [lax.dynamic_slice_in_dim(pos_sum, first_row, height, axis=0)]
    plans = ([(0, 0, sizes.attn_rows)], [(1, 0, height)], [(2, 0, height)])
    return (layer.output, layer.in_grad), (attn_terms + mlp_terms + pos_terms, plans)


def step_by_hand(layer, me, piece):
    sizes = layer.sizes
    small, large = sizes.attn_rows, sizes.mlp_rows
    z, plane, core = me // BIT_Z, (me // BIT_X) % 4, me % 2
    plan = sum_plan()
    pieces = spread_z(piece)
    pieces, layer.onehot = together(pieces, layer.onehot)
    table = lax.select_n(z, *[p[small:] for p in pieces])
    attn = spread_xy(jnp.concatenate([p[:small] for p in pieces] + [table], axis=0))
    attn, pieces = together(attn, pieces)
    attn = attn + [swap(a, BIT_CORE) for a in attn]
    mlp = jnp.concatenate([p[small:] for p in pieces], axis=0)
    attn, mlp = together(attn, mlp)
    mlp_far = swap(mlp, BIT_CORE)
    mlp = spread_xy(mlp)
    at = 4 * small
    pos_plan = [(n, at) for n in range(8)]
    pos_names = jnp.stack([jnp.where(plane == n % 4, core if n < 4 else 1 - core, -1) for n in range(8)])
    layer.project(me.reshape(1), numbered(attn), pos_plan, pos_names)
    layer.attend()
    mlp, mlp_far, layer.residual = together(mlp, mlp_far, layer.residual)
    mlp = mlp + [mlp_far] + [swap(a, BIT_CORE) for a in mlp[1:]]
    mlp_sent = layer.feed_forward(numbered(mlp), layer.mask, plan)

    parts = add_core(mlp_sent)
    parts, layer.d_residual = together(parts, layer.d_residual)
    mlp_terms = swap_xy(parts)
    layer.attend_back()
    pos_grad, attn_sent = layer.project_back(plan)
    mlp_terms, pos_grad, attn_sent = together(mlp_terms, pos_grad, attn_sent)

    offset = layer.entries[1] // TILE * 8
    pos_parts = [pos_grad[:large], pos_grad[offset : offset + large]]
    pos_keep = jnp.where(core == 0, pos_parts[0], pos_parts[1])
    pos_send = jnp.where(core == 0, pos_parts[1], pos_parts[0])
    parts, pos = add_core(attn_sent), total([pos_keep, swap(pos_send, BIT_CORE)])
    sent = [jnp.concatenate([part, pos], axis=0) for part in parts]
    sent, mlp_terms = together(sent, mlp_terms)
    came = swap_xy(sent)
    mlp_came = swap_z(quarters(total(mlp_terms)))
    came = together(came)[0]
    whole_sum = total(came)
    pos = whole_sum[at:]
    sent = [jnp.concatenate([part, pos], axis=0) for part in quarters(whole_sum[:at])]
    came = swap_z(together(sent)[0])
    plans = (
        [(n, 0, small) for n in range(4)],
        [(n, 0, large) for n in range(4, 8)],
        [(n, small, large) for n in range(4)],
    )
    return (layer.output, layer.in_grad), (came + mlp_came, plans)


def body(
    by_hand,
    tokens,
    cotangent,
    lengths,
    pos_map,
    attn_params,
    attn_first,
    attn_second,
    mlp_params,
    mlp_first,
    mlp_second,
):
    slots = tokens.shape[0]
    rows = -(-slots // PART) * PART
    count = lax.axis_size("dp") * lax.axis_size("rep")
    entries = (attn_params.shape[0], mlp_params.shape[0])
    sizes = Sizes(count, slots, *entries)
    me = lax.axis_index("dp") * lax.axis_size("rep") + lax.axis_index("rep")
    me = me.astype(jnp.int32)

    starts = [(me * n) % TILE for n in entries]
    place = jnp.stack(
        [starts[0] % LANES, starts[0] // LANES, starts[1] % LANES, starts[1] // LANES, (me < 2).astype(jnp.int32)]
    )
    heights = (sizes.attn_rows, sizes.mlp_rows)
    piece = pl.pallas_call(
        functools.partial(align_kernel, heights),
        in_specs=[SMEM_SPEC, HBM_SPEC, HBM_SPEC],
        out_specs=VMEM_SPEC,
        out_shape=jax.ShapeDtypeStruct((sum(heights), LANES), BF16),
        scratch_shapes=[
            pltpu.VMEM(attn_params.shape, F32),
            pltpu.VMEM(mlp_params.shape, F32),
            pltpu.SemaphoreType.DMA((2,)),
        ],
        compiler_params=params(8),
        name="align",
    )(place, attn_params, mlp_params)

    pos_full = jnp.pad(pos_map, (0, rows - slots), constant_values=255)
    onehot = (pos_full[:, None] == jnp.arange(256, dtype=jnp.int32)[None, :]).astype(BF16)
    layer = Layer(entries, sizes, slots, tokens, cotangent, lengths, onehot)
    if by_hand:
        outputs, terms = step_by_hand(layer, me, piece)
    else:
        outputs, terms = step_by_axes(layer, me, piece)
        place = place.at[4].set(1)
    scale = 1.0 / math.sqrt(slots * count)
    attn_state, mlp_state = (attn_params, attn_first, attn_second), (mlp_params, mlp_first, mlp_second)
    updated = settle(scale, place, *terms, attn_state, mlp_state)
    return (*outputs, *updated)


def solution(mesh):
    split = P(AXES)
    split_rows = P(AXES, None)
    by_hand = mesh.shape["dp"] == 8 and mesh.shape["rep"] == 4
    return jax.shard_map(
        functools.partial(body, by_hand),
        mesh=mesh,
        in_specs=(split_rows, split_rows) + (split,) * 8,
        out_specs=(split_rows, split_rows) + (split,) * 8,
        check_vma=False,
    )
```

```python
import functools
import math

import jax
import jax.numpy as jnp
from jax import lax
from jax.experimental import pallas as pl
from jax.experimental.pallas import tpu as pltpu
from jax.sharding import PartitionSpec as P

D = 384
H = 6
DH = 64
FF = 1536
POS = 145
SHORT = 50
LONG = 145
MOST_LONG = 4
STEP = 10
LANES = 128
TILE = 8 * LANES
PAIRS = H // 2
QKV_COLS = 3 * D // LANES
D_COLS = D // LANES
FF_COLS = FF // LANES

LEARNING_RATE = 0.001
WEIGHT_DECAY = 0.05
BETA_FIRST = 0.9
BETA_SECOND = 0.999
adam_eps = 1e-08

F32 = jnp.float32
BF16 = jnp.bfloat16
NT = (((1,), (1,)), ((), ()))
TN = (((0,), (0,)), ((), ()))
NN = (((1,), (0,)), ((), ()))
BLOCK = 128
PART = 512

ROW_GAIN_ONE = 0
ROW_BIAS_ONE = ROW_GAIN_ONE + D_COLS
ROW_W_QKV = ROW_BIAS_ONE + D_COLS
ROW_B_QKV = ROW_W_QKV + D * QKV_COLS
ROW_W_OUT = ROW_B_QKV + QKV_COLS
ROW_B_OUT = ROW_W_OUT + D * D_COLS
ATTN_ROWS = ROW_B_OUT + D_COLS
ROW_POS = 0
ROW_GAIN_TWO = ROW_POS + POS * D_COLS
ROW_BIAS_TWO = ROW_GAIN_TWO + D_COLS
ROW_W_IN = ROW_BIAS_TWO + D_COLS
ROW_B_IN = ROW_W_IN + D * FF_COLS
ROW_W_BACK = ROW_B_IN + FF_COLS
ROW_B_BACK = ROW_W_BACK + FF * D_COLS
MLP_ROWS = ROW_B_BACK + D_COLS


def dot(a, b, dims=NN):
    return lax.dot_general(a, b, dims, preferred_element_type=F32)


def tile_row(entries, j):
    return pl.multiple_of(((j * entries) // TILE) * 8, 8)


def piece_rows(entries, count):
    most = max((entries * j) % TILE + entries for j in range(count))
    return -(-most // (16 * LANES)) * 16


def flat_rows(entries, count, rows):
    return max((entries * j) // TILE * 8 + rows for j in range(count))


def in_hbm(value):
    return pltpu.with_memory_space_constraint(value, pltpu.HBM)


def params(mebibytes):
    return pltpu.CompilerParams(vmem_limit_bytes=mebibytes * 1024 * 1024)


def cost(microseconds):
    return pl.CostEstimate(flops=int(microseconds * 1.15e9), bytes_accessed=1024, transcendentals=0)


def whole(shape):
    return pl.BlockSpec(shape, lambda *_: (0,) * len(shape))


SMEM_SPEC = pl.BlockSpec(memory_space=pltpu.SMEM)
VMEM_SPEC = pl.BlockSpec(memory_space=pltpu.VMEM)
HBM_SPEC = pl.BlockSpec(memory_space=pltpu.HBM)


def tall(vector, rows):
    entries = vector.shape[0]
    full = entries // TILE * TILE
    parts = [vector[pl.ds(0, full)].reshape(full // LANES, LANES)] if full else []
    if entries > full:
        rest = jnp.concatenate([vector[pl.ds(full, entries - full)], jnp.zeros((full + TILE - entries,), F32)])
        parts.append(rest.reshape(8, LANES))
    height = sum(part.shape[0] for part in parts)
    if height < rows:
        parts.append(jnp.zeros((rows - height, LANES), F32))
    return jnp.concatenate(parts, axis=0)


def put_flat(vector, value):
    entries = vector.shape[0]
    full = entries // TILE * TILE
    if full:
        vector[pl.ds(0, full)] = value[: full // LANES].reshape(full)
    if entries > full:
        vector[pl.ds(full, entries - full)] = value[full // LANES : full // LANES + 8].reshape(TILE)[: entries - full]


def align_kernel(heights, place, attn, mlp, out, attn_here, mlp_here, arrived):
    sources = ((attn, attn_here), (mlp, mlp_here))
    copies = [pltpu.make_async_copy(*source, arrived.at[n]) for n, source in enumerate(sources)]
    for copy in copies:
        copy.start()
    first = 0
    for n, height in enumerate(heights):
        copies[n].wait()
        lanes, rows = place[2 * n], place[2 * n + 1]
        value = tall(sources[n][1], height)
        turned = pltpu.roll(value, lanes, 1)
        below = pltpu.roll(turned, 1, 0)
        lane = lax.broadcasted_iota(jnp.int32, value.shape, 1)
        moved = jnp.where(lane >= lanes, turned, below)
        out[first : first + height, :] = pltpu.roll(moved, rows, 0).astype(BF16)
        first += height


def take_share(value, lanes, rows):
    height = value.shape[0]
    value = pltpu.roll(value, (height - rows) % height, 0)
    turned = pltpu.roll(value, (LANES - lanes) % LANES, 1)
    above = pltpu.roll(turned, height - 1, 0)
    lane = lax.broadcasted_iota(jnp.int32, value.shape, 1)
    return jnp.where(lane < LANES - lanes, turned, above)


def unpack(flat, arrays, entries, rows, me):
    alone = entries // TILE * 8
    edges = [(0, 8), (alone, rows)] if alone > 8 else [(0, rows)]
    for add in (False, True):
        for ref, (numbers, first) in arrays:
            for t, number in enumerate(numbers):
                start, piece = tile_row(entries, number ^ me), first + t * rows
                for low, high in edges:
                    at = pl.ds(pl.multiple_of(start + low, 8), high - low)
                    if add:
                        flat[at, :] += ref[piece + low : piece + high, :].astype(F32)
                    else:
                        flat[at, :] = jnp.zeros((high - low, LANES), F32)
                if add and alone > 8:
                    at = pl.ds(pl.multiple_of(start + 8, 8), alone - 8)
                    flat[at, :] = ref[piece + 8 : piece + alone, :].astype(F32)


def read_matrix(flat, row, depth, cols, target):
    for c in range(cols):
        target[:, c * LANES : (c + 1) * LANES] = flat[pl.ds(row + c, depth, stride=cols), :].astype(BF16)


def read_row(flat, row, cols):
    return jnp.concatenate([flat[row + c : row + c + 1, :] for c in range(cols)], axis=1)


def write_row(flat, row, value):
    for c in range(value.shape[1] // LANES):
        flat[row + c : row + c + 1, :] = value[:, c * LANES : (c + 1) * LANES]


def norm_parts(value):
    average = jnp.mean(value, axis=-1, keepdims=True)
    centred = value - average
    variance = jnp.mean(centred * centred, axis=-1, keepdims=True)
    inverse = lax.rsqrt(variance + 1e-06)
    return centred * inverse, inverse


def norm_back(normed, inverse, gain, grad):
    scaled = grad * gain
    first = jnp.mean(scaled, axis=-1, keepdims=True)
    second = jnp.mean(scaled * normed, axis=-1, keepdims=True)
    return (scaled - first - normed * second) * inverse


def fold_rows(value):
    return jnp.sum(value.reshape(-1, 8, value.shape[-1]), axis=0)


def call(kernel, name, operands, outs, scratch, mebibytes, microseconds):
    return pl.pallas_call(
        kernel,
        in_specs=[SMEM_SPEC if a.dtype == jnp.int32 and a.ndim == 1 else VMEM_SPEC for a in operands],
        out_specs=[VMEM_SPEC] * len(outs),
        out_shape=[jax.ShapeDtypeStruct(shape, kind) for shape, kind in outs],
        scratch_shapes=scratch,
        compiler_params=params(mebibytes),
        cost_estimate=cost(microseconds),
        name=name,
    )(*operands)


def project_kernel(entries, attn_plan, pos_plan, attn_rows, mlp_rows, me, pos_names, onehot, tokens, *refs):
    attn_arrays = [(refs[i], plan) for i, plan in enumerate(attn_plan)]
    refs = refs[len(attn_plan) :]
    embedded, normed_out, qkv, w_qkv, w_out, vectors, pieces_out = refs[:7]
    flat, pos_flat, pos_table = refs[7:]
    slots, rows = tokens.shape[0], embedded.shape[0]

    pos_flat[...] = jnp.zeros_like(pos_flat)
    for n, (array, first) in enumerate(pos_plan):
        pieces_out[n * mlp_rows : (n + 1) * mlp_rows, :] = attn_arrays[array][0][first : first + mlp_rows, :]
        name = pos_names[n]

        @pl.when(name >= 0)
        def _():
            at = pl.ds(tile_row(entries[1], name), mlp_rows)
            pos_flat[at, :] += attn_arrays[array][0][first : first + mlp_rows, :].astype(F32)

    pos_table[...] = jnp.zeros_like(pos_table)
    most = POS // 16 * 16
    for c in range(D_COLS):
        column = pos_flat[pl.ds(ROW_POS + c, most, stride=D_COLS), :]
        pos_table[0:most, c * LANES : (c + 1) * LANES] = column.astype(BF16)
    last = [read_row(pos_flat, ROW_POS + r * D_COLS, D_COLS) for r in range(most, POS)]
    last = jnp.concatenate(last + [jnp.zeros((16 - len(last), D), F32)], axis=0)
    pos_table[most : most + 16, :] = last.astype(BF16)

    unpack(flat, attn_arrays, entries[0], attn_rows, me[0])
    read_matrix(flat, ROW_W_QKV, D, QKV_COLS, w_qkv)
    read_matrix(flat, ROW_W_OUT, D, D_COLS, w_out)
    gain = read_row(flat, ROW_GAIN_ONE, D_COLS)
    bias = read_row(flat, ROW_BIAS_ONE, D_COLS)
    b_qkv = read_row(flat, ROW_B_QKV, QKV_COLS)
    vectors[...] = jnp.zeros_like(vectors)
    vectors[0:1, :] = gain
    vectors[1:2, :] = read_row(flat, ROW_B_OUT, D_COLS)

    embedded[0:slots, :] = tokens[...].astype(F32)
    embedded[slots:rows, :] = jnp.zeros((rows - slots, D), F32)
    for c in range(QKV_COLS):
        qkv[c, rows : qkv.shape[1], :] = jnp.zeros((qkv.shape[1] - rows, LANES), F32)

    def project(i, _):
        at = pl.ds(pl.multiple_of(i * PART, PART), PART)
        value = embedded[at, :] + dot(onehot[at, :], pos_table[...])
        embedded[at, :] = value
        normed, _ = norm_parts(value)
        normed = (normed * gain + bias).astype(BF16)
        normed_out[at, :] = normed
        for k in range(3):
            cols = slice(k * D, (k + 1) * D)
            part = (dot(normed, w_qkv[:, cols]) + b_qkv[:, cols]).astype(BF16).astype(F32)
            if k == 0:
                part = part * DH ** (-0.5)
            for c in range(D_COLS):
                qkv[k * D_COLS + c, at, :] = part[:, c * LANES : (c + 1) * LANES]
        return 0

    lax.fori_loop(0, rows // PART, project, 0)


def project(entries, attn_arrays, pos_plan, pos_names, me, onehot, tokens, sizes):
    rows = onehot.shape[0]
    plan = [numbers for _, numbers in attn_arrays]
    operands = [me, pos_names, onehot, tokens] + [a for a, _ in attn_arrays]
    outs = [
        ((rows, D), F32),
        ((rows, D), BF16),
        ((QKV_COLS, sizes.reach, LANES), F32),
        ((D, 3 * D), BF16),
        ((D, D), BF16),
        ((8, D), F32),
        ((len(pos_plan) * sizes.mlp_rows, LANES), BF16),
    ]
    scratch = [
        pltpu.VMEM((sizes.attn_flat, LANES), F32),
        pltpu.VMEM((sizes.pos_flat, LANES), F32),
        pltpu.VMEM((256, D), BF16),
    ]
    kernel = functools.partial(
        project_kernel, entries, plan, pos_plan, sizes.attn_rows, sizes.mlp_rows
    )
    return call(kernel, "project", operands, outs, scratch, 17, 8)


def image_table(lengths, table):
    images = table.shape[1]
    longs = sum((lengths[i] == LONG).astype(jnp.int32) for i in range(images))
    start, long_seen, short_seen = jnp.int32(0), jnp.int32(0), longs
    for i in range(images):
        length = lengths[i]
        is_long = length == LONG
        place = jnp.where(is_long, long_seen, short_seen)
        table[0, place] = start
        table[1, place] = length
        start = start + length
        long_seen = long_seen + is_long.astype(jnp.int32)
        short_seen = short_seen + 1 - is_long.astype(jnp.int32)
    return start


def image_rows(slot):
    return -(-((LONG if slot < MOST_LONG else SHORT) + 7) // 32) * 32


class Unit:
    def __init__(self, slots, table):
        self.slots = slots
        self.height = image_rows(slots[0])
        self.lows = [table[0, slot] % 8 for slot in slots]
        self.at = [pl.ds(pl.multiple_of(table[0, s] - low, 8), self.height) for s, low in zip(slots, self.lows)]
        self.lengths = [table[1, slot] for slot in slots]
        self.valid = jnp.concatenate([inside(self.height, *span) for span in zip(self.lows, self.lengths)], axis=0)

    def load(self, ref, *index):
        return jnp.concatenate([ref[(*index, at, slice(None))] for at in self.at], axis=0)

    def store(self, ref, index, value):
        for n, at in enumerate(self.at):
            here = slice(n * self.height, (n + 1) * self.height)
            pltpu.store(ref.at[index, at, :], value[here], mask=self.valid[here])

    def mask(self):
        count, height = len(self.slots), self.height
        shape = (count * height, count * height)
        key = lax.broadcasted_iota(jnp.int32, shape, 1)
        row = lax.broadcasted_iota(jnp.int32, shape, 0)
        seen = None
        for n in range(count):
            low = n * height + self.lows[n]
            part = (key >= low) & (key < low + self.lengths[n])
            if count > 1:
                part = part & (row >= n * height) & (row < (n + 1) * height)
            seen = part if seen is None else seen | part
        bias = jnp.where(seen, 0.0, -1e30)
        return jnp.concatenate([bias, bias], axis=0)


def units(images, table):
    shorts = list(range(MOST_LONG, images))
    slots = [[slot] for slot in range(MOST_LONG)] + [shorts[i : i + 2] for i in range(0, len(shorts), 2)]
    return [Unit(these, table) for these in slots]


def both_heads(value):
    left = lax.broadcasted_iota(jnp.int32, value.shape, 1) < DH
    zero = jnp.zeros_like(value)
    return jnp.concatenate([jnp.where(left, value, zero), jnp.where(left, zero, value)], axis=0)


def one_of_heads(value):
    height = value.shape[0] // 2
    left = lax.broadcasted_iota(jnp.int32, (height, LANES), 1) < DH
    return jnp.where(left, value[:height], value[height:])


def inside(height, low, length):
    row = lax.broadcasted_iota(jnp.int32, (height, LANES), 0)
    return (row >= low) & (row < low + length)


def attend(queries, keys, values, bias):
    scores = dot(both_heads(queries), keys, NT) + bias
    peak = jnp.max(scores, axis=1, keepdims=True)
    probs = jnp.exp(scores - peak).astype(BF16)
    out = dot(probs, jnp.concatenate([values, jnp.ones_like(values)], axis=1))
    total = out[:, LANES:]
    return one_of_heads(out[:, :LANES] / total), peak + jnp.log(total)


def attend_kernel(slots, lengths, qkv, embedded, w_out, vectors, mixed, log_total, residual, table):
    images = lengths.shape[0]
    rows = residual.shape[0]
    live = image_table(lengths, table)
    ahead = slots // 8 * 8
    for pair in range(PAIRS):
        mixed[pair, ahead:, :] = jnp.zeros((mixed.shape[1] - ahead, LANES), F32)
    items = [(n, unit, pair) for n, unit in enumerate(units(images, table)) for pair in range(PAIRS)]
    biases, log_totals = {}, {}

    def first(n, unit, pair):
        if n not in biases:
            biases[n] = unit.mask()
            log_totals[n] = jnp.zeros((biases[n].shape[0], LANES), F32)
        queries, keys, values = (unit.load(qkv, k * PAIRS + pair).astype(BF16) for k in range(3))
        return values, dot(both_heads(queries), keys, NT)

    def second(n, unit, pair, values, scores):
        scores = scores + biases[n]
        peak = jnp.max(scores, axis=1, keepdims=True)
        return values, peak, jnp.exp(scores - peak).astype(BF16)

    def third(n, unit, pair, values, peak, probs):
        out = dot(probs, jnp.concatenate([values, jnp.ones_like(values)], axis=1))
        total = out[:, LANES:]
        lane = lax.broadcasted_iota(jnp.int32, total.shape, 1)
        log_totals[n] = jnp.where(lane == pair, peak + jnp.log(total), log_totals[n])
        unit.store(mixed, pair, one_of_heads(out[:, :LANES] / total).astype(BF16).astype(F32))
        if pair == PAIRS - 1:
            log_total[n, 0 : total.shape[0], :] = log_totals.pop(n)

    ones, twos = {}, {}
    for t in range(len(items) + 2):
        if t < len(items):
            ones[t] = first(*items[t])
        if 0 <= t - 1 < len(items):
            twos[t - 1] = second(*items[t - 1], *ones.pop(t - 1))
        if 0 <= t - 2 < len(items):
            third(*items[t - 2], *twos.pop(t - 2))

    low = live % 8
    base = pl.multiple_of(live - low, 8)
    length = slots - live
    most = -(-(slots - images * SHORT + (7 if (images * SHORT) % 8 else 0)) // BLOCK)
    for blocks in range(1, most + 1):

        @pl.when((low + length > (blocks - 1) * BLOCK) & (low + length <= blocks * BLOCK))
        def _():
            height = blocks * BLOCK
            key = lax.broadcasted_iota(jnp.int32, (2 * BLOCK, height), 1)
            bias = jnp.where((key >= low) & (key < low + length), 0.0, -1e30)
            for pair in range(PAIRS):
                keys = qkv[PAIRS + pair, pl.ds(base, height), :].astype(BF16)
                values = qkv[2 * PAIRS + pair, pl.ds(base, height), :].astype(BF16)
                for block in range(blocks):
                    at = pl.ds(pl.multiple_of(base + block * BLOCK, 8), BLOCK)
                    out, _ = attend(qkv[pair, at, :].astype(BF16), keys, values, bias)
                    valid = inside(BLOCK, low - block * BLOCK, length)
                    pltpu.store(mixed.at[pair, at, :], out.astype(BF16).astype(F32), mask=valid)

    def finish(i, _):
        at = pl.ds(pl.multiple_of(i * PART, PART), PART)
        together = jnp.concatenate([mixed[c, at, :] for c in range(D_COLS)], axis=1).astype(BF16)
        residual[at, :] = embedded[at, :] + dot(together, w_out[...]) + vectors[1:2, :]
        return 0

    lax.fori_loop(0, rows // PART, finish, 0)


def attend_all(slots, lengths, qkv, embedded, w_out, vectors):
    rows = embedded.shape[0]
    images = lengths.shape[0]
    units_count = MOST_LONG + -(-(images - MOST_LONG) // 2)
    height = 2 * max(image_rows(0), 2 * image_rows(MOST_LONG))
    outs = [((PAIRS,) + qkv.shape[1:], F32), ((units_count, height, LANES), F32), ((rows, D), F32)]
    scratch = [pltpu.SMEM((2, images), jnp.int32)]
    operands = [lengths, qkv, embedded, w_out, vectors]
    return call(functools.partial(attend_kernel, slots), "attend", operands, outs, scratch, 15, 10)


def gelu_parts(value):
    share = 0.5 + 0.5 * lax.erf(value * math.sqrt(0.5))
    bell = jnp.exp2((value * value) * (-0.5 * math.log2(math.e)))
    return value * share, share + value * (bell * (1.0 / math.sqrt(2.0 * math.pi)))


def with_ones(value_t):
    return jnp.concatenate([value_t, jnp.ones((16, value_t.shape[1]), BF16)], axis=0)


def pack(flat, entries, rows, me, targets):
    for ref, numbers in targets:
        for t, number in enumerate(numbers):
            start = tile_row(entries, number ^ me)
            ref[t * rows : (t + 1) * rows, :] = flat[pl.ds(start, rows), :].astype(BF16)


def mlp_kernel(entries, in_plan, out_plan, piece, mask, me, lengths, residual, cotangent, *refs):
    arrays = [(refs[i], plan) for i, plan in enumerate(in_plan)]
    refs = refs[len(in_plan) :]
    output, d_residual = refs[:2]
    targets = [(refs[2 + i], plan) for i, plan in enumerate(out_plan)]
    refs = refs[2 + len(out_plan) :]
    flat, w_in, w_back, normed_b, active_b, d_hidden_b, out_f32, sums, out_grad = refs
    slots, rows = cotangent.shape[0], residual.shape[0]
    live = sum(lengths[i] for i in range(lengths.shape[0]))
    row = lax.broadcasted_iota(jnp.int32, (slots, D), 0)
    out_grad[0:slots, :] = jnp.where(row < live, cotangent[...].astype(F32), 0.0).astype(BF16)
    out_grad[slots:rows, :] = jnp.zeros((rows - slots, D), BF16)

    unpack(flat, arrays, entries, piece, mask[0])
    read_matrix(flat, ROW_W_IN, D, FF_COLS, w_in)
    read_matrix(flat, ROW_W_BACK, FF, D_COLS, w_back)
    gain = read_row(flat, ROW_GAIN_TWO, D_COLS)
    bias = read_row(flat, ROW_BIAS_TWO, D_COLS)
    b_in = read_row(flat, ROW_B_IN, FF_COLS)
    b_back = read_row(flat, ROW_B_BACK, D_COLS)
    sums[...] = jnp.zeros_like(sums)

    def step(i, _):
        at = pl.ds(pl.multiple_of(i * PART, PART), PART)
        value = residual[at, :]
        grad_b = out_grad[at, :]
        normed, inverse = norm_parts(value)
        low = (normed * gain + bias).astype(BF16)
        normed_b[at, :] = low
        for c in range(FF // 256):
            cols = slice(c * 256, (c + 1) * 256)
            hidden = dot(low, w_in[:, cols]) + b_in[:, cols]
            d_active = dot(grad_b, w_back[cols, :], NT)
            active, slope = gelu_parts(hidden)
            d_hidden = (d_active * slope).astype(BF16)
            active_b[at, cols] = active.astype(BF16)
            d_hidden_b[at, cols] = d_hidden
        out_f32[at, :] = value + b_back + dot(active_b[at, :], w_back[...])
        d_normed = dot(d_hidden_b[at, :], w_in[...], NT)
        grad = grad_b.astype(F32)
        d_residual[at, :] = grad + norm_back(normed, inverse, gain, d_normed)
        sums[0] += fold_rows(d_normed * normed)
        sums[1] += fold_rows(d_normed)
        return 0

    lax.fori_loop(0, rows // PART, step, 0)
    output[...] = out_f32[0 : output.shape[0], :].astype(BF16)

    flat[0:ROW_GAIN_TWO, :] = jnp.zeros((ROW_GAIN_TWO, LANES), F32)
    flat[MLP_ROWS:, :] = jnp.zeros((flat.shape[0] - MLP_ROWS, LANES), F32)
    write_row(flat, ROW_GAIN_TWO, jnp.sum(sums[0], axis=0, keepdims=True))
    write_row(flat, ROW_BIAS_TWO, jnp.sum(sums[1], axis=0, keepdims=True))
    normed_t = with_ones(normed_b[...].T)
    column_sums = dot(jnp.ones((16, rows), BF16), out_grad[...])
    write_row(flat, ROW_B_BACK, column_sums[0:1])
    for c in range(0, FF_COLS, 2):
        part = dot(normed_t, d_hidden_b[:, c * LANES : (c + 2) * LANES])
        for k in range(2):
            flat[pl.ds(ROW_W_IN + c + k, D, stride=FF_COLS), :] = part[0:D, k * LANES : (k + 1) * LANES]
        write_row(flat, ROW_B_IN + c, part[D : D + 1])
    for r in range(0, FF, 256):
        part = dot(active_b[:, r : r + 256], out_grad[...], TN)
        for c in range(D_COLS):
            flat[pl.ds(ROW_W_BACK + r * D_COLS + c, 256, stride=D_COLS), :] = part[:, c * LANES : (c + 1) * LANES]
    pack(flat, entries, piece, me[0], targets)


def mlp_both(entries, arrays, mask, me, lengths, residual, cotangent, out_plan, sizes):
    rows = residual.shape[0]
    plan = [numbers for _, numbers in arrays]
    operands = [mask, me, lengths, residual, cotangent] + [a for a, _ in arrays]
    outs = [(cotangent.shape, BF16), ((rows, D), F32)]
    outs += [((len(n) * sizes.mlp_rows, LANES), BF16) for n in out_plan]
    scratch = [
        pltpu.VMEM((sizes.mlp_flat, LANES), F32),
        pltpu.VMEM((D, FF), BF16),
        pltpu.VMEM((FF, D), BF16),
        pltpu.VMEM((rows, D), BF16),
        pltpu.VMEM((rows, FF), BF16),
        pltpu.VMEM((rows, FF), BF16),
        pltpu.VMEM((rows, D), F32),
        pltpu.VMEM((2, 8, D), F32),
        pltpu.VMEM((rows, D), BF16),
    ]
    kernel = functools.partial(mlp_kernel, entries, plan, out_plan, sizes.mlp_rows)
    return call(kernel, "feed_forward", operands, outs, scratch, 28, 18)


def attend_back_kernel(lengths, qkv, mixed, log_total, w_out, d_residual, d_qkv, d_branch_b, d_mixed, table):
    images = lengths.shape[0]
    rows = d_residual.shape[0]
    image_table(lengths, table)
    ahead = images * SHORT // 8 * 8
    for c in range(QKV_COLS):
        d_qkv[c, ahead:, :] = jnp.zeros((d_qkv.shape[1] - ahead, LANES), F32)

    def enter(i, _):
        at = pl.ds(pl.multiple_of(i * PART, PART), PART)
        branch = d_residual[at, :].astype(BF16)
        d_branch_b[at, :] = branch
        value = dot(branch, w_out[...], NT).astype(BF16).astype(F32)
        for c in range(D_COLS):
            d_mixed[c, at, :] = value[:, c * LANES : (c + 1) * LANES]
        return 0

    lax.fori_loop(0, rows // PART, enter, 0)
    for c in range(D_COLS):
        d_mixed[c, rows : d_mixed.shape[1], :] = jnp.zeros((d_mixed.shape[1] - rows, LANES), F32)

    items = [(n, unit, pair) for n, unit in enumerate(units(images, table)) for pair in range(PAIRS)]
    biases = {}

    def first(n, unit, pair):
        if n not in biases:
            biases[n] = unit.mask()
        queries, keys, values = (unit.load(qkv, k * PAIRS + pair).astype(BF16) for k in range(3))
        queries = both_heads(queries)
        grad = jnp.where(unit.valid, unit.load(d_mixed, pair), 0.0)
        grads = both_heads(grad.astype(BF16))
        product = both_heads((grad * unit.load(mixed, pair)).astype(BF16))
        left = jnp.concatenate([grads, product], axis=1)
        right = jnp.concatenate([values, -jnp.ones_like(values)], axis=1)
        return queries, keys, grads, dot(queries, keys, NT), dot(left, right, NT)

    def second(n, unit, pair, queries, keys, grads, scores, d_probs):
        log_totals = log_total[n, 0 : scores.shape[0], :]
        probs = jnp.exp(scores + biases[n] - log_totals[:, pair : pair + 1])
        return queries, keys, grads, probs.astype(BF16), (probs * d_probs).astype(BF16)

    def third(n, unit, pair, queries, keys, grads, probs, d_scores):
        unit.store(d_qkv, pair, one_of_heads(dot(d_scores, keys)) * DH ** (-0.5))
        unit.store(d_qkv, PAIRS + pair, dot(d_scores, queries, TN))
        unit.store(d_qkv, 2 * PAIRS + pair, dot(probs, grads, TN))

    ones, twos = {}, {}
    for t in range(len(items) + 2):
        if t < len(items):
            ones[t] = first(*items[t])
        if 0 <= t - 1 < len(items):
            twos[t - 1] = second(*items[t - 1], *ones.pop(t - 1))
        if 0 <= t - 2 < len(items):
            third(*items[t - 2], *twos.pop(t - 2))


def attend_back(lengths, qkv, mixed, log_total, w_out, d_residual):
    rows = d_residual.shape[0]
    outs = [(qkv.shape, F32), ((rows, D), BF16)]
    scratch = [pltpu.VMEM(mixed.shape, F32), pltpu.SMEM((2, lengths.shape[0]), jnp.int32)]
    operands = [lengths, qkv, mixed, log_total, w_out, d_residual]
    return call(attend_back_kernel, "attend_back", operands, outs, scratch, 22, 12)


def project_back_kernel(entries, out_plan, piece, me, *refs):
    (onehot, embedded, normed_b, mixed, d_qkv, d_branch_b, w_qkv, vectors, d_residual) = refs[:9]
    in_grad, pos_out = refs[9:11]
    targets = [(refs[11 + i], plan) for i, plan in enumerate(out_plan)]
    flat, d_qkv_b, d_embedded_b, mixed_b, sums = refs[11 + len(out_plan) :]
    rows = embedded.shape[0]
    gain = vectors[0:1, :]
    sums[...] = jnp.zeros_like(sums)

    def leave(i, _):
        at = pl.ds(pl.multiple_of(i * PART, PART), PART)
        grads = jnp.concatenate([d_qkv[c, at, :] for c in range(QKV_COLS)], axis=1).astype(BF16)
        d_qkv_b[at, :] = grads
        mixed_b[at, :] = jnp.concatenate([mixed[c, at, :] for c in range(D_COLS)], axis=1).astype(BF16)
        d_normed = dot(grads, w_qkv[...], NT)
        normed, inverse = norm_parts(embedded[at, :])
        value = d_residual[at, :] + norm_back(normed, inverse, gain, d_normed)
        d_embedded_b[at, :] = value.astype(BF16)
        sums[0] += fold_rows(d_normed * normed)
        sums[1] += fold_rows(d_normed)
        return 0

    lax.fori_loop(0, rows // PART, leave, 0)
    in_grad[...] = d_embedded_b[0 : in_grad.shape[0], :]

    flat[ATTN_ROWS:, :] = jnp.zeros((flat.shape[0] - ATTN_ROWS, LANES), F32)
    write_row(flat, ROW_GAIN_ONE, jnp.sum(sums[0], axis=0, keepdims=True))
    write_row(flat, ROW_BIAS_ONE, jnp.sum(sums[1], axis=0, keepdims=True))
    normed_t = with_ones(normed_b[...].T)
    for k in range(3):
        cols = slice(k * D, (k + 1) * D)
        part = dot(normed_t, d_qkv_b[:, cols])
        write_row(flat, ROW_B_QKV + k * D_COLS, part[D : D + 1])
        for c in range(D_COLS):
            flat[pl.ds(ROW_W_QKV + k * D_COLS + c, D, stride=QKV_COLS), :] = part[0:D, c * LANES : (c + 1) * LANES]
    part = dot(with_ones(mixed_b[...].T), d_branch_b[...])
    write_row(flat, ROW_B_OUT, part[D : D + 1])
    for c in range(D_COLS):
        flat[pl.ds(ROW_W_OUT + c, D, stride=D_COLS), :] = part[0:D, c * LANES : (c + 1) * LANES]
    pack(flat, entries, piece, me[0], targets)

    pos_grad = dot(onehot[...], d_embedded_b[...], TN)
    flat[ROW_GAIN_TWO : pos_out.shape[0], :] = jnp.zeros((pos_out.shape[0] - ROW_GAIN_TWO, LANES), F32)
    for c in range(D_COLS):
        flat[pl.ds(ROW_POS + c, POS, stride=D_COLS), :] = pos_grad[0:POS, c * LANES : (c + 1) * LANES]
    pos_out[...] = flat[0 : pos_out.shape[0], :].astype(BF16)


def project_back(entries, me, kept, out_rows, out_plan, sizes):
    rows = kept[1].shape[0]
    outs = [((out_rows, D), BF16), ((sizes.pos_flat, LANES), BF16)]
    outs += [((len(n) * sizes.attn_rows, LANES), BF16) for n in out_plan]
    scratch = [
        pltpu.VMEM((max(sizes.attn_flat, sizes.pos_flat), LANES), F32),
        pltpu.VMEM((rows, 3 * D), BF16),
        pltpu.VMEM((rows, D), BF16),
        pltpu.VMEM((rows, D), BF16),
        pltpu.VMEM((2, 8, D), F32),
    ]
    kernel = functools.partial(project_back_kernel, entries, out_plan, sizes.attn_rows)
    return call(kernel, "project_back", [me, *kept], outs, scratch, 25, 10)


def adamw_step(gradient, weights, first, second):
    first_new = BETA_FIRST * first + (1.0 - BETA_FIRST) * gradient
    second_new = BETA_SECOND * second + (1.0 - BETA_SECOND) * gradient * gradient
    first_hat = first_new / (1.0 - BETA_FIRST**STEP)
    second_hat = second_new / (1.0 - BETA_SECOND**STEP)
    update = LEARNING_RATE * (first_hat / (jnp.sqrt(second_hat) + adam_eps) + WEIGHT_DECAY * weights)
    return (update, first_new, second_new)


def settle_kernel(scale, plan, late_plan, count, place, *refs):
    terms, state, outs = refs[:count], refs[count : count + 3], refs[count + 3 :]
    value = sum(terms[n][first : first + rows, :].astype(F32) for n, first, rows in plan)
    rows = value.shape[0]
    if late_plan:
        late = jnp.concatenate([terms[n][first : first + r, :] for n, first, r in late_plan], axis=0)
        value = value + jnp.where(place[2] > 0, late.astype(F32), 0.0)
    gradient = take_share(value, place[0], place[1]) * scale
    weights, first, second = (tall(ref, rows) for ref in state)
    for ref, result in zip(outs, (gradient, *adamw_step(gradient, weights, first, second))):
        put_flat(ref, result)


def settle(scale, place, terms, plan, late_plan, state):
    operands = list(terms) + list(state)
    return pl.pallas_call(
        functools.partial(settle_kernel, scale, plan, late_plan, len(terms)),
        in_specs=[SMEM_SPEC] + [VMEM_SPEC] * len(operands),
        out_specs=[VMEM_SPEC] * 4,
        out_shape=[jax.ShapeDtypeStruct(state[0].shape, F32)] * 4,
        compiler_params=params(8),
        name="settle",
    )(place, *operands)


AXES = ("dp", "rep")
BIT_CORE, BIT_X, BIT_Y, BIT_Z = 1, 2, 4, 8
PLANE = (BIT_X, BIT_Y, BIT_X | BIT_Y)
DEVICES = 32


def swap(value, bits):
    return lax.ppermute(value, AXES, [(j, j ^ bits) for j in range(DEVICES)])


def together(*values):
    return lax.optimization_barrier(values)


def spread_z(piece):
    return [piece] + [swap(piece, k * BIT_Z) for k in (1, 2, 3)]


def spread_xy(value):
    return [value] + [swap(value, bits) for bits in PLANE]


def numbered(arrays, along_z, first=0):
    offsets = [core | bits for core in (0, BIT_CORE) for bits in (0, *PLANE)]
    return [(a, ([offset | z * BIT_Z for z in along_z], first)) for a, offset in zip(arrays, offsets)]


def sum_plan():
    return [[BIT_CORE | bits | z * BIT_Z for bits in (0, *PLANE) for z in range(4)]] + [
        [bits | z * BIT_Z for z in range(4)] for bits in (0, *PLANE)
    ]


def total(values):
    return sum(value.astype(F32) for value in values).astype(BF16)


def quarters(value):
    return [value[k * value.shape[0] // 4 : (k + 1) * value.shape[0] // 4] for k in range(4)]


def add_core(sent):
    came = quarters(swap(sent[0], BIT_CORE))
    return [total(both) for both in zip(sent[1:], came)]


def swap_xy(parts):
    return [parts[0]] + [swap(part, bits) for part, bits in zip(parts[1:], PLANE)]


def swap_z(parts):
    return [parts[0]] + [swap(parts[k], k * BIT_Z) for k in (1, 2, 3)]


class Sizes:
    def __init__(self, count, slots, attn_entries, mlp_entries):
        self.attn_rows = piece_rows(attn_entries, count)
        self.mlp_rows = piece_rows(mlp_entries, count)
        self.attn_flat = max(flat_rows(attn_entries, count, self.attn_rows), ATTN_ROWS)
        self.mlp_flat = max(flat_rows(mlp_entries, count, self.mlp_rows), MLP_ROWS)
        self.pos_count = -(-POS * D // mlp_entries)
        self.pos_flat = flat_rows(mlp_entries, self.pos_count, self.mlp_rows)
        self.pos_flat = max(-(-self.pos_flat // 16) * 16, -(-POS * D_COLS // 16) * 16)
        self.reach = -(-max(slots + BLOCK, slots - SHORT + image_rows(0)) // 8) * 8


class Layer:
    def __init__(self, entries, sizes, slots, tokens, cotangent, lengths, onehot):
        self.entries, self.sizes, self.slots = entries, sizes, slots
        self.tokens, self.cotangent, self.lengths, self.onehot = tokens, cotangent, lengths, onehot

    def project(self, mask, attn_arrays, pos_plan, pos_names):
        self.mask = mask
        (self.embedded, self.normed_b, self.qkv, self.w_qkv, self.w_out, self.vectors, self.passed) = project(
            self.entries, attn_arrays, pos_plan, pos_names, mask, self.onehot, self.tokens, self.sizes
        )

    def attend(self):
        self.mixed, self.log_total, self.residual = attend_all(
            self.slots, self.lengths, self.qkv, self.embedded, self.w_out, self.vectors
        )

    def feed_forward(self, mlp_arrays, mask, plan):
        self.output, self.d_residual, *sent = mlp_both(
            self.entries[1], mlp_arrays, mask, self.mask, self.lengths, self.residual, self.cotangent, plan, self.sizes
        )
        return sent

    def attend_back(self):
        self.d_qkv, self.d_branch_b = attend_back(
            self.lengths, self.qkv, self.mixed, self.log_total, self.w_out, self.d_residual
        )

    def project_back(self, plan):
        kept = (self.onehot, self.embedded, self.normed_b, self.mixed, self.d_qkv, self.d_branch_b)
        kept += (self.w_qkv, self.vectors, self.d_residual)
        self.in_grad, pos_grad, *sent = project_back(self.entries[0], self.mask, kept, self.slots, plan, self.sizes)
        return pos_grad, sent


def step_by_axes(layer, me, piece):
    sizes, count = layer.sizes, lax.axis_size("dp") * lax.axis_size("rep")
    order = list(range(count))
    height = sizes.mlp_rows
    attn_all = lax.all_gather(piece[: sizes.attn_rows], AXES, axis=0, tiled=True)
    mlp_all = lax.all_gather(piece[sizes.attn_rows :], AXES, axis=0, tiled=True)
    pos_plan = [(1, j * height) for j in range(sizes.pos_count)]
    pos_names = jnp.arange(sizes.pos_count, dtype=jnp.int32)
    layer.project(jnp.zeros((1,), jnp.int32), [(attn_all, (order, 0)), (mlp_all, ([], 0))], pos_plan, pos_names)
    layer.attend()
    mlp_sent = layer.feed_forward([(mlp_all, (order, 0))], layer.mask, [order])
    layer.attend_back()
    pos_grad, attn_sent = layer.project_back([order])
    mlp_terms = [lax.psum_scatter(mlp_sent[0], AXES, scatter_dimension=0, tiled=True)]
    attn_terms = [lax.psum_scatter(attn_sent[0], AXES, scatter_dimension=0, tiled=True)]
    pos_sum = jnp.pad(lax.psum(pos_grad, AXES), ((0, height), (0, 0)))
    first_row = jnp.minimum((me * layer.entries[1]) // TILE * 8, sizes.pos_flat)
    pos_terms = [lax.dynamic_slice_in_dim(pos_sum, first_row, height, axis=0)]
    plans = ([(0, 0, sizes.attn_rows)], [(0, 0, height)], [(1, 0, height)])
    return (layer.output, layer.in_grad), (attn_terms, mlp_terms + pos_terms, plans)


def step_by_hand(layer, me, piece):
    sizes = layer.sizes
    small, large = sizes.attn_rows, sizes.mlp_rows
    z, plane, core = me // BIT_Z, (me // BIT_X) % 4, me % 2
    plan = sum_plan()
    pieces = spread_z(piece)
    mask, near_mask = me.reshape(1), (me % BIT_Z).reshape(1)
    pos_names = jnp.stack([jnp.where(plane == n % 4, core if n < 4 else 1 - core, -1) for n in range(8)])
    pieces, layer.onehot, layer.places, mask, near_mask, pos_names = together(
        pieces, layer.onehot, layer.places, mask, near_mask, pos_names
    )
    table = lax.select_n(z, *[p[small:] for p in pieces])
    attn = spread_xy(jnp.concatenate([p[:small] for p in pieces] + [table], axis=0))
    attn, pieces = together(attn, pieces)
    attn = attn + [swap(a, BIT_CORE) for a in attn]
    mlp = [lax.select_n(z, *[pieces[k ^ here][small:] for here in range(4)]) for k in (1, 2, 3)]
    mlp = jnp.concatenate(mlp, axis=0)
    attn, mlp = together(attn, mlp)
    mlp_far = swap(mlp, BIT_CORE)
    mlp = spread_xy(mlp)
    at = 4 * small
    pos_plan = [(n, at) for n in range(8)]
    layer.project(mask, numbered(attn, range(4)), pos_plan, pos_names)
    layer.attend()
    mlp, mlp_far, layer.residual = together(mlp, mlp_far, layer.residual)
    mlp = mlp + [mlp_far] + [swap(a, BIT_CORE) for a in mlp[1:]]
    near = [offset | bits for offset in (0, BIT_CORE) for bits in (0, *PLANE)]
    arrays = numbered(mlp, (1, 2, 3)) + [(layer.passed, (near, 0))]
    mlp_sent = layer.feed_forward(arrays, near_mask, plan)

    parts = add_core(mlp_sent)
    parts, layer.d_residual = together(parts, layer.d_residual)
    mlp_terms = swap_xy(parts)
    layer.attend_back()
    pos_grad, attn_sent = layer.project_back(plan)
    mlp_terms, pos_grad, attn_sent = together(mlp_terms, pos_grad, attn_sent)

    offset = layer.entries[1] // TILE * 8
    pos_parts = [pos_grad[:large], pos_grad[offset : offset + large]]
    pos_keep = jnp.where(core == 0, pos_parts[0], pos_parts[1])
    pos_send = jnp.where(core == 0, pos_parts[1], pos_parts[0])
    parts, pos = add_core(attn_sent), total([pos_keep, swap(pos_send, BIT_CORE)])
    share = large // 4
    sent = [
        jnp.concatenate([part, lax.dynamic_slice_in_dim(pos, (plane ^ k) * share, share, axis=0)], axis=0)
        for k, part in enumerate(parts)
    ]
    sent, mlp_terms = together(sent, mlp_terms)
    came = swap_xy(sent)
    mlp_came = swap_z(quarters(total(mlp_terms)))
    came = together(came)[0]
    whole_sum = total(came)
    sent = [jnp.concatenate([part, whole_sum[at:]], axis=0) for part in quarters(whole_sum[:at])]
    came, mlp_came = together(swap_z(together(sent)[0]), mlp_came)
    pos = spread_xy(total([value[small:] for value in came]))
    plans = (
        [(n, 0, small) for n in range(4)],
        [(n, 0, large) for n in range(4)],
        [(n, 0, share) for n in range(4, 8)],
    )
    return (layer.output, layer.in_grad), (came, mlp_came + pos, plans)


def body(
    by_hand,
    tokens,
    cotangent,
    lengths,
    pos_map,
    attn_params,
    attn_first,
    attn_second,
    mlp_params,
    mlp_first,
    mlp_second,
):
    slots = tokens.shape[0]
    rows = -(-slots // PART) * PART
    count = lax.axis_size("dp") * lax.axis_size("rep")
    entries = (attn_params.shape[0], mlp_params.shape[0])
    sizes = Sizes(count, slots, *entries)
    me = lax.axis_index("dp") * lax.axis_size("rep") + lax.axis_index("rep")
    me = me.astype(jnp.int32)

    starts = [(me * n) % TILE for n in entries]
    place = jnp.stack(
        [starts[0] % LANES, starts[0] // LANES, starts[1] % LANES, starts[1] // LANES, (me < 2).astype(jnp.int32)]
    )
    heights = (sizes.attn_rows, sizes.mlp_rows)
    piece = pl.pallas_call(
        functools.partial(align_kernel, heights),
        in_specs=[SMEM_SPEC, HBM_SPEC, HBM_SPEC],
        out_specs=VMEM_SPEC,
        out_shape=jax.ShapeDtypeStruct((sum(heights), LANES), BF16),
        scratch_shapes=[
            pltpu.VMEM(attn_params.shape, F32),
            pltpu.VMEM(mlp_params.shape, F32),
            pltpu.SemaphoreType.DMA((2,)),
        ],
        compiler_params=params(8),
        name="align",
    )(place, in_hbm(attn_params), in_hbm(mlp_params))

    pos_full = jnp.pad(pos_map, (0, rows - slots), constant_values=255)
    onehot = (pos_full[:, None] == jnp.arange(256, dtype=jnp.int32)[None, :]).astype(BF16)
    layer = Layer(entries, sizes, slots, tokens, cotangent, lengths, onehot)
    layer.places = (place[:2], place[2:])
    if by_hand:
        outputs, terms = step_by_hand(layer, me, piece)
    else:
        outputs, terms = step_by_axes(layer, me, piece)
        layer.places = (place[:2], place[2:].at[2].set(1))
    scale = 1.0 / math.sqrt(slots * count)
    attn_state, mlp_state = (attn_params, attn_first, attn_second), (mlp_params, mlp_first, mlp_second)
    attn_terms, mlp_terms, plans = terms
    attn_new = settle(scale, layer.places[0], attn_terms, plans[0], (), attn_state)
    mlp_new = settle(scale, layer.places[1], mlp_terms, plans[1], plans[2], mlp_state)
    return (*outputs, *attn_new, *mlp_new)


def solution(mesh):
    split = P(AXES)
    split_rows = P(AXES, None)
    by_hand = mesh.shape["dp"] == 8 and mesh.shape["rep"] == 4
    return jax.shard_map(
        functools.partial(body, by_hand),
        mesh=mesh,
        in_specs=(split_rows, split_rows) + (split,) * 8,
        out_specs=(split_rows, split_rows) + (split,) * 8,
        check_vma=False,
    )
```

```python
import functools
import math

import jax
import jax.numpy as jnp
from jax import lax
from jax.experimental import pallas as pl
from jax.experimental.pallas import tpu as pltpu
from jax.sharding import PartitionSpec as P

D = 384
H = 6
DH = 64
FF = 1536
POS = 145
SHORT = 50
LONG = 145
MOST_LONG = 4
STEP = 10
LANES = 128
TILE = 8 * LANES
PAIRS = H // 2
QKV_COLS = 3 * D // LANES
D_COLS = D // LANES
FF_COLS = FF // LANES

LEARNING_RATE = 0.001
WEIGHT_DECAY = 0.05
BETA_FIRST = 0.9
BETA_SECOND = 0.999
adam_eps = 1e-08

F32 = jnp.float32
BF16 = jnp.bfloat16
NT = (((1,), (1,)), ((), ()))
TN = (((0,), (0,)), ((), ()))
NN = (((1,), (0,)), ((), ()))
BLOCK = 128
PART = 512

ROW_GAIN_ONE = 0
ROW_BIAS_ONE = ROW_GAIN_ONE + D_COLS
ROW_W_QKV = ROW_BIAS_ONE + D_COLS
ROW_B_QKV = ROW_W_QKV + D * QKV_COLS
ROW_W_OUT = ROW_B_QKV + QKV_COLS
ROW_B_OUT = ROW_W_OUT + D * D_COLS
ATTN_ROWS = ROW_B_OUT + D_COLS
ROW_POS = 0
ROW_GAIN_TWO = ROW_POS + POS * D_COLS
ROW_BIAS_TWO = ROW_GAIN_TWO + D_COLS
ROW_W_IN = ROW_BIAS_TWO + D_COLS
ROW_B_IN = ROW_W_IN + D * FF_COLS
ROW_W_BACK = ROW_B_IN + FF_COLS
ROW_B_BACK = ROW_W_BACK + FF * D_COLS
MLP_ROWS = ROW_B_BACK + D_COLS


def dot(a, b, dims=NN):
    return lax.dot_general(a, b, dims, preferred_element_type=F32)


def tile_row(entries, j):
    return pl.multiple_of(((j * entries) // TILE) * 8, 8)


def piece_rows(entries, count):
    most = max((entries * j) % TILE + entries for j in range(count))
    return -(-most // (16 * LANES)) * 16


def flat_rows(entries, count, rows):
    return max((entries * j) // TILE * 8 + rows for j in range(count))


def in_hbm(value):
    return pltpu.with_memory_space_constraint(value, pltpu.HBM)


def params(mebibytes):
    return pltpu.CompilerParams(vmem_limit_bytes=mebibytes * 1024 * 1024)


def cost(microseconds):
    return pl.CostEstimate(flops=int(microseconds * 1.15e9), bytes_accessed=1024, transcendentals=0)


def whole(shape):
    return pl.BlockSpec(shape, lambda *_: (0,) * len(shape))


SMEM_SPEC = pl.BlockSpec(memory_space=pltpu.SMEM)
VMEM_SPEC = pl.BlockSpec(memory_space=pltpu.VMEM)
HBM_SPEC = pl.BlockSpec(memory_space=pltpu.HBM)


def tall(vector, rows):
    entries = vector.shape[0]
    full = entries // TILE * TILE
    parts = [vector[pl.ds(0, full)].reshape(full // LANES, LANES)] if full else []
    if entries > full:
        rest = jnp.concatenate([vector[pl.ds(full, entries - full)], jnp.zeros((full + TILE - entries,), F32)])
        parts.append(rest.reshape(8, LANES))
    height = sum(part.shape[0] for part in parts)
    if height < rows:
        parts.append(jnp.zeros((rows - height, LANES), F32))
    return jnp.concatenate(parts, axis=0)


def put_flat(vector, value):
    entries = vector.shape[0]
    full = entries // TILE * TILE
    if full:
        vector[pl.ds(0, full)] = value[: full // LANES].reshape(full)
    if entries > full:
        vector[pl.ds(full, entries - full)] = value[full // LANES : full // LANES + 8].reshape(TILE)[: entries - full]


def align_kernel(heights, place, attn, mlp, out, attn_here, mlp_here, arrived):
    sources = ((attn, attn_here), (mlp, mlp_here))
    copies = [pltpu.make_async_copy(*source, arrived.at[n]) for n, source in enumerate(sources)]
    for copy in copies:
        copy.start()
    first = 0
    for n, height in enumerate(heights):
        copies[n].wait()
        lanes, rows = place[2 * n], place[2 * n + 1]
        value = tall(sources[n][1], height)
        turned = pltpu.roll(value, lanes, 1)
        below = pltpu.roll(turned, 1, 0)
        lane = lax.broadcasted_iota(jnp.int32, value.shape, 1)
        moved = jnp.where(lane >= lanes, turned, below)
        out[first : first + height, :] = pltpu.roll(moved, rows, 0).astype(BF16)
        first += height


def take_share(value, lanes, rows):
    height = value.shape[0]
    value = pltpu.roll(value, (height - rows) % height, 0)
    turned = pltpu.roll(value, (LANES - lanes) % LANES, 1)
    above = pltpu.roll(turned, height - 1, 0)
    lane = lax.broadcasted_iota(jnp.int32, value.shape, 1)
    return jnp.where(lane < LANES - lanes, turned, above)


def unpack(flat, arrays, entries, rows, me):
    alone = entries // TILE * 8
    edges = [(0, 8), (alone, rows)] if alone > 8 else [(0, rows)]
    for add in (False, True):
        for ref, (numbers, first) in arrays:
            for t, number in enumerate(numbers):
                start, piece = tile_row(entries, number ^ me), first + t * rows
                for low, high in edges:
                    at = pl.ds(pl.multiple_of(start + low, 8), high - low)
                    if add:
                        flat[at, :] += ref[piece + low : piece + high, :].astype(F32)
                    else:
                        flat[at, :] = jnp.zeros((high - low, LANES), F32)
                if add and alone > 8:
                    at = pl.ds(pl.multiple_of(start + 8, 8), alone - 8)
                    flat[at, :] = ref[piece + 8 : piece + alone, :].astype(F32)


def read_matrix(flat, row, depth, cols, target):
    for c in range(cols):
        target[:, c * LANES : (c + 1) * LANES] = flat[pl.ds(row + c, depth, stride=cols), :].astype(BF16)


def read_row(flat, row, cols):
    return jnp.concatenate([flat[row + c : row + c + 1, :] for c in range(cols)], axis=1)


def write_row(flat, row, value):
    for c in range(value.shape[1] // LANES):
        flat[row + c : row + c + 1, :] = value[:, c * LANES : (c + 1) * LANES]


def norm_parts(value):
    average = jnp.mean(value, axis=-1, keepdims=True)
    centred = value - average
    variance = jnp.mean(centred * centred, axis=-1, keepdims=True)
    inverse = lax.rsqrt(variance + 1e-06)
    return centred * inverse, inverse


def norm_back(normed, inverse, gain, grad):
    scaled = grad * gain
    first = jnp.mean(scaled, axis=-1, keepdims=True)
    second = jnp.mean(scaled * normed, axis=-1, keepdims=True)
    return (scaled - first - normed * second) * inverse


def fold_rows(value):
    return jnp.sum(value.reshape(-1, 8, value.shape[-1]), axis=0)


def call(kernel, name, operands, outs, scratch, mebibytes, microseconds):
    return pl.pallas_call(
        kernel,
        in_specs=[SMEM_SPEC if a.dtype == jnp.int32 and a.ndim == 1 else VMEM_SPEC for a in operands],
        out_specs=[VMEM_SPEC] * len(outs),
        out_shape=[jax.ShapeDtypeStruct(shape, kind) for shape, kind in outs],
        scratch_shapes=scratch,
        compiler_params=params(mebibytes),
        cost_estimate=cost(microseconds),
        name=name,
    )(*operands)


def project_kernel(entries, attn_plan, pos_plan, attn_rows, mlp_rows, me, pos_names, onehot, tokens, *refs):
    attn_arrays = [(refs[i], plan) for i, plan in enumerate(attn_plan)]
    refs = refs[len(attn_plan) :]
    embedded, normed_out, qkv, w_qkv, w_out, vectors, pieces_out = refs[:7]
    flat, pos_flat, pos_table = refs[7:]
    slots, rows = tokens.shape[0], embedded.shape[0]

    pos_flat[...] = jnp.zeros_like(pos_flat)
    for n, (array, first) in enumerate(pos_plan):
        pieces_out[n * mlp_rows : (n + 1) * mlp_rows, :] = attn_arrays[array][0][first : first + mlp_rows, :]
        name = pos_names[n]

        @pl.when(name >= 0)
        def _():
            at = pl.ds(tile_row(entries[1], name), mlp_rows)
            pos_flat[at, :] += attn_arrays[array][0][first : first + mlp_rows, :].astype(F32)

    pos_table[...] = jnp.zeros_like(pos_table)
    most = POS // 16 * 16
    for c in range(D_COLS):
        column = pos_flat[pl.ds(ROW_POS + c, most, stride=D_COLS), :]
        pos_table[0:most, c * LANES : (c + 1) * LANES] = column.astype(BF16)
    last = [read_row(pos_flat, ROW_POS + r * D_COLS, D_COLS) for r in range(most, POS)]
    last = jnp.concatenate(last + [jnp.zeros((16 - len(last), D), F32)], axis=0)
    pos_table[most : most + 16, :] = last.astype(BF16)

    unpack(flat, attn_arrays, entries[0], attn_rows, me[0])
    read_matrix(flat, ROW_W_QKV, D, QKV_COLS, w_qkv)
    read_matrix(flat, ROW_W_OUT, D, D_COLS, w_out)
    gain = read_row(flat, ROW_GAIN_ONE, D_COLS)
    bias = read_row(flat, ROW_BIAS_ONE, D_COLS)
    b_qkv = read_row(flat, ROW_B_QKV, QKV_COLS)
    vectors[...] = jnp.zeros_like(vectors)
    vectors[0:1, :] = gain
    vectors[1:2, :] = read_row(flat, ROW_B_OUT, D_COLS)

    embedded[0:slots, :] = tokens[...].astype(F32)
    embedded[slots:rows, :] = jnp.zeros((rows - slots, D), F32)
    for c in range(QKV_COLS):
        qkv[c, rows : qkv.shape[1], :] = jnp.zeros((qkv.shape[1] - rows, LANES), F32)

    def project(i, _):
        at = pl.ds(pl.multiple_of(i * PART, PART), PART)
        value = embedded[at, :] + dot(onehot[at, :], pos_table[...])
        embedded[at, :] = value
        normed, _ = norm_parts(value)
        normed = (normed * gain + bias).astype(BF16)
        normed_out[at, :] = normed
        for k in range(3):
            cols = slice(k * D, (k + 1) * D)
            part = (dot(normed, w_qkv[:, cols]) + b_qkv[:, cols]).astype(BF16).astype(F32)
            if k == 0:
                part = part * DH ** (-0.5)
            for c in range(D_COLS):
                qkv[k * D_COLS + c, at, :] = part[:, c * LANES : (c + 1) * LANES]
        return 0

    lax.fori_loop(0, rows // PART, project, 0)


def project(entries, attn_arrays, pos_plan, pos_names, me, onehot, tokens, sizes):
    rows = onehot.shape[0]
    plan = [numbers for _, numbers in attn_arrays]
    operands = [me, pos_names, onehot, tokens] + [a for a, _ in attn_arrays]
    outs = [
        ((rows, D), F32),
        ((rows, D), BF16),
        ((QKV_COLS, sizes.reach, LANES), F32),
        ((D, 3 * D), BF16),
        ((D, D), BF16),
        ((8, D), F32),
        ((len(pos_plan) * sizes.mlp_rows, LANES), BF16),
    ]
    scratch = [
        pltpu.VMEM((sizes.attn_flat, LANES), F32),
        pltpu.VMEM((sizes.pos_flat, LANES), F32),
        pltpu.VMEM((256, D), BF16),
    ]
    kernel = functools.partial(
        project_kernel, entries, plan, pos_plan, sizes.attn_rows, sizes.mlp_rows
    )
    return call(kernel, "project", operands, outs, scratch, 17, 8)


def image_table(lengths, table):
    images = table.shape[1]
    longs = sum((lengths[i] == LONG).astype(jnp.int32) for i in range(images))
    start, long_seen, short_seen = jnp.int32(0), jnp.int32(0), longs
    for i in range(images):
        length = lengths[i]
        is_long = length == LONG
        place = jnp.where(is_long, long_seen, short_seen)
        table[0, place] = start
        table[1, place] = length
        start = start + length
        long_seen = long_seen + is_long.astype(jnp.int32)
        short_seen = short_seen + 1 - is_long.astype(jnp.int32)
    return start


def image_rows(slot):
    return -(-((LONG if slot < MOST_LONG else SHORT) + 7) // 32) * 32


class Unit:
    def __init__(self, slots, table):
        self.slots = slots
        self.height = image_rows(slots[0])
        self.lows = [table[0, slot] % 8 for slot in slots]
        self.at = [pl.ds(pl.multiple_of(table[0, s] - low, 8), self.height) for s, low in zip(slots, self.lows)]
        self.lengths = [table[1, slot] for slot in slots]
        self.valid = jnp.concatenate([inside(self.height, *span) for span in zip(self.lows, self.lengths)], axis=0)

    def load(self, ref, *index):
        return jnp.concatenate([ref[(*index, at, slice(None))] for at in self.at], axis=0)

    def store(self, ref, index, value):
        for n, at in enumerate(self.at):
            here = slice(n * self.height, (n + 1) * self.height)
            pltpu.store(ref.at[index, at, :], value[here], mask=self.valid[here])

    def mask(self):
        count, height = len(self.slots), self.height
        shape = (count * height, count * height)
        key = lax.broadcasted_iota(jnp.int32, shape, 1)
        row = lax.broadcasted_iota(jnp.int32, shape, 0)
        seen = None
        for n in range(count):
            low = n * height + self.lows[n]
            part = (key >= low) & (key < low + self.lengths[n])
            if count > 1:
                part = part & (row >= n * height) & (row < (n + 1) * height)
            seen = part if seen is None else seen | part
        bias = jnp.where(seen, 0.0, -1e30)
        return jnp.concatenate([bias, bias], axis=0)


def units(images, table):
    shorts = list(range(MOST_LONG, images))
    slots = [[slot] for slot in range(MOST_LONG)] + [shorts[i : i + 2] for i in range(0, len(shorts), 2)]
    return [Unit(these, table) for these in slots]


def both_heads(value):
    left = lax.broadcasted_iota(jnp.int32, value.shape, 1) < DH
    zero = jnp.zeros_like(value)
    return jnp.concatenate([jnp.where(left, value, zero), jnp.where(left, zero, value)], axis=0)


def one_of_heads(value):
    height = value.shape[0] // 2
    left = lax.broadcasted_iota(jnp.int32, (height, LANES), 1) < DH
    return jnp.where(left, value[:height], value[height:])


def inside(height, low, length):
    row = lax.broadcasted_iota(jnp.int32, (height, LANES), 0)
    return (row >= low) & (row < low + length)


def attend(queries, keys, values, bias):
    scores = dot(both_heads(queries), keys, NT) + bias
    peak = jnp.max(scores, axis=1, keepdims=True)
    probs = jnp.exp(scores - peak).astype(BF16)
    out = dot(probs, jnp.concatenate([values, jnp.ones_like(values)], axis=1))
    total = out[:, LANES:]
    return one_of_heads(out[:, :LANES] / total), peak + jnp.log(total)


def attend_kernel(slots, lengths, qkv, embedded, w_out, vectors, mixed, log_total, residual, table):
    images = lengths.shape[0]
    rows = residual.shape[0]
    live = image_table(lengths, table)
    ahead = slots // 8 * 8
    for pair in range(PAIRS):
        mixed[pair, ahead:, :] = jnp.zeros((mixed.shape[1] - ahead, LANES), F32)
    items = [(n, unit, pair) for n, unit in enumerate(units(images, table)) for pair in range(PAIRS)]
    biases, log_totals = {}, {}

    def first(n, unit, pair):
        if n not in biases:
            biases[n] = unit.mask()
            log_totals[n] = jnp.zeros((biases[n].shape[0], LANES), F32)
        queries, keys, values = (unit.load(qkv, k * PAIRS + pair).astype(BF16) for k in range(3))
        return values, dot(both_heads(queries), keys, NT)

    def second(n, unit, pair, values, scores):
        scores = scores + biases[n]
        peak = jnp.max(scores, axis=1, keepdims=True)
        return values, peak, jnp.exp(scores - peak).astype(BF16)

    def third(n, unit, pair, values, peak, probs):
        out = dot(probs, jnp.concatenate([values, jnp.ones_like(values)], axis=1))
        total = out[:, LANES:]
        lane = lax.broadcasted_iota(jnp.int32, total.shape, 1)
        log_totals[n] = jnp.where(lane == pair, peak + jnp.log(total), log_totals[n])
        unit.store(mixed, pair, one_of_heads(out[:, :LANES] / total).astype(BF16).astype(F32))
        if pair == PAIRS - 1:
            log_total[n, 0 : total.shape[0], :] = log_totals.pop(n)

    ones, twos = {}, {}
    for t in range(len(items) + 2):
        if t < len(items):
            ones[t] = first(*items[t])
        if 0 <= t - 1 < len(items):
            twos[t - 1] = second(*items[t - 1], *ones.pop(t - 1))
        if 0 <= t - 2 < len(items):
            third(*items[t - 2], *twos.pop(t - 2))

    low = live % 8
    base = pl.multiple_of(live - low, 8)
    length = slots - live
    most = -(-(slots - images * SHORT + (7 if (images * SHORT) % 8 else 0)) // BLOCK)
    for blocks in range(1, most + 1):

        @pl.when((low + length > (blocks - 1) * BLOCK) & (low + length <= blocks * BLOCK))
        def _():
            height = blocks * BLOCK
            key = lax.broadcasted_iota(jnp.int32, (2 * BLOCK, height), 1)
            bias = jnp.where((key >= low) & (key < low + length), 0.0, -1e30)
            for pair in range(PAIRS):
                keys = qkv[PAIRS + pair, pl.ds(base, height), :].astype(BF16)
                values = qkv[2 * PAIRS + pair, pl.ds(base, height), :].astype(BF16)
                for block in range(blocks):
                    at = pl.ds(pl.multiple_of(base + block * BLOCK, 8), BLOCK)
                    out, _ = attend(qkv[pair, at, :].astype(BF16), keys, values, bias)
                    valid = inside(BLOCK, low - block * BLOCK, length)
                    pltpu.store(mixed.at[pair, at, :], out.astype(BF16).astype(F32), mask=valid)

    def finish(i, _):
        at = pl.ds(pl.multiple_of(i * PART, PART), PART)
        together = jnp.concatenate([mixed[c, at, :] for c in range(D_COLS)], axis=1).astype(BF16)
        residual[at, :] = embedded[at, :] + dot(together, w_out[...]) + vectors[1:2, :]
        return 0

    lax.fori_loop(0, rows // PART, finish, 0)


def attend_all(slots, lengths, qkv, embedded, w_out, vectors):
    rows = embedded.shape[0]
    images = lengths.shape[0]
    units_count = MOST_LONG + -(-(images - MOST_LONG) // 2)
    height = 2 * max(image_rows(0), 2 * image_rows(MOST_LONG))
    outs = [((PAIRS,) + qkv.shape[1:], F32), ((units_count, height, LANES), F32), ((rows, D), F32)]
    scratch = [pltpu.SMEM((2, images), jnp.int32)]
    operands = [lengths, qkv, embedded, w_out, vectors]
    return call(functools.partial(attend_kernel, slots), "attend", operands, outs, scratch, 15, 10)


def gelu_parts(value):
    share = 0.5 + 0.5 * lax.erf(value * math.sqrt(0.5))
    bell = jnp.exp2((value * value) * (-0.5 * math.log2(math.e)))
    return value * share, share + value * (bell * (1.0 / math.sqrt(2.0 * math.pi)))


def with_ones(value_t):
    return jnp.concatenate([value_t, jnp.ones((16, value_t.shape[1]), BF16)], axis=0)


def pack(flat, entries, rows, me, targets):
    for ref, numbers in targets:
        for t, number in enumerate(numbers):
            start = tile_row(entries, number ^ me)
            ref[t * rows : (t + 1) * rows, :] = flat[pl.ds(start, rows), :].astype(BF16)


def mlp_kernel(entries, in_plan, out_plan, piece, mask, me, lengths, residual, cotangent, *refs):
    arrays = [(refs[i], plan) for i, plan in enumerate(in_plan)]
    refs = refs[len(in_plan) :]
    output, d_residual = refs[:2]
    targets = [(refs[2 + i], plan) for i, plan in enumerate(out_plan)]
    refs = refs[2 + len(out_plan) :]
    flat, w_in, w_back, normed_b, active_b, d_hidden_b, out_f32, sums, out_grad = refs
    slots, rows = cotangent.shape[0], residual.shape[0]
    live = sum(lengths[i] for i in range(lengths.shape[0]))
    row = lax.broadcasted_iota(jnp.int32, (slots, D), 0)
    out_grad[0:slots, :] = jnp.where(row < live, cotangent[...].astype(F32), 0.0).astype(BF16)
    out_grad[slots:rows, :] = jnp.zeros((rows - slots, D), BF16)

    unpack(flat, arrays, entries, piece, mask[0])
    read_matrix(flat, ROW_W_IN, D, FF_COLS, w_in)
    read_matrix(flat, ROW_W_BACK, FF, D_COLS, w_back)
    gain = read_row(flat, ROW_GAIN_TWO, D_COLS)
    bias = read_row(flat, ROW_BIAS_TWO, D_COLS)
    b_in = read_row(flat, ROW_B_IN, FF_COLS)
    b_back = read_row(flat, ROW_B_BACK, D_COLS)
    sums[...] = jnp.zeros_like(sums)

    def step(i, _):
        at = pl.ds(pl.multiple_of(i * PART, PART), PART)
        value = residual[at, :]
        grad_b = out_grad[at, :]
        normed, inverse = norm_parts(value)
        low = (normed * gain + bias).astype(BF16)
        normed_b[at, :] = low
        for c in range(FF // 256):
            cols = slice(c * 256, (c + 1) * 256)
            hidden = dot(low, w_in[:, cols]) + b_in[:, cols]
            d_active = dot(grad_b, w_back[cols, :], NT)
            active, slope = gelu_parts(hidden)
            d_hidden = (d_active * slope).astype(BF16)
            active_b[at, cols] = active.astype(BF16)
            d_hidden_b[at, cols] = d_hidden
        out_f32[at, :] = value + b_back + dot(active_b[at, :], w_back[...])
        d_normed = dot(d_hidden_b[at, :], w_in[...], NT)
        grad = grad_b.astype(F32)
        d_residual[at, :] = grad + norm_back(normed, inverse, gain, d_normed)
        sums[0] += fold_rows(d_normed * normed)
        sums[1] += fold_rows(d_normed)
        return 0

    lax.fori_loop(0, rows // PART, step, 0)
    output[...] = out_f32[0 : output.shape[0], :].astype(BF16)

    flat[0:ROW_GAIN_TWO, :] = jnp.zeros((ROW_GAIN_TWO, LANES), F32)
    flat[MLP_ROWS:, :] = jnp.zeros((flat.shape[0] - MLP_ROWS, LANES), F32)
    write_row(flat, ROW_GAIN_TWO, jnp.sum(sums[0], axis=0, keepdims=True))
    write_row(flat, ROW_BIAS_TWO, jnp.sum(sums[1], axis=0, keepdims=True))
    normed_t = with_ones(normed_b[...].T)
    column_sums = dot(jnp.ones((16, rows), BF16), out_grad[...])
    write_row(flat, ROW_B_BACK, column_sums[0:1])
    for c in range(0, FF_COLS, 2):
        part = dot(normed_t, d_hidden_b[:, c * LANES : (c + 2) * LANES])
        for k in range(2):
            flat[pl.ds(ROW_W_IN + c + k, D, stride=FF_COLS), :] = part[0:D, k * LANES : (k + 1) * LANES]
        write_row(flat, ROW_B_IN + c, part[D : D + 1])
    for r in range(0, FF, 256):
        part = dot(active_b[:, r : r + 256], out_grad[...], TN)
        for c in range(D_COLS):
            flat[pl.ds(ROW_W_BACK + r * D_COLS + c, 256, stride=D_COLS), :] = part[:, c * LANES : (c + 1) * LANES]
    pack(flat, entries, piece, me[0], targets)


def mlp_both(entries, arrays, mask, me, lengths, residual, cotangent, out_plan, sizes):
    rows = residual.shape[0]
    plan = [numbers for _, numbers in arrays]
    operands = [mask, me, lengths, residual, cotangent] + [a for a, _ in arrays]
    outs = [(cotangent.shape, BF16), ((rows, D), F32)]
    outs += [((len(n) * sizes.mlp_rows, LANES), BF16) for n in out_plan]
    scratch = [
        pltpu.VMEM((sizes.mlp_flat, LANES), F32),
        pltpu.VMEM((D, FF), BF16),
        pltpu.VMEM((FF, D), BF16),
        pltpu.VMEM((rows, D), BF16),
        pltpu.VMEM((rows, FF), BF16),
        pltpu.VMEM((rows, FF), BF16),
        pltpu.VMEM((rows, D), F32),
        pltpu.VMEM((2, 8, D), F32),
        pltpu.VMEM((rows, D), BF16),
    ]
    kernel = functools.partial(mlp_kernel, entries, plan, out_plan, sizes.mlp_rows)
    return call(kernel, "feed_forward", operands, outs, scratch, 28, 18)


def attend_back_kernel(lengths, qkv, mixed, log_total, w_out, d_residual, d_qkv, d_branch_b, d_mixed, table):
    images = lengths.shape[0]
    rows = d_residual.shape[0]
    image_table(lengths, table)
    ahead = images * SHORT // 8 * 8
    for c in range(QKV_COLS):
        d_qkv[c, ahead:, :] = jnp.zeros((d_qkv.shape[1] - ahead, LANES), F32)

    def enter(i, _):
        at = pl.ds(pl.multiple_of(i * PART, PART), PART)
        branch = d_residual[at, :].astype(BF16)
        d_branch_b[at, :] = branch
        value = dot(branch, w_out[...], NT).astype(BF16).astype(F32)
        for c in range(D_COLS):
            d_mixed[c, at, :] = value[:, c * LANES : (c + 1) * LANES]
        return 0

    lax.fori_loop(0, rows // PART, enter, 0)
    for c in range(D_COLS):
        d_mixed[c, rows : d_mixed.shape[1], :] = jnp.zeros((d_mixed.shape[1] - rows, LANES), F32)

    items = [(n, unit, pair) for n, unit in enumerate(units(images, table)) for pair in range(PAIRS)]
    biases = {}

    def first(n, unit, pair):
        if n not in biases:
            biases[n] = unit.mask()
        queries, keys, values = (unit.load(qkv, k * PAIRS + pair).astype(BF16) for k in range(3))
        queries = both_heads(queries)
        grad = jnp.where(unit.valid, unit.load(d_mixed, pair), 0.0)
        grads = both_heads(grad.astype(BF16))
        product = both_heads((grad * unit.load(mixed, pair)).astype(BF16))
        left = jnp.concatenate([grads, product], axis=1)
        right = jnp.concatenate([values, -jnp.ones_like(values)], axis=1)
        return queries, keys, grads, dot(queries, keys, NT), dot(left, right, NT)

    def second(n, unit, pair, queries, keys, grads, scores, d_probs):
        log_totals = log_total[n, 0 : scores.shape[0], :]
        probs = jnp.exp(scores + biases[n] - log_totals[:, pair : pair + 1])
        return queries, keys, grads, probs.astype(BF16), (probs * d_probs).astype(BF16)

    def third(n, unit, pair, queries, keys, grads, probs, d_scores):
        unit.store(d_qkv, pair, one_of_heads(dot(d_scores, keys)) * DH ** (-0.5))
        unit.store(d_qkv, PAIRS + pair, dot(d_scores, queries, TN))
        unit.store(d_qkv, 2 * PAIRS + pair, dot(probs, grads, TN))

    ones, twos = {}, {}
    for t in range(len(items) + 2):
        if t < len(items):
            ones[t] = first(*items[t])
        if 0 <= t - 1 < len(items):
            twos[t - 1] = second(*items[t - 1], *ones.pop(t - 1))
        if 0 <= t - 2 < len(items):
            third(*items[t - 2], *twos.pop(t - 2))


def attend_back(lengths, qkv, mixed, log_total, w_out, d_residual):
    rows = d_residual.shape[0]
    outs = [(qkv.shape, F32), ((rows, D), BF16)]
    scratch = [pltpu.VMEM(mixed.shape, F32), pltpu.SMEM((2, lengths.shape[0]), jnp.int32)]
    operands = [lengths, qkv, mixed, log_total, w_out, d_residual]
    return call(attend_back_kernel, "attend_back", operands, outs, scratch, 22, 12)


def project_back_kernel(entries, out_plan, piece, mlp_rows, pos_count, me, pos_names, *refs):
    (onehot, embedded, normed_b, mixed, d_qkv, d_branch_b, w_qkv, vectors, d_residual) = refs[:9]
    in_grad, pos_out = refs[9], refs[10 : 10 + pos_count]
    refs = refs[10 + pos_count :]
    targets = [(refs[i], plan) for i, plan in enumerate(out_plan)]
    flat, d_qkv_b, d_embedded_b, mixed_b, sums = refs[len(out_plan) :]
    rows = embedded.shape[0]
    gain = vectors[0:1, :]
    sums[...] = jnp.zeros_like(sums)

    def leave(i, _):
        at = pl.ds(pl.multiple_of(i * PART, PART), PART)
        grads = jnp.concatenate([d_qkv[c, at, :] for c in range(QKV_COLS)], axis=1).astype(BF16)
        d_qkv_b[at, :] = grads
        mixed_b[at, :] = jnp.concatenate([mixed[c, at, :] for c in range(D_COLS)], axis=1).astype(BF16)
        d_normed = dot(grads, w_qkv[...], NT)
        normed, inverse = norm_parts(embedded[at, :])
        value = d_residual[at, :] + norm_back(normed, inverse, gain, d_normed)
        d_embedded_b[at, :] = value.astype(BF16)
        sums[0] += fold_rows(d_normed * normed)
        sums[1] += fold_rows(d_normed)
        return 0

    lax.fori_loop(0, rows // PART, leave, 0)
    in_grad[...] = d_embedded_b[0 : in_grad.shape[0], :]

    flat[ATTN_ROWS:, :] = jnp.zeros((flat.shape[0] - ATTN_ROWS, LANES), F32)
    write_row(flat, ROW_GAIN_ONE, jnp.sum(sums[0], axis=0, keepdims=True))
    write_row(flat, ROW_BIAS_ONE, jnp.sum(sums[1], axis=0, keepdims=True))
    normed_t = with_ones(normed_b[...].T)
    for k in range(3):
        cols = slice(k * D, (k + 1) * D)
        part = dot(normed_t, d_qkv_b[:, cols])
        write_row(flat, ROW_B_QKV + k * D_COLS, part[D : D + 1])
        for c in range(D_COLS):
            flat[pl.ds(ROW_W_QKV + k * D_COLS + c, D, stride=QKV_COLS), :] = part[0:D, c * LANES : (c + 1) * LANES]
    part = dot(with_ones(mixed_b[...].T), d_branch_b[...])
    write_row(flat, ROW_B_OUT, part[D : D + 1])
    for c in range(D_COLS):
        flat[pl.ds(ROW_W_OUT + c, D, stride=D_COLS), :] = part[0:D, c * LANES : (c + 1) * LANES]
    pack(flat, entries[0], piece, me[0], targets)

    pos_grad = dot(onehot[...], d_embedded_b[...], TN)
    flat[ROW_GAIN_TWO:, :] = jnp.zeros((flat.shape[0] - ROW_GAIN_TWO, LANES), F32)
    for c in range(D_COLS):
        flat[pl.ds(ROW_POS + c, POS, stride=D_COLS), :] = pos_grad[0:POS, c * LANES : (c + 1) * LANES]
    for n, ref in enumerate(pos_out):
        if ref.shape[0] == mlp_rows:
            ref[...] = flat[pl.ds(tile_row(entries[1], pos_names[n]), mlp_rows), :].astype(BF16)
        else:
            ref[...] = flat[0 : ref.shape[0], :].astype(BF16)


def project_back(entries, me, pos_names, pos_shapes, kept, out_rows, out_plan, sizes):
    rows = kept[1].shape[0]
    outs = [((out_rows, D), BF16)] + [((height, LANES), BF16) for height in pos_shapes]
    outs += [((len(n) * sizes.attn_rows, LANES), BF16) for n in out_plan]
    scratch = [
        pltpu.VMEM((max(sizes.attn_flat, sizes.pos_flat), LANES), F32),
        pltpu.VMEM((rows, 3 * D), BF16),
        pltpu.VMEM((rows, D), BF16),
        pltpu.VMEM((rows, D), BF16),
        pltpu.VMEM((2, 8, D), F32),
    ]
    kernel = functools.partial(
        project_back_kernel, entries, out_plan, sizes.attn_rows, sizes.mlp_rows, len(pos_shapes)
    )
    return call(kernel, "project_back", [me, pos_names, *kept], outs, scratch, 25, 10)


def adamw_step(gradient, weights, first, second):
    first_new = BETA_FIRST * first + (1.0 - BETA_FIRST) * gradient
    second_new = BETA_SECOND * second + (1.0 - BETA_SECOND) * gradient * gradient
    first_hat = first_new / (1.0 - BETA_FIRST**STEP)
    second_hat = second_new / (1.0 - BETA_SECOND**STEP)
    update = LEARNING_RATE * (first_hat / (jnp.sqrt(second_hat) + adam_eps) + WEIGHT_DECAY * weights)
    return (update, first_new, second_new)


def settle_kernel(scale, plan, late_plan, count, place, *refs):
    terms, state, outs = refs[:count], refs[count : count + 3], refs[count + 3 :]
    value = sum(terms[n][first : first + rows, :].astype(F32) for n, first, rows in plan)
    rows = value.shape[0]
    if late_plan:
        late = jnp.concatenate([terms[n][first : first + r, :] for n, first, r in late_plan], axis=0)
        value = value + jnp.where(place[2] > 0, late.astype(F32), 0.0)
    gradient = take_share(value, place[0], place[1]) * scale
    weights, first, second = (tall(ref, rows) for ref in state)
    for ref, result in zip(outs, (gradient, *adamw_step(gradient, weights, first, second))):
        put_flat(ref, result)


def settle(scale, place, terms, plan, late_plan, state):
    operands = list(terms) + list(state)
    return pl.pallas_call(
        functools.partial(settle_kernel, scale, plan, late_plan, len(terms)),
        in_specs=[SMEM_SPEC] + [VMEM_SPEC] * len(operands),
        out_specs=[VMEM_SPEC] * 4,
        out_shape=[jax.ShapeDtypeStruct(state[0].shape, F32)] * 4,
        compiler_params=params(8),
        name="settle",
    )(place, *operands)


AXES = ("dp", "rep")
BIT_CORE, BIT_X, BIT_Y, BIT_Z = 1, 2, 4, 8
PLANE = (BIT_X, BIT_Y, BIT_X | BIT_Y)
DEVICES = 32


def swap(value, bits):
    return lax.ppermute(value, AXES, [(j, j ^ bits) for j in range(DEVICES)])


def together(*values):
    return lax.optimization_barrier(values)


def spread_z(piece):
    return [piece] + [swap(piece, k * BIT_Z) for k in (1, 2, 3)]


def spread_xy(value):
    return [value] + [swap(value, bits) for bits in PLANE]


def numbered(arrays, along_z, first=0):
    offsets = [core | bits for core in (0, BIT_CORE) for bits in (0, *PLANE)]
    return [(a, ([offset | z * BIT_Z for z in along_z], first)) for a, offset in zip(arrays, offsets)]


def sum_plan():
    return [[BIT_CORE | bits | z * BIT_Z for bits in (0, *PLANE) for z in range(4)]] + [
        [bits | z * BIT_Z for z in range(4)] for bits in (0, *PLANE)
    ]


def total(values):
    return sum(value.astype(F32) for value in values).astype(BF16)


def quarters(value):
    return [value[k * value.shape[0] // 4 : (k + 1) * value.shape[0] // 4] for k in range(4)]


def add_kernel(terms, quarter, plane, *refs):
    outs = refs[len(refs) - terms[-1] :]
    rows = outs[0].shape[0] - quarter
    for n, out in enumerate(outs):
        value = sum(
            refs[t][n * rows : (n + 1) * rows, :].astype(F32) for t in range(terms[0])
        )
        if terms[1]:
            value = value + refs[terms[0] + n][...].astype(F32)
        out[0:rows, :] = value.astype(BF16)
        if quarter:
            at = pl.ds(pl.multiple_of((plane[0] ^ n) * quarter, 16), quarter)
            one, two = refs[terms[0] + terms[1] : terms[0] + terms[1] + 2]
            out[rows : rows + quarter, :] = (one[at, :].astype(F32) + two[at, :].astype(F32)).astype(BF16)


def add_parts(stacked, parts, count, plane, late=()):
    rows = stacked[0].shape[0] // count
    quarter = late[0].shape[0] // count if late else 0
    operands = [*stacked, *parts, *late]
    return pl.pallas_call(
        functools.partial(add_kernel, (len(stacked), len(parts), count), quarter),
        in_specs=[SMEM_SPEC] + [VMEM_SPEC] * len(operands),
        out_specs=[VMEM_SPEC] * count,
        out_shape=[jax.ShapeDtypeStruct((rows + quarter, LANES), BF16)] * count,
        compiler_params=params(8),
        name="add_parts",
    )(plane, *operands)


def swap_xy(parts):
    return [parts[0]] + [swap(part, bits) for part, bits in zip(parts[1:], PLANE)]


def swap_z(parts):
    return [parts[0]] + [swap(parts[k], k * BIT_Z) for k in (1, 2, 3)]


class Sizes:
    def __init__(self, count, slots, attn_entries, mlp_entries):
        self.attn_rows = piece_rows(attn_entries, count)
        self.mlp_rows = piece_rows(mlp_entries, count)
        self.attn_flat = max(flat_rows(attn_entries, count, self.attn_rows), ATTN_ROWS)
        self.mlp_flat = max(flat_rows(mlp_entries, count, self.mlp_rows), MLP_ROWS)
        self.pos_count = -(-POS * D // mlp_entries)
        self.pos_flat = flat_rows(mlp_entries, self.pos_count, self.mlp_rows)
        self.pos_flat = max(-(-self.pos_flat // 16) * 16, -(-POS * D_COLS // 16) * 16)
        self.reach = -(-max(slots + BLOCK, slots - SHORT + image_rows(0)) // 8) * 8


class Layer:
    def __init__(self, entries, sizes, slots, tokens, cotangent, lengths, onehot):
        self.entries, self.sizes, self.slots = entries, sizes, slots
        self.tokens, self.cotangent, self.lengths, self.onehot = tokens, cotangent, lengths, onehot

    def project(self, mask, attn_arrays, pos_plan, pos_names):
        self.mask = mask
        (self.embedded, self.normed_b, self.qkv, self.w_qkv, self.w_out, self.vectors, self.passed) = project(
            self.entries, attn_arrays, pos_plan, pos_names, mask, self.onehot, self.tokens, self.sizes
        )

    def attend(self):
        self.mixed, self.log_total, self.residual = attend_all(
            self.slots, self.lengths, self.qkv, self.embedded, self.w_out, self.vectors
        )

    def feed_forward(self, mlp_arrays, mask, plan):
        self.output, self.d_residual, *sent = mlp_both(
            self.entries[1], mlp_arrays, mask, self.mask, self.lengths, self.residual, self.cotangent, plan, self.sizes
        )
        return sent

    def attend_back(self):
        self.d_qkv, self.d_branch_b = attend_back(
            self.lengths, self.qkv, self.mixed, self.log_total, self.w_out, self.d_residual
        )

    def project_back(self, plan, pos_names, pos_shapes):
        kept = (self.onehot, self.embedded, self.normed_b, self.mixed, self.d_qkv, self.d_branch_b)
        kept += (self.w_qkv, self.vectors, self.d_residual)
        self.in_grad, *sent = project_back(
            self.entries, self.mask, pos_names, pos_shapes, kept, self.slots, plan, self.sizes
        )
        return sent[: len(pos_shapes)], sent[len(pos_shapes) :]


def step_by_axes(layer, me, piece):
    sizes, count = layer.sizes, lax.axis_size("dp") * lax.axis_size("rep")
    order = list(range(count))
    height = sizes.mlp_rows
    attn_all = lax.all_gather(piece[: sizes.attn_rows], AXES, axis=0, tiled=True)
    mlp_all = lax.all_gather(piece[sizes.attn_rows :], AXES, axis=0, tiled=True)
    pos_plan = [(1, j * height) for j in range(sizes.pos_count)]
    pos_names = jnp.arange(sizes.pos_count, dtype=jnp.int32)
    layer.project(jnp.zeros((1,), jnp.int32), [(attn_all, (order, 0)), (mlp_all, ([], 0))], pos_plan, pos_names)
    layer.attend()
    mlp_sent = layer.feed_forward([(mlp_all, (order, 0))], layer.mask, [order])
    layer.attend_back()
    (pos_grad,), attn_sent = layer.project_back([order], pos_names, [sizes.pos_flat])
    mlp_terms = [lax.psum_scatter(mlp_sent[0], AXES, scatter_dimension=0, tiled=True)]
    attn_terms = [lax.psum_scatter(attn_sent[0], AXES, scatter_dimension=0, tiled=True)]
    pos_sum = jnp.pad(lax.psum(pos_grad, AXES), ((0, height), (0, 0)))
    first_row = jnp.minimum((me * layer.entries[1]) // TILE * 8, sizes.pos_flat)
    pos_terms = [lax.dynamic_slice_in_dim(pos_sum, first_row, height, axis=0)]
    plans = ([(0, 0, sizes.attn_rows)], [(0, 0, height)], [(1, 0, height)])
    return (layer.output, layer.in_grad), (attn_terms, mlp_terms + pos_terms, plans)


def step_by_hand(layer, me, piece):
    sizes = layer.sizes
    small, large = sizes.attn_rows, sizes.mlp_rows
    z, plane, core = me // BIT_Z, (me // BIT_X) % 4, me % 2
    plan = sum_plan()
    pieces = spread_z(piece)
    mask, near_mask = me.reshape(1), (me % BIT_Z).reshape(1)
    pos_names = jnp.stack([jnp.where(plane == n % 4, core if n < 4 else 1 - core, -1) for n in range(8)])
    back_names, plane_here = jnp.stack([1 - core, core]), plane.reshape(1)
    pieces, layer.onehot, layer.places, mask, near_mask, pos_names, back_names, plane_here = together(
        pieces, layer.onehot, layer.places, mask, near_mask, pos_names, back_names, plane_here
    )
    table = lax.select_n(z, *[p[small:] for p in pieces])
    attn = spread_xy(jnp.concatenate([p[:small] for p in pieces] + [table], axis=0))
    attn, pieces = together(attn, pieces)
    attn = attn + [swap(a, BIT_CORE) for a in attn]
    mlp = [lax.select_n(z, *[pieces[k ^ here][small:] for here in range(4)]) for k in (1, 2, 3)]
    mlp = jnp.concatenate(mlp, axis=0)
    attn, mlp = together(attn, mlp)
    mlp_far = swap(mlp, BIT_CORE)
    mlp = spread_xy(mlp)
    at = 4 * small
    pos_plan = [(n, at) for n in range(8)]
    layer.project(mask, numbered(attn, range(4)), pos_plan, pos_names)
    layer.attend()
    mlp, mlp_far, layer.residual = together(mlp, mlp_far, layer.residual)
    mlp = mlp + [mlp_far] + [swap(a, BIT_CORE) for a in mlp[1:]]
    near = [offset | bits for offset in (0, BIT_CORE) for bits in (0, *PLANE)]
    arrays = numbered(mlp, (1, 2, 3)) + [(layer.passed, (near, 0))]
    mlp_sent = layer.feed_forward(arrays, near_mask, plan)

    parts = add_parts([swap(mlp_sent[0], BIT_CORE)], mlp_sent[1:], 4, plane_here)
    parts, layer.d_residual = together(parts, layer.d_residual)
    mlp_terms = swap_xy(parts)
    layer.attend_back()
    (pos_send, pos_keep), attn_sent = layer.project_back(plan, back_names, [large, large])
    mlp_terms, pos_send, pos_keep, attn_sent = together(mlp_terms, pos_send, pos_keep, attn_sent)

    share = large // 4
    pos_terms = [pos_keep, swap(pos_send, BIT_CORE)]
    sent = add_parts([swap(attn_sent[0], BIT_CORE)], attn_sent[1:], 4, plane_here, pos_terms)
    sent, mlp_terms = together(sent, mlp_terms)
    came = swap_xy(sent)
    mlp_came = swap_z(add_parts(mlp_terms, [], 4, plane_here))
    came = together(came)[0]
    whole_sum = total(came)
    sent = [jnp.concatenate([part, whole_sum[at:]], axis=0) for part in quarters(whole_sum[:at])]
    came, mlp_came = together(swap_z(together(sent)[0]), mlp_came)
    pos = spread_xy(total([value[small:] for value in came]))
    plans = (
        [(n, 0, small) for n in range(4)],
        [(n, 0, large) for n in range(4)],
        [(n, 0, share) for n in range(4, 8)],
    )
    return (layer.output, layer.in_grad), (came, mlp_came + pos, plans)


def body(
    by_hand,
    tokens,
    cotangent,
    lengths,
    pos_map,
    attn_params,
    attn_first,
    attn_second,
    mlp_params,
    mlp_first,
    mlp_second,
):
    slots = tokens.shape[0]
    rows = -(-slots // PART) * PART
    count = lax.axis_size("dp") * lax.axis_size("rep")
    entries = (attn_params.shape[0], mlp_params.shape[0])
    sizes = Sizes(count, slots, *entries)
    me = lax.axis_index("dp") * lax.axis_size("rep") + lax.axis_index("rep")
    me = me.astype(jnp.int32)

    starts = [(me * n) % TILE for n in entries]
    place = jnp.stack(
        [starts[0] % LANES, starts[0] // LANES, starts[1] % LANES, starts[1] // LANES, (me < 2).astype(jnp.int32)]
    )
    heights = (sizes.attn_rows, sizes.mlp_rows)
    piece = pl.pallas_call(
        functools.partial(align_kernel, heights),
        in_specs=[SMEM_SPEC, HBM_SPEC, HBM_SPEC],
        out_specs=VMEM_SPEC,
        out_shape=jax.ShapeDtypeStruct((sum(heights), LANES), BF16),
        scratch_shapes=[
            pltpu.VMEM(attn_params.shape, F32),
            pltpu.VMEM(mlp_params.shape, F32),
            pltpu.SemaphoreType.DMA((2,)),
        ],
        compiler_params=params(8),
        name="align",
    )(place, in_hbm(attn_params), in_hbm(mlp_params))

    pos_full = jnp.pad(pos_map, (0, rows - slots), constant_values=255)
    onehot = (pos_full[:, None] == jnp.arange(256, dtype=jnp.int32)[None, :]).astype(BF16)
    layer = Layer(entries, sizes, slots, tokens, cotangent, lengths, onehot)
    layer.places = (place[:2], place[2:])
    if by_hand:
        outputs, terms = step_by_hand(layer, me, piece)
    else:
        outputs, terms = step_by_axes(layer, me, piece)
        layer.places = (place[:2], place[2:].at[2].set(1))
    scale = 1.0 / math.sqrt(slots * count)
    attn_state, mlp_state = (attn_params, attn_first, attn_second), (mlp_params, mlp_first, mlp_second)
    attn_terms, mlp_terms, plans = terms
    attn_new = settle(scale, layer.places[0], attn_terms, plans[0], (), attn_state)
    mlp_new = settle(scale, layer.places[1], mlp_terms, plans[1], plans[2], mlp_state)
    return (*outputs, *attn_new, *mlp_new)


def solution(mesh):
    split = P(AXES)
    split_rows = P(AXES, None)
    by_hand = mesh.shape["dp"] == 8 and mesh.shape["rep"] == 4
    return jax.shard_map(
        functools.partial(body, by_hand),
        mesh=mesh,
        in_specs=(split_rows, split_rows) + (split,) * 8,
        out_specs=(split_rows, split_rows) + (split,) * 8,
        check_vma=False,
    )
```

```python
import functools
import math

import jax
import jax.numpy as jnp
from jax import lax
from jax.experimental import pallas as pl
from jax.experimental.pallas import tpu as pltpu
from jax.sharding import PartitionSpec as P

D = 384
H = 6
DH = 64
FF = 1536
POS = 145
SHORT = 50
LONG = 145
MOST_LONG = 4
STEP = 10
LANES = 128
TILE = 8 * LANES
PAIRS = H // 2
QKV_COLS = 3 * D // LANES
D_COLS = D // LANES
FF_COLS = FF // LANES

LEARNING_RATE = 0.001
WEIGHT_DECAY = 0.05
BETA_FIRST = 0.9
BETA_SECOND = 0.999
adam_eps = 1e-08

F32 = jnp.float32
BF16 = jnp.bfloat16
NT = (((1,), (1,)), ((), ()))
TN = (((0,), (0,)), ((), ()))
NN = (((1,), (0,)), ((), ()))
BLOCK = 128
PART = 512

ROW_GAIN_ONE = 0
ROW_BIAS_ONE = ROW_GAIN_ONE + D_COLS
ROW_W_QKV = ROW_BIAS_ONE + D_COLS
ROW_B_QKV = ROW_W_QKV + D * QKV_COLS
ROW_W_OUT = ROW_B_QKV + QKV_COLS
ROW_B_OUT = ROW_W_OUT + D * D_COLS
ATTN_ROWS = ROW_B_OUT + D_COLS
ROW_POS = 0
ROW_GAIN_TWO = ROW_POS + POS * D_COLS
ROW_BIAS_TWO = ROW_GAIN_TWO + D_COLS
ROW_W_IN = ROW_BIAS_TWO + D_COLS
ROW_B_IN = ROW_W_IN + D * FF_COLS
ROW_W_BACK = ROW_B_IN + FF_COLS
ROW_B_BACK = ROW_W_BACK + FF * D_COLS
MLP_ROWS = ROW_B_BACK + D_COLS


def dot(a, b, dims=NN):
    return lax.dot_general(a, b, dims, preferred_element_type=F32)


def tile_row(entries, j):
    return pl.multiple_of(((j * entries) // TILE) * 8, 8)


def piece_rows(entries, count):
    most = max((entries * j) % TILE + entries for j in range(count))
    return -(-most // (16 * LANES)) * 16


def flat_rows(entries, count, rows):
    return max((entries * j) // TILE * 8 + rows for j in range(count))


def in_hbm(value):
    return pltpu.with_memory_space_constraint(value, pltpu.HBM)


def params(mebibytes):
    return pltpu.CompilerParams(vmem_limit_bytes=mebibytes * 1024 * 1024)


def cost(microseconds):
    return pl.CostEstimate(flops=int(microseconds * 1.15e9), bytes_accessed=1024, transcendentals=0)


def whole(shape):
    return pl.BlockSpec(shape, lambda *_: (0,) * len(shape))


SMEM_SPEC = pl.BlockSpec(memory_space=pltpu.SMEM)
VMEM_SPEC = pl.BlockSpec(memory_space=pltpu.VMEM)
HBM_SPEC = pl.BlockSpec(memory_space=pltpu.HBM)


def tall(vector, rows):
    entries = vector.shape[0]
    full = entries // TILE * TILE
    parts = [vector[pl.ds(0, full)].reshape(full // LANES, LANES)] if full else []
    if entries > full:
        rest = jnp.concatenate([vector[pl.ds(full, entries - full)], jnp.zeros((full + TILE - entries,), F32)])
        parts.append(rest.reshape(8, LANES))
    height = sum(part.shape[0] for part in parts)
    if height < rows:
        parts.append(jnp.zeros((rows - height, LANES), F32))
    return jnp.concatenate(parts, axis=0)


def put_flat(vector, value):
    entries = vector.shape[0]
    full = entries // TILE * TILE
    if full:
        vector[pl.ds(0, full)] = value[: full // LANES].reshape(full)
    if entries > full:
        vector[pl.ds(full, entries - full)] = value[full // LANES : full // LANES + 8].reshape(TILE)[: entries - full]


def align_kernel(heights, place, attn, mlp, out, attn_here, mlp_here, arrived):
    sources = ((attn, attn_here), (mlp, mlp_here))
    copies = [pltpu.make_async_copy(*source, arrived.at[n]) for n, source in enumerate(sources)]
    for copy in copies:
        copy.start()
    first = 0
    for n, height in enumerate(heights):
        copies[n].wait()
        lanes, rows = place[2 * n], place[2 * n + 1]
        value = tall(sources[n][1], height)
        turned = pltpu.roll(value, lanes, 1)
        below = pltpu.roll(turned, 1, 0)
        lane = lax.broadcasted_iota(jnp.int32, value.shape, 1)
        moved = jnp.where(lane >= lanes, turned, below)
        out[first : first + height, :] = pltpu.roll(moved, rows, 0).astype(BF16)
        first += height


def take_share(value, lanes, rows):
    height = value.shape[0]
    value = pltpu.roll(value, (height - rows) % height, 0)
    turned = pltpu.roll(value, (LANES - lanes) % LANES, 1)
    above = pltpu.roll(turned, height - 1, 0)
    lane = lax.broadcasted_iota(jnp.int32, value.shape, 1)
    return jnp.where(lane < LANES - lanes, turned, above)


def unpack(flat, arrays, entries, rows, me):
    alone = entries // TILE * 8
    edges = [(0, 8), (alone, rows)] if alone > 8 else [(0, rows)]
    for add in (False, True):
        for ref, (numbers, first) in arrays:
            for t, number in enumerate(numbers):
                start, piece = tile_row(entries, number ^ me), first + t * rows
                for low, high in edges:
                    at = pl.ds(pl.multiple_of(start + low, 8), high - low)
                    if add:
                        flat[at, :] += ref[piece + low : piece + high, :].astype(F32)
                    else:
                        flat[at, :] = jnp.zeros((high - low, LANES), F32)
                if add and alone > 8:
                    at = pl.ds(pl.multiple_of(start + 8, 8), alone - 8)
                    flat[at, :] = ref[piece + 8 : piece + alone, :].astype(F32)


def read_matrix(flat, row, depth, cols, target):
    for c in range(cols):
        target[:, c * LANES : (c + 1) * LANES] = flat[pl.ds(row + c, depth, stride=cols), :].astype(BF16)


def read_row(flat, row, cols):
    return jnp.concatenate([flat[row + c : row + c + 1, :] for c in range(cols)], axis=1)


def write_row(flat, row, value):
    for c in range(value.shape[1] // LANES):
        flat[row + c : row + c + 1, :] = value[:, c * LANES : (c + 1) * LANES]


def norm_parts(value):
    average = jnp.mean(value, axis=-1, keepdims=True)
    centred = value - average
    variance = jnp.mean(centred * centred, axis=-1, keepdims=True)
    inverse = lax.rsqrt(variance + 1e-06)
    return centred * inverse, inverse


def norm_back(normed, inverse, gain, grad):
    scaled = grad * gain
    first = jnp.mean(scaled, axis=-1, keepdims=True)
    second = jnp.mean(scaled * normed, axis=-1, keepdims=True)
    return (scaled - first - normed * second) * inverse


def fold_rows(value):
    return jnp.sum(value.reshape(-1, 8, value.shape[-1]), axis=0)


def call(kernel, name, operands, outs, scratch, mebibytes, microseconds):
    return pl.pallas_call(
        kernel,
        in_specs=[SMEM_SPEC if a.dtype == jnp.int32 and a.ndim == 1 else VMEM_SPEC for a in operands],
        out_specs=[VMEM_SPEC] * len(outs),
        out_shape=[jax.ShapeDtypeStruct(shape, kind) for shape, kind in outs],
        scratch_shapes=scratch,
        compiler_params=params(mebibytes),
        cost_estimate=cost(microseconds),
        name=name,
    )(*operands)


def project_kernel(entries, attn_plan, pos_plan, attn_rows, mlp_rows, me, pos_names, onehot, tokens, *refs):
    attn_arrays = [(refs[i], plan) for i, plan in enumerate(attn_plan)]
    refs = refs[len(attn_plan) :]
    embedded, normed_out, qkv, w_qkv, w_out, vectors, pieces_out = refs[:7]
    flat, pos_flat, pos_table = refs[7:]
    slots, rows = tokens.shape[0], embedded.shape[0]

    pos_flat[...] = jnp.zeros_like(pos_flat)
    for n, (array, first) in enumerate(pos_plan):
        pieces_out[n * mlp_rows : (n + 1) * mlp_rows, :] = attn_arrays[array][0][first : first + mlp_rows, :]
        name = pos_names[n]

        @pl.when(name >= 0)
        def _():
            at = pl.ds(tile_row(entries[1], name), mlp_rows)
            pos_flat[at, :] += attn_arrays[array][0][first : first + mlp_rows, :].astype(F32)

    pos_table[...] = jnp.zeros_like(pos_table)
    most = POS // 16 * 16
    for c in range(D_COLS):
        column = pos_flat[pl.ds(ROW_POS + c, most, stride=D_COLS), :]
        pos_table[0:most, c * LANES : (c + 1) * LANES] = column.astype(BF16)
    last = [read_row(pos_flat, ROW_POS + r * D_COLS, D_COLS) for r in range(most, POS)]
    last = jnp.concatenate(last + [jnp.zeros((16 - len(last), D), F32)], axis=0)
    pos_table[most : most + 16, :] = last.astype(BF16)

    unpack(flat, attn_arrays, entries[0], attn_rows, me[0])
    read_matrix(flat, ROW_W_QKV, D, QKV_COLS, w_qkv)
    read_matrix(flat, ROW_W_OUT, D, D_COLS, w_out)
    gain = read_row(flat, ROW_GAIN_ONE, D_COLS)
    bias = read_row(flat, ROW_BIAS_ONE, D_COLS)
    b_qkv = read_row(flat, ROW_B_QKV, QKV_COLS)
    vectors[...] = jnp.zeros_like(vectors)
    vectors[0:1, :] = gain
    vectors[1:2, :] = read_row(flat, ROW_B_OUT, D_COLS)

    embedded[0:slots, :] = tokens[...].astype(F32)
    embedded[slots:rows, :] = jnp.zeros((rows - slots, D), F32)
    for c in range(QKV_COLS):
        qkv[c, rows : qkv.shape[1], :] = jnp.zeros((qkv.shape[1] - rows, LANES), F32)

    def project(i, _):
        at = pl.ds(pl.multiple_of(i * PART, PART), PART)
        value = embedded[at, :] + dot(onehot[at, :], pos_table[...])
        embedded[at, :] = value
        normed, _ = norm_parts(value)
        normed = (normed * gain + bias).astype(BF16)
        normed_out[at, :] = normed
        for k in range(3):
            cols = slice(k * D, (k + 1) * D)
            part = (dot(normed, w_qkv[:, cols]) + b_qkv[:, cols]).astype(BF16).astype(F32)
            if k == 0:
                part = part * DH ** (-0.5)
            for c in range(D_COLS):
                qkv[k * D_COLS + c, at, :] = part[:, c * LANES : (c + 1) * LANES]
        return 0

    lax.fori_loop(0, rows // PART, project, 0)


def project(entries, attn_arrays, pos_plan, pos_names, me, onehot, tokens, sizes):
    rows = onehot.shape[0]
    plan = [numbers for _, numbers in attn_arrays]
    operands = [me, pos_names, onehot, tokens] + [a for a, _ in attn_arrays]
    outs = [
        ((rows, D), F32),
        ((rows, D), BF16),
        ((QKV_COLS, sizes.reach, LANES), F32),
        ((D, 3 * D), BF16),
        ((D, D), BF16),
        ((8, D), F32),
        ((len(pos_plan) * sizes.mlp_rows, LANES), BF16),
    ]
    scratch = [
        pltpu.VMEM((sizes.attn_flat, LANES), F32),
        pltpu.VMEM((sizes.pos_flat, LANES), F32),
        pltpu.VMEM((256, D), BF16),
    ]
    kernel = functools.partial(
        project_kernel, entries, plan, pos_plan, sizes.attn_rows, sizes.mlp_rows
    )
    return call(kernel, "project", operands, outs, scratch, 17, 8)


def image_table(lengths, table):
    images = table.shape[1]
    longs = sum((lengths[i] == LONG).astype(jnp.int32) for i in range(images))
    start, long_seen, short_seen = jnp.int32(0), jnp.int32(0), longs
    for i in range(images):
        length = lengths[i]
        is_long = length == LONG
        place = jnp.where(is_long, long_seen, short_seen)
        table[0, place] = start
        table[1, place] = length
        start = start + length
        long_seen = long_seen + is_long.astype(jnp.int32)
        short_seen = short_seen + 1 - is_long.astype(jnp.int32)
    return start


def image_rows(slot):
    return -(-((LONG if slot < MOST_LONG else SHORT) + 7) // 32) * 32


class Unit:
    def __init__(self, slots, table):
        self.slots = slots
        self.height = image_rows(slots[0])
        self.lows = [table[0, slot] % 8 for slot in slots]
        self.at = [pl.ds(pl.multiple_of(table[0, s] - low, 8), self.height) for s, low in zip(slots, self.lows)]
        self.lengths = [table[1, slot] for slot in slots]
        self.valid = jnp.concatenate([inside(self.height, *span) for span in zip(self.lows, self.lengths)], axis=0)

    def load(self, ref, *index):
        return jnp.concatenate([ref[(*index, at, slice(None))] for at in self.at], axis=0)

    def store(self, ref, index, value):
        for n, at in enumerate(self.at):
            here = slice(n * self.height, (n + 1) * self.height)
            pltpu.store(ref.at[index, at, :], value[here], mask=self.valid[here])

    def mask(self):
        count, height = len(self.slots), self.height
        shape = (count * height, count * height)
        key = lax.broadcasted_iota(jnp.int32, shape, 1)
        row = lax.broadcasted_iota(jnp.int32, shape, 0)
        seen = None
        for n in range(count):
            low = n * height + self.lows[n]
            part = (key >= low) & (key < low + self.lengths[n])
            if count > 1:
                part = part & (row >= n * height) & (row < (n + 1) * height)
            seen = part if seen is None else seen | part
        bias = jnp.where(seen, 0.0, -1e30)
        return jnp.concatenate([bias, bias], axis=0)


def units(images, table):
    shorts = list(range(MOST_LONG, images))
    slots = [[slot] for slot in range(MOST_LONG)] + [shorts[i : i + 2] for i in range(0, len(shorts), 2)]
    return [Unit(these, table) for these in slots]


def both_heads(value):
    left = lax.broadcasted_iota(jnp.int32, value.shape, 1) < DH
    zero = jnp.zeros_like(value)
    return jnp.concatenate([jnp.where(left, value, zero), jnp.where(left, zero, value)], axis=0)


def one_of_heads(value):
    height = value.shape[0] // 2
    left = lax.broadcasted_iota(jnp.int32, (height, LANES), 1) < DH
    return jnp.where(left, value[:height], value[height:])


def inside(height, low, length):
    row = lax.broadcasted_iota(jnp.int32, (height, LANES), 0)
    return (row >= low) & (row < low + length)


def attend(queries, keys, values, bias):
    scores = dot(both_heads(queries), keys, NT) + bias
    peak = jnp.max(scores, axis=1, keepdims=True)
    probs = jnp.exp(scores - peak).astype(BF16)
    out = dot(probs, jnp.concatenate([values, jnp.ones_like(values)], axis=1))
    total = out[:, LANES:]
    return one_of_heads(out[:, :LANES] / total), peak + jnp.log(total)


def attend_kernel(slots, lengths, qkv, embedded, w_out, vectors, mixed, log_total, residual, table):
    images = lengths.shape[0]
    rows = residual.shape[0]
    live = image_table(lengths, table)
    ahead = slots // 8 * 8
    for pair in range(PAIRS):
        mixed[pair, ahead:, :] = jnp.zeros((mixed.shape[1] - ahead, LANES), F32)
    items = [(n, unit, pair) for n, unit in enumerate(units(images, table)) for pair in range(PAIRS)]
    biases, log_totals = {}, {}

    def first(n, unit, pair):
        if n not in biases:
            biases[n] = unit.mask()
            log_totals[n] = jnp.zeros((biases[n].shape[0], LANES), F32)
        queries, keys, values = (unit.load(qkv, k * PAIRS + pair).astype(BF16) for k in range(3))
        return values, dot(both_heads(queries), keys, NT)

    def second(n, unit, pair, values, scores):
        scores = scores + biases[n]
        peak = jnp.max(scores, axis=1, keepdims=True)
        return values, peak, jnp.exp(scores - peak).astype(BF16)

    def third(n, unit, pair, values, peak, probs):
        out = dot(probs, jnp.concatenate([values, jnp.ones_like(values)], axis=1))
        total = out[:, LANES:]
        lane = lax.broadcasted_iota(jnp.int32, total.shape, 1)
        log_totals[n] = jnp.where(lane == pair, peak + jnp.log(total), log_totals[n])
        unit.store(mixed, pair, one_of_heads(out[:, :LANES] / total).astype(BF16).astype(F32))
        if pair == PAIRS - 1:
            log_total[n, 0 : total.shape[0], :] = log_totals.pop(n)

    ones, twos = {}, {}
    for t in range(len(items) + 2):
        if t < len(items):
            ones[t] = first(*items[t])
        if 0 <= t - 1 < len(items):
            twos[t - 1] = second(*items[t - 1], *ones.pop(t - 1))
        if 0 <= t - 2 < len(items):
            third(*items[t - 2], *twos.pop(t - 2))

    low = live % 8
    base = pl.multiple_of(live - low, 8)
    length = slots - live
    most = -(-(slots - images * SHORT + (7 if (images * SHORT) % 8 else 0)) // BLOCK)
    for blocks in range(1, most + 1):

        @pl.when((low + length > (blocks - 1) * BLOCK) & (low + length <= blocks * BLOCK))
        def _():
            height = blocks * BLOCK
            key = lax.broadcasted_iota(jnp.int32, (2 * BLOCK, height), 1)
            bias = jnp.where((key >= low) & (key < low + length), 0.0, -1e30)
            for pair in range(PAIRS):
                keys = qkv[PAIRS + pair, pl.ds(base, height), :].astype(BF16)
                values = qkv[2 * PAIRS + pair, pl.ds(base, height), :].astype(BF16)
                for block in range(blocks):
                    at = pl.ds(pl.multiple_of(base + block * BLOCK, 8), BLOCK)
                    out, _ = attend(qkv[pair, at, :].astype(BF16), keys, values, bias)
                    valid = inside(BLOCK, low - block * BLOCK, length)
                    pltpu.store(mixed.at[pair, at, :], out.astype(BF16).astype(F32), mask=valid)

    def finish(i, _):
        at = pl.ds(pl.multiple_of(i * PART, PART), PART)
        together = jnp.concatenate([mixed[c, at, :] for c in range(D_COLS)], axis=1).astype(BF16)
        residual[at, :] = embedded[at, :] + dot(together, w_out[...]) + vectors[1:2, :]
        return 0

    lax.fori_loop(0, rows // PART, finish, 0)


def attend_all(slots, lengths, qkv, embedded, w_out, vectors):
    rows = embedded.shape[0]
    images = lengths.shape[0]
    units_count = MOST_LONG + -(-(images - MOST_LONG) // 2)
    height = 2 * max(image_rows(0), 2 * image_rows(MOST_LONG))
    outs = [((PAIRS,) + qkv.shape[1:], F32), ((units_count, height, LANES), F32), ((rows, D), F32)]
    scratch = [pltpu.SMEM((2, images), jnp.int32)]
    operands = [lengths, qkv, embedded, w_out, vectors]
    return call(functools.partial(attend_kernel, slots), "attend", operands, outs, scratch, 15, 10)


def gelu_parts(value):
    share = 0.5 + 0.5 * lax.erf(value * math.sqrt(0.5))
    bell = jnp.exp2((value * value) * (-0.5 * math.log2(math.e)))
    return value * share, share + value * (bell * (1.0 / math.sqrt(2.0 * math.pi)))


def with_ones(value_t):
    return jnp.concatenate([value_t, jnp.ones((16, value_t.shape[1]), BF16)], axis=0)


def pack(flat, entries, rows, me, targets):
    for ref, numbers in targets:
        for t, number in enumerate(numbers):
            start = tile_row(entries, number ^ me)
            ref[t * rows : (t + 1) * rows, :] = flat[pl.ds(start, rows), :].astype(BF16)


def mlp_kernel(entries, in_plan, out_plan, piece, mask, me, lengths, residual, cotangent, *refs):
    arrays = [(refs[i], plan) for i, plan in enumerate(in_plan)]
    refs = refs[len(in_plan) :]
    output, d_residual = refs[:2]
    targets = [(refs[2 + i], plan) for i, plan in enumerate(out_plan)]
    refs = refs[2 + len(out_plan) :]
    flat, w_in, w_back, normed_b, active_b, d_hidden_b, out_f32, sums, out_grad = refs
    slots, rows = cotangent.shape[0], residual.shape[0]
    live = sum(lengths[i] for i in range(lengths.shape[0]))
    row = lax.broadcasted_iota(jnp.int32, (slots, D), 0)
    out_grad[0:slots, :] = jnp.where(row < live, cotangent[...].astype(F32), 0.0).astype(BF16)
    out_grad[slots:rows, :] = jnp.zeros((rows - slots, D), BF16)

    unpack(flat, arrays, entries, piece, mask[0])
    read_matrix(flat, ROW_W_IN, D, FF_COLS, w_in)
    read_matrix(flat, ROW_W_BACK, FF, D_COLS, w_back)
    gain = read_row(flat, ROW_GAIN_TWO, D_COLS)
    bias = read_row(flat, ROW_BIAS_TWO, D_COLS)
    b_in = read_row(flat, ROW_B_IN, FF_COLS)
    b_back = read_row(flat, ROW_B_BACK, D_COLS)
    sums[...] = jnp.zeros_like(sums)

    def step(i, _):
        at = pl.ds(pl.multiple_of(i * PART, PART), PART)
        value = residual[at, :]
        grad_b = out_grad[at, :]
        normed, inverse = norm_parts(value)
        low = (normed * gain + bias).astype(BF16)
        normed_b[at, :] = low
        for c in range(FF // 256):
            cols = slice(c * 256, (c + 1) * 256)
            hidden = dot(low, w_in[:, cols]) + b_in[:, cols]
            d_active = dot(grad_b, w_back[cols, :], NT)
            active, slope = gelu_parts(hidden)
            d_hidden = (d_active * slope).astype(BF16)
            active_b[at, cols] = active.astype(BF16)
            d_hidden_b[at, cols] = d_hidden
        out_f32[at, :] = value + b_back + dot(active_b[at, :], w_back[...])
        d_normed = dot(d_hidden_b[at, :], w_in[...], NT)
        grad = grad_b.astype(F32)
        d_residual[at, :] = grad + norm_back(normed, inverse, gain, d_normed)
        sums[0] += fold_rows(d_normed * normed)
        sums[1] += fold_rows(d_normed)
        return 0

    lax.fori_loop(0, rows // PART, step, 0)
    output[...] = out_f32[0 : output.shape[0], :].astype(BF16)

    flat[0:ROW_GAIN_TWO, :] = jnp.zeros((ROW_GAIN_TWO, LANES), F32)
    flat[MLP_ROWS:, :] = jnp.zeros((flat.shape[0] - MLP_ROWS, LANES), F32)
    write_row(flat, ROW_GAIN_TWO, jnp.sum(sums[0], axis=0, keepdims=True))
    write_row(flat, ROW_BIAS_TWO, jnp.sum(sums[1], axis=0, keepdims=True))
    normed_t = with_ones(normed_b[...].T)
    column_sums = dot(jnp.ones((16, rows), BF16), out_grad[...])
    write_row(flat, ROW_B_BACK, column_sums[0:1])
    for c in range(0, FF_COLS, 2):
        part = dot(normed_t, d_hidden_b[:, c * LANES : (c + 2) * LANES])
        for k in range(2):
            flat[pl.ds(ROW_W_IN + c + k, D, stride=FF_COLS), :] = part[0:D, k * LANES : (k + 1) * LANES]
        write_row(flat, ROW_B_IN + c, part[D : D + 1])
    for r in range(0, FF, 256):
        part = dot(active_b[:, r : r + 256], out_grad[...], TN)
        for c in range(D_COLS):
            flat[pl.ds(ROW_W_BACK + r * D_COLS + c, 256, stride=D_COLS), :] = part[:, c * LANES : (c + 1) * LANES]
    pack(flat, entries, piece, me[0], targets)


def mlp_both(entries, arrays, mask, me, lengths, residual, cotangent, out_plan, sizes):
    rows = residual.shape[0]
    plan = [numbers for _, numbers in arrays]
    operands = [mask, me, lengths, residual, cotangent] + [a for a, _ in arrays]
    outs = [(cotangent.shape, BF16), ((rows, D), F32)]
    outs += [((len(n) * sizes.mlp_rows, LANES), BF16) for n in out_plan]
    scratch = [
        pltpu.VMEM((sizes.mlp_flat, LANES), F32),
        pltpu.VMEM((D, FF), BF16),
        pltpu.VMEM((FF, D), BF16),
        pltpu.VMEM((rows, D), BF16),
        pltpu.VMEM((rows, FF), BF16),
        pltpu.VMEM((rows, FF), BF16),
        pltpu.VMEM((rows, D), F32),
        pltpu.VMEM((2, 8, D), F32),
        pltpu.VMEM((rows, D), BF16),
    ]
    kernel = functools.partial(mlp_kernel, entries, plan, out_plan, sizes.mlp_rows)
    return call(kernel, "feed_forward", operands, outs, scratch, 28, 18)


def attend_back_kernel(lengths, qkv, mixed, log_total, w_out, d_residual, d_qkv, d_branch_b, d_mixed, table):
    images = lengths.shape[0]
    rows = d_residual.shape[0]
    image_table(lengths, table)
    ahead = images * SHORT // 8 * 8
    for c in range(QKV_COLS):
        d_qkv[c, ahead:, :] = jnp.zeros((d_qkv.shape[1] - ahead, LANES), F32)

    def enter(i, _):
        at = pl.ds(pl.multiple_of(i * PART, PART), PART)
        branch = d_residual[at, :].astype(BF16)
        d_branch_b[at, :] = branch
        value = dot(branch, w_out[...], NT).astype(BF16).astype(F32)
        for c in range(D_COLS):
            d_mixed[c, at, :] = value[:, c * LANES : (c + 1) * LANES]
        return 0

    lax.fori_loop(0, rows // PART, enter, 0)
    for c in range(D_COLS):
        d_mixed[c, rows : d_mixed.shape[1], :] = jnp.zeros((d_mixed.shape[1] - rows, LANES), F32)

    items = [(n, unit, pair) for n, unit in enumerate(units(images, table)) for pair in range(PAIRS)]
    biases = {}

    def first(n, unit, pair):
        if n not in biases:
            biases[n] = unit.mask()
        queries, keys, values = (unit.load(qkv, k * PAIRS + pair).astype(BF16) for k in range(3))
        queries = both_heads(queries)
        grad = jnp.where(unit.valid, unit.load(d_mixed, pair), 0.0)
        grads = both_heads(grad.astype(BF16))
        product = both_heads((grad * unit.load(mixed, pair)).astype(BF16))
        left = jnp.concatenate([grads, product], axis=1)
        right = jnp.concatenate([values, -jnp.ones_like(values)], axis=1)
        return queries, keys, grads, dot(queries, keys, NT), dot(left, right, NT)

    def second(n, unit, pair, queries, keys, grads, scores, d_probs):
        log_totals = log_total[n, 0 : scores.shape[0], :]
        probs = jnp.exp(scores + biases[n] - log_totals[:, pair : pair + 1])
        return queries, keys, grads, probs.astype(BF16), (probs * d_probs).astype(BF16)

    def third(n, unit, pair, queries, keys, grads, probs, d_scores):
        unit.store(d_qkv, pair, one_of_heads(dot(d_scores, keys)) * DH ** (-0.5))
        unit.store(d_qkv, PAIRS + pair, dot(d_scores, queries, TN))
        unit.store(d_qkv, 2 * PAIRS + pair, dot(probs, grads, TN))

    ones, twos = {}, {}
    for t in range(len(items) + 2):
        if t < len(items):
            ones[t] = first(*items[t])
        if 0 <= t - 1 < len(items):
            twos[t - 1] = second(*items[t - 1], *ones.pop(t - 1))
        if 0 <= t - 2 < len(items):
            third(*items[t - 2], *twos.pop(t - 2))


def attend_back(lengths, qkv, mixed, log_total, w_out, d_residual):
    rows = d_residual.shape[0]
    outs = [(qkv.shape, F32), ((rows, D), BF16)]
    scratch = [pltpu.VMEM(mixed.shape, F32), pltpu.SMEM((2, lengths.shape[0]), jnp.int32)]
    operands = [lengths, qkv, mixed, log_total, w_out, d_residual]
    return call(attend_back_kernel, "attend_back", operands, outs, scratch, 22, 12)


def project_back_kernel(entries, out_plan, piece, mlp_rows, pos_count, me, pos_names, *refs):
    (onehot, embedded, normed_b, mixed, d_qkv, d_branch_b, w_qkv, vectors, d_residual) = refs[:9]
    in_grad, pos_out = refs[9], refs[10 : 10 + pos_count]
    refs = refs[10 + pos_count :]
    targets = [(refs[i], plan) for i, plan in enumerate(out_plan)]
    flat, d_qkv_b, d_embedded_b, mixed_b, sums = refs[len(out_plan) :]
    rows = embedded.shape[0]
    gain = vectors[0:1, :]
    sums[...] = jnp.zeros_like(sums)

    def leave(i, _):
        at = pl.ds(pl.multiple_of(i * PART, PART), PART)
        grads = jnp.concatenate([d_qkv[c, at, :] for c in range(QKV_COLS)], axis=1).astype(BF16)
        d_qkv_b[at, :] = grads
        mixed_b[at, :] = jnp.concatenate([mixed[c, at, :] for c in range(D_COLS)], axis=1).astype(BF16)
        d_normed = dot(grads, w_qkv[...], NT)
        normed, inverse = norm_parts(embedded[at, :])
        value = d_residual[at, :] + norm_back(normed, inverse, gain, d_normed)
        d_embedded_b[at, :] = value.astype(BF16)
        sums[0] += fold_rows(d_normed * normed)
        sums[1] += fold_rows(d_normed)
        return 0

    lax.fori_loop(0, rows // PART, leave, 0)
    in_grad[...] = d_embedded_b[0 : in_grad.shape[0], :]

    flat[ATTN_ROWS:, :] = jnp.zeros((flat.shape[0] - ATTN_ROWS, LANES), F32)
    write_row(flat, ROW_GAIN_ONE, jnp.sum(sums[0], axis=0, keepdims=True))
    write_row(flat, ROW_BIAS_ONE, jnp.sum(sums[1], axis=0, keepdims=True))
    normed_t = with_ones(normed_b[...].T)
    for k in range(3):
        cols = slice(k * D, (k + 1) * D)
        part = dot(normed_t, d_qkv_b[:, cols])
        write_row(flat, ROW_B_QKV + k * D_COLS, part[D : D + 1])
        for c in range(D_COLS):
            flat[pl.ds(ROW_W_QKV + k * D_COLS + c, D, stride=QKV_COLS), :] = part[0:D, c * LANES : (c + 1) * LANES]
    part = dot(with_ones(mixed_b[...].T), d_branch_b[...])
    write_row(flat, ROW_B_OUT, part[D : D + 1])
    for c in range(D_COLS):
        flat[pl.ds(ROW_W_OUT + c, D, stride=D_COLS), :] = part[0:D, c * LANES : (c + 1) * LANES]
    pack(flat, entries[0], piece, me[0], targets)

    pos_grad = dot(onehot[...], d_embedded_b[...], TN)
    flat[ROW_GAIN_TWO:, :] = jnp.zeros((flat.shape[0] - ROW_GAIN_TWO, LANES), F32)
    for c in range(D_COLS):
        flat[pl.ds(ROW_POS + c, POS, stride=D_COLS), :] = pos_grad[0:POS, c * LANES : (c + 1) * LANES]
    for n, ref in enumerate(pos_out):
        if ref.shape[0] == mlp_rows:
            ref[...] = flat[pl.ds(tile_row(entries[1], pos_names[n]), mlp_rows), :].astype(BF16)
        else:
            ref[...] = flat[0 : ref.shape[0], :].astype(BF16)


def project_back(entries, me, pos_names, pos_shapes, kept, out_rows, out_plan, sizes):
    rows = kept[1].shape[0]
    outs = [((out_rows, D), BF16)] + [((height, LANES), BF16) for height in pos_shapes]
    outs += [((len(n) * sizes.attn_rows, LANES), BF16) for n in out_plan]
    scratch = [
        pltpu.VMEM((max(sizes.attn_flat, sizes.pos_flat), LANES), F32),
        pltpu.VMEM((rows, 3 * D), BF16),
        pltpu.VMEM((rows, D), BF16),
        pltpu.VMEM((rows, D), BF16),
        pltpu.VMEM((2, 8, D), F32),
    ]
    kernel = functools.partial(
        project_back_kernel, entries, out_plan, sizes.attn_rows, sizes.mlp_rows, len(pos_shapes)
    )
    return call(kernel, "project_back", [me, pos_names, *kept], outs, scratch, 25, 10)


def adamw_step(gradient, weights, first, second):
    first_new = BETA_FIRST * first + (1.0 - BETA_FIRST) * gradient
    second_new = BETA_SECOND * second + (1.0 - BETA_SECOND) * gradient * gradient
    first_hat = first_new / (1.0 - BETA_FIRST**STEP)
    second_hat = second_new / (1.0 - BETA_SECOND**STEP)
    update = LEARNING_RATE * (first_hat / (jnp.sqrt(second_hat) + adam_eps) + WEIGHT_DECAY * weights)
    return (update, first_new, second_new)


def settle_kernel(scale, plan, late_plan, count, place, *refs):
    terms, state, outs = refs[:count], refs[count : count + 3], refs[count + 3 :]
    value = sum(terms[n][first : first + rows, :].astype(F32) for n, first, rows in plan)
    rows = value.shape[0]
    if late_plan:
        late = jnp.concatenate([terms[n][first : first + r, :] for n, first, r in late_plan], axis=0)
        value = value + jnp.where(place[2] > 0, late.astype(F32), 0.0)
    gradient = take_share(value, place[0], place[1]) * scale
    weights, first, second = (tall(ref, rows) for ref in state)
    for ref, result in zip(outs, (gradient, *adamw_step(gradient, weights, first, second))):
        put_flat(ref, result)


def settle(scale, place, terms, plan, late_plan, state):
    operands = list(terms) + list(state)
    return pl.pallas_call(
        functools.partial(settle_kernel, scale, plan, late_plan, len(terms)),
        in_specs=[SMEM_SPEC] + [VMEM_SPEC] * len(operands),
        out_specs=[VMEM_SPEC] * 4,
        out_shape=[jax.ShapeDtypeStruct(state[0].shape, F32)] * 4,
        compiler_params=params(8),
        name="settle",
    )(place, *operands)


AXES = ("dp", "rep")
BIT_CORE, BIT_X, BIT_Y, BIT_Z = 1, 2, 4, 8
PLANE = (BIT_X, BIT_Y, BIT_X | BIT_Y)
DEVICES = 32


def swap(value, bits):
    return lax.ppermute(value, AXES, [(j, j ^ bits) for j in range(DEVICES)])


def together(*values):
    return lax.optimization_barrier(values)


def spread_z(piece):
    return [piece] + [swap(piece, k * BIT_Z) for k in (1, 2, 3)]


def spread_xy(value):
    return [value] + [swap(value, bits) for bits in PLANE]


def numbered(arrays, along_z, first=0):
    offsets = [core | bits for core in (0, BIT_CORE) for bits in (0, *PLANE)]
    return [(a, ([offset | z * BIT_Z for z in along_z], first)) for a, offset in zip(arrays, offsets)]


def sum_plan():
    return [[BIT_CORE | bits | z * BIT_Z for bits in (0, *PLANE) for z in range(4)]] + [
        [bits | z * BIT_Z for z in range(4)] for bits in (0, *PLANE)
    ]


def total(values):
    return sum(value.astype(F32) for value in values).astype(BF16)


def quarters(value):
    return [value[k * value.shape[0] // 4 : (k + 1) * value.shape[0] // 4] for k in range(4)]


def add_kernel(terms, quarter, plane, *refs):
    outs = refs[len(refs) - terms[-1] :]
    rows = outs[0].shape[0] - quarter
    for n, out in enumerate(outs):
        value = sum(
            refs[t][n * rows : (n + 1) * rows, :].astype(F32) for t in range(terms[0])
        )
        if terms[1]:
            value = value + refs[terms[0] + n][...].astype(F32)
        out[0:rows, :] = value.astype(BF16)
        if quarter:
            at = pl.ds(pl.multiple_of((plane[0] ^ n) * quarter, 16), quarter)
            one, two = refs[terms[0] + terms[1] : terms[0] + terms[1] + 2]
            out[rows : rows + quarter, :] = (one[at, :].astype(F32) + two[at, :].astype(F32)).astype(BF16)


def add_parts(stacked, parts, count, plane, late=()):
    rows = stacked[0].shape[0] // count
    quarter = late[0].shape[0] // count if late else 0
    operands = [*stacked, *parts, *late]
    return pl.pallas_call(
        functools.partial(add_kernel, (len(stacked), len(parts), count), quarter),
        in_specs=[SMEM_SPEC] + [VMEM_SPEC] * len(operands),
        out_specs=[VMEM_SPEC] * count,
        out_shape=[jax.ShapeDtypeStruct((rows + quarter, LANES), BF16)] * count,
        compiler_params=params(8),
        name="add_parts",
    )(plane, *operands)


def swap_xy(parts):
    return [parts[0]] + [swap(part, bits) for part, bits in zip(parts[1:], PLANE)]


def swap_z(parts):
    return [parts[0]] + [swap(parts[k], k * BIT_Z) for k in (1, 2, 3)]


class Sizes:
    def __init__(self, count, slots, attn_entries, mlp_entries):
        self.attn_rows = piece_rows(attn_entries, count)
        self.mlp_rows = piece_rows(mlp_entries, count)
        self.attn_flat = max(flat_rows(attn_entries, count, self.attn_rows), ATTN_ROWS)
        self.mlp_flat = max(flat_rows(mlp_entries, count, self.mlp_rows), MLP_ROWS)
        self.pos_count = -(-POS * D // mlp_entries)
        self.pos_flat = flat_rows(mlp_entries, self.pos_count, self.mlp_rows)
        self.pos_flat = max(-(-self.pos_flat // 16) * 16, -(-POS * D_COLS // 16) * 16)
        self.reach = -(-max(slots + BLOCK, slots - SHORT + image_rows(0)) // 8) * 8


class Layer:
    def __init__(self, entries, sizes, slots, tokens, cotangent, lengths, onehot):
        self.entries, self.sizes, self.slots = entries, sizes, slots
        self.tokens, self.cotangent, self.lengths, self.onehot = tokens, cotangent, lengths, onehot

    def project(self, mask, attn_arrays, pos_plan, pos_names):
        self.mask = mask
        (self.embedded, self.normed_b, self.qkv, self.w_qkv, self.w_out, self.vectors, self.passed) = project(
            self.entries, attn_arrays, pos_plan, pos_names, mask, self.onehot, self.tokens, self.sizes
        )

    def attend(self):
        self.mixed, self.log_total, self.residual = attend_all(
            self.slots, self.lengths, self.qkv, self.embedded, self.w_out, self.vectors
        )

    def feed_forward(self, mlp_arrays, mask, plan):
        self.output, self.d_residual, *sent = mlp_both(
            self.entries[1], mlp_arrays, mask, self.mask, self.lengths, self.residual, self.cotangent, plan, self.sizes
        )
        return sent

    def attend_back(self):
        self.d_qkv, self.d_branch_b = attend_back(
            self.lengths, self.qkv, self.mixed, self.log_total, self.w_out, self.d_residual
        )

    def project_back(self, plan, pos_names, pos_shapes):
        kept = (self.onehot, self.embedded, self.normed_b, self.mixed, self.d_qkv, self.d_branch_b)
        kept += (self.w_qkv, self.vectors, self.d_residual)
        self.in_grad, *sent = project_back(
            self.entries, self.mask, pos_names, pos_shapes, kept, self.slots, plan, self.sizes
        )
        return sent[: len(pos_shapes)], sent[len(pos_shapes) :]


def step_by_axes(layer, me, piece):
    sizes, count = layer.sizes, lax.axis_size("dp") * lax.axis_size("rep")
    order = list(range(count))
    height = sizes.mlp_rows
    attn_all = lax.all_gather(piece[: sizes.attn_rows], AXES, axis=0, tiled=True)
    mlp_all = lax.all_gather(piece[sizes.attn_rows :], AXES, axis=0, tiled=True)
    pos_plan = [(1, j * height) for j in range(sizes.pos_count)]
    pos_names = jnp.arange(sizes.pos_count, dtype=jnp.int32)
    layer.project(jnp.zeros((1,), jnp.int32), [(attn_all, (order, 0)), (mlp_all, ([], 0))], pos_plan, pos_names)
    layer.attend()
    mlp_sent = layer.feed_forward([(mlp_all, (order, 0))], layer.mask, [order])
    layer.attend_back()
    (pos_grad,), attn_sent = layer.project_back([order], pos_names, [sizes.pos_flat])
    mlp_terms = [lax.psum_scatter(mlp_sent[0], AXES, scatter_dimension=0, tiled=True)]
    attn_terms = [lax.psum_scatter(attn_sent[0], AXES, scatter_dimension=0, tiled=True)]
    pos_sum = jnp.pad(lax.psum(pos_grad, AXES), ((0, height), (0, 0)))
    first_row = jnp.minimum((me * layer.entries[1]) // TILE * 8, sizes.pos_flat)
    pos_terms = [lax.dynamic_slice_in_dim(pos_sum, first_row, height, axis=0)]
    plans = ([(0, 0, sizes.attn_rows)], [(0, 0, height)], [(1, 0, height)])
    return (layer.output, layer.in_grad), (attn_terms, mlp_terms + pos_terms, plans)


def step_by_hand(layer, me, piece):
    sizes = layer.sizes
    small, large = sizes.attn_rows, sizes.mlp_rows
    z, plane, core = me // BIT_Z, (me // BIT_X) % 4, me % 2
    plan = sum_plan()
    pieces = spread_z(piece)
    mask, near_mask = me.reshape(1), (me % BIT_Z).reshape(1)
    pos_names = jnp.stack([jnp.where(plane == n % 4, core if n < 4 else 1 - core, -1) for n in range(8)])
    back_names, plane_here = jnp.stack([1 - core, core]), plane.reshape(1)
    pieces, layer.onehot, layer.places, mask, near_mask, pos_names, back_names, plane_here = together(
        pieces, layer.onehot, layer.places, mask, near_mask, pos_names, back_names, plane_here
    )
    table = lax.select_n(z, *[p[small:] for p in pieces])
    attn = spread_xy(jnp.concatenate([p[:small] for p in pieces] + [table], axis=0))
    attn, pieces = together(attn, pieces)
    attn = attn + [swap(a, BIT_CORE) for a in attn]
    mlp = [lax.select_n(z, *[pieces[k ^ here][small:] for here in range(4)]) for k in (1, 2, 3)]
    mlp = jnp.concatenate(mlp, axis=0)
    mlp_far = swap(mlp, BIT_CORE)
    mlp = spread_xy(mlp)
    at = 4 * small
    pos_plan = [(n, at) for n in range(8)]
    layer.project(mask, numbered(attn, range(4)), pos_plan, pos_names)
    layer.attend()
    mlp, mlp_far, layer.residual = together(mlp, mlp_far, layer.residual)
    mlp = mlp + [mlp_far] + [swap(a, BIT_CORE) for a in mlp[1:]]
    near = [offset | bits for offset in (0, BIT_CORE) for bits in (0, *PLANE)]
    arrays = numbered(mlp, (1, 2, 3)) + [(layer.passed, (near, 0))]
    mlp_sent = layer.feed_forward(arrays, near_mask, plan)

    parts = add_parts([swap(mlp_sent[0], BIT_CORE)], mlp_sent[1:], 4, plane_here)
    parts, layer.d_residual = together(parts, layer.d_residual)
    mlp_terms = swap_xy(parts)
    layer.attend_back()
    (pos_send, pos_keep), attn_sent = layer.project_back(plan, back_names, [large, large])
    mlp_terms, pos_send, pos_keep, attn_sent = together(mlp_terms, pos_send, pos_keep, attn_sent)

    share = large // 4
    pos_terms = [pos_keep, swap(pos_send, BIT_CORE)]
    sent = add_parts([swap(attn_sent[0], BIT_CORE)], attn_sent[1:], 4, plane_here, pos_terms)
    sent, mlp_terms = together(sent, mlp_terms)
    came = swap_xy(sent)
    mlp_came = swap_z(add_parts(mlp_terms, [], 4, plane_here))
    came = together(came)[0]
    whole_sum = total(came)
    sent = [jnp.concatenate([part, whole_sum[at:]], axis=0) for part in quarters(whole_sum[:at])]
    came, mlp_came = together(swap_z(together(sent)[0]), mlp_came)
    pos = spread_xy(total([value[small:] for value in came]))
    plans = (
        [(n, 0, small) for n in range(4)],
        [(n, 0, large) for n in range(4)],
        [(n, 0, share) for n in range(4, 8)],
    )
    return (layer.output, layer.in_grad), (came, mlp_came + pos, plans)


def body(
    by_hand,
    tokens,
    cotangent,
    lengths,
    pos_map,
    attn_params,
    attn_first,
    attn_second,
    mlp_params,
    mlp_first,
    mlp_second,
):
    slots = tokens.shape[0]
    rows = -(-slots // PART) * PART
    count = lax.axis_size("dp") * lax.axis_size("rep")
    entries = (attn_params.shape[0], mlp_params.shape[0])
    sizes = Sizes(count, slots, *entries)
    me = lax.axis_index("dp") * lax.axis_size("rep") + lax.axis_index("rep")
    me = me.astype(jnp.int32)

    starts = [(me * n) % TILE for n in entries]
    place = jnp.stack(
        [starts[0] % LANES, starts[0] // LANES, starts[1] % LANES, starts[1] // LANES, (me < 2).astype(jnp.int32)]
    )
    heights = (sizes.attn_rows, sizes.mlp_rows)
    piece = pl.pallas_call(
        functools.partial(align_kernel, heights),
        in_specs=[SMEM_SPEC, HBM_SPEC, HBM_SPEC],
        out_specs=VMEM_SPEC,
        out_shape=jax.ShapeDtypeStruct((sum(heights), LANES), BF16),
        scratch_shapes=[
            pltpu.VMEM(attn_params.shape, F32),
            pltpu.VMEM(mlp_params.shape, F32),
            pltpu.SemaphoreType.DMA((2,)),
        ],
        compiler_params=params(8),
        name="align",
    )(place, in_hbm(attn_params), in_hbm(mlp_params))

    pos_full = jnp.pad(pos_map, (0, rows - slots), constant_values=255)
    onehot = (pos_full[:, None] == jnp.arange(256, dtype=jnp.int32)[None, :]).astype(BF16)
    layer = Layer(entries, sizes, slots, tokens, cotangent, lengths, onehot)
    layer.places = (place[:2], place[2:])
    if by_hand:
        outputs, terms = step_by_hand(layer, me, piece)
    else:
        outputs, terms = step_by_axes(layer, me, piece)
        layer.places = (place[:2], place[2:].at[2].set(1))
    scale = 1.0 / math.sqrt(slots * count)
    attn_state, mlp_state = (attn_params, attn_first, attn_second), (mlp_params, mlp_first, mlp_second)
    attn_terms, mlp_terms, plans = terms
    attn_new = settle(scale, layer.places[0], attn_terms, plans[0], (), attn_state)
    mlp_new = settle(scale, layer.places[1], mlp_terms, plans[1], plans[2], mlp_state)
    return (*outputs, *attn_new, *mlp_new)


def solution(mesh):
    split = P(AXES)
    split_rows = P(AXES, None)
    by_hand = mesh.shape["dp"] == 8 and mesh.shape["rep"] == 4
    return jax.shard_map(
        functools.partial(body, by_hand),
        mesh=mesh,
        in_specs=(split_rows, split_rows) + (split,) * 8,
        out_specs=(split_rows, split_rows) + (split,) * 8,
        check_vma=False,
    )
```
